32 devices in a mesh: dp: 8 (over z, x), mp: 4 (over y, core).
Axes of the slice: x: 2, y: 2, z: 4, core: 2. Of those that a mesh axis runs over, the one named last changes fastest.
Arguments:
- char_ids: int32 [1024, 6], P('dp'), may hold values from 0 to 274
- next_chars: int32 [1024, 6], P('dp'), may hold values from 0 to 274
- resets: int32 [1024, 6], P('dp'), may hold values 0 or 1
- embedding: bfloat16 [275, 100], replicated, may hold values from -6 to 6
- input_weight: bfloat16 [100, 4, 2048], P(None, None, 'mp'), may hold values from -0.625 to 0.625
- recurrent_weight: bfloat16 [2048, 4, 2048], P('dp', None, 'mp'), may hold values from -0.125 to 0.125
- gate_bias: float32 [4, 2048], P(None, 'mp'), may hold values from -4 to 4
- decoder_weight: bfloat16 [4, 8, 64, 275], P('mp', 'dp'), may hold values from -1 to 1
- decoder_bias: float32 [275], replicated, may hold values from -4 to 4
Outputs:
- loss: float32 [], replicated
- grad_embedding: float32 [275, 100], replicated
- grad_input_weight: float32 [100, 4, 2048], P(None, None, 'mp')
- grad_recurrent_weight: float32 [2048, 4, 2048], P('dp', None, 'mp')
- grad_gate_bias: float32 [4, 2048], P(None, 'mp')
- grad_decoder_weight: float32 [4, 8, 64, 275], P('mp', 'dp')
- grad_decoder_bias: float32 [275], replicated
The draws below stay inside these ranges and needn't reach their ends.
Inputs may be any that keep to these rules, and one draw needn't show every extreme that they name: `resets`: 1 marks the first character of a sentence: the state is zeroed before it.
All inputs are finite; a program needn't handle non-finite values. No bound on the sum of `resets` on one device may be relied on, other than what follows from the above.
Results may differ from the reference program's by a relative error of at most 0.0049.
Values may be sent and summed in bfloat16 or wider, within the bound.
A program may use at most 128 MiB of HBM per device.

```python
import math
import jax
import jax.numpy as jnp
import numpy as np
from jax import lax

H = 2048
E = 100
V = 275
B_DEV = 128
LEN = 6
BATCH = 1024
HB = 64
N_DP = 8
N_MP = 4


def with_ends(drawn, own_key, low, largest):
    longest = drawn.shape.index(max(drawn.shape))
    spots = []
    for shift in (0, 1):
        where = [jax.random.randint(jax.random.fold_in(own_key, axis), (), 0, length) for axis, length in enumerate(drawn.shape)]
        where[longest] = (where[longest] + shift) % drawn.shape[longest]
        spots.append(tuple(where))
    return drawn.at[spots[0]].set(low).at[spots[1]].set(largest)


def shard_levels(own_key, shape, shards, low, largest):
    def one(axis_at, parts):
        steps = jax.random.uniform(jax.random.fold_in(jax.random.fold_in(own_key, 6), axis_at), (parts,), jnp.float32, low / len(shards), largest / len(shards))
        return jnp.repeat(jnp.exp(steps), shape[axis_at] // parts).reshape((-1,) + (1,) * (len(shape) - axis_at - 1))

    gain = one(*shards[0])
    for cut in shards[1:]:
        gain = gain * one(*cut)
    return gain


def rank_bounds(number_of, skew):
    loads = [(1 << 20) // math.isqrt(rank ** skew) + 1 for rank in range(1, number_of + 1)]
    scale = 1 + sum(loads) // (1 << 30)
    return np.cumsum(np.array([max(1, weight // scale) for weight in loads]))


def skewed_ids(key, dims, number_of, lean):
    table = rank_bounds(number_of, lean)
    ticket = jax.random.randint(jax.random.fold_in(key, 1), dims, 0, int(table[number_of - 1]))
    standing = jnp.searchsorted(jnp.asarray(table, jnp.int32), ticket, side="right")
    return jax.random.permutation(jax.random.fold_in(key, 2), number_of)[standing].astype(jnp.int32)


def noise(rng, shape, scale, limit, pieces=(), held_as=jnp.bfloat16):
    result = scale * jax.random.normal(rng, shape, jnp.float32)
    if pieces:
        result = result * shard_levels(rng, shape, pieces, -0.22, 0.18)
    return jnp.clip(result, -limit, limit).astype(held_as)


def setup_inputs(seed: int = 0) -> dict:
    seeds = jax.random.split(jax.random.key(seed), 10)
    return {
        "char_ids": with_ends(skewed_ids(seeds[0], (BATCH, LEN), V, 2), jax.random.fold_in(seeds[0], 3), 0, V - 1).astype(jnp.int32),
        "next_chars": with_ends(skewed_ids(seeds[1], (BATCH, LEN), V, 2), jax.random.fold_in(seeds[1], 3), 0, V - 1).astype(jnp.int32),
        "resets": with_ends((jax.random.randint(seeds[2], (BATCH, LEN), 0, 12) < 1).astype(jnp.int32), jax.random.fold_in(seeds[2], 1), 0, 1),
        "embedding": noise(seeds[3], (V, E), 1.0, 6.0),
        "input_weight": noise(seeds[4], (E, 4, H), E ** -0.5, 0.625, ((2, 4),)),
        "recurrent_weight": noise(seeds[5], (H, 4, H), H ** -0.5, 0.125, ((0, 8), (2, 4))),
        "gate_bias": noise(seeds[6], (4, H), 1.0, 4.0, ((1, 4),), jnp.float32),
        "decoder_weight": noise(seeds[7], (N_MP, N_DP, HB, V), (H // 64) ** -0.5, 1.0, ((0, 4), (1, 8))),
        "decoder_bias": noise(seeds[8], (V,), 1.0, 4.0, (), jnp.float32),
    }


@jax.custom_vjp
def low(v):
    return lax.optimization_barrier(v.astype(jnp.bfloat16)).astype(jnp.float32)

@jax.custom_vjp
def low_back(v):
    return v

def low_keep(v):
    return (low(v), None)

def low_pass(kept, grad):
    return (grad,)

def back_keep(v):
    return (v, None)

def back_low(kept, grad):
    return (low(grad),)
low.defvjp(low_keep, low_pass)
low_back.defvjp(back_keep, back_low)

def forward(params, char_rows, reset_rows, target_rows):
    embedding, input_weight, recurrent_weight, gate_bias, decoder_weight, decoder_bias = params
    highest = lax.Precision.HIGHEST
    embedded = embedding[char_rows]
    projected = jnp.einsum('gle,ekh->lgkh', embedded, input_weight, precision=highest) + gate_bias
    keep_mask = (1 - reset_rows).T.astype(jnp.float32)

    def time_step(state_pair, inputs):
        hidden_state, cell_state = state_pair
        proj_now, keep_now = inputs
        previous = hidden_state * keep_now[:, None]
        preact = low_back(proj_now + jnp.einsum('gh,hkj->gkj', previous, recurrent_weight, precision=highest))
        in_gate = jax.nn.sigmoid(preact[:, 0])
        forget_gate = jax.nn.sigmoid(preact[:, 1])
        cell_gate = jnp.tanh(preact[:, 2])
        out_gate = jax.nn.sigmoid(preact[:, 3])
        new_cell = forget_gate * cell_state * keep_now[:, None] + in_gate * cell_gate
        new_hidden = low(out_gate * jnp.tanh(new_cell))
        return ((new_hidden, new_cell), new_hidden)
    zero_state = jnp.zeros((B_DEV, H), jnp.float32)
    _, hiddens = lax.scan(jax.checkpoint(time_step), (zero_state, zero_state), (projected, keep_mask))
    logits = low_back(jnp.einsum('lgh,hv->lgv', hiddens, decoder_weight.reshape(H, V), precision=highest) + decoder_bias)
    log_total = jax.nn.logsumexp(logits, axis=-1)
    picked = jnp.take_along_axis(logits, target_rows.T[:, :, None], axis=-1)[:, :, 0]
    return jnp.sum(log_total - picked) / (B_DEV * LEN * N_DP)

def reference(char_ids, next_chars, resets, embedding, input_weight, recurrent_weight, gate_bias, decoder_weight, decoder_bias):
    params = (embedding.astype(jnp.float32), input_weight.astype(jnp.float32), recurrent_weight.astype(jnp.float32), gate_bias.astype(jnp.float32), decoder_weight.astype(jnp.float32), decoder_bias.astype(jnp.float32))
    id_groups = char_ids.reshape(N_DP, B_DEV, LEN)
    reset_groups = resets.reshape(N_DP, B_DEV, LEN)
    target_groups = next_chars.reshape(N_DP, B_DEV, LEN)

    def group_step(running, batch_in):
        group_ids, group_resets, group_targets = batch_in
        group_loss, pullback = jax.vjp(lambda params_in: forward(params_in, group_ids, group_resets, group_targets), params)
        grads = pullback(jnp.ones((), jnp.float32))[0]
        return ((running[0] + group_loss, jax.tree.map(jnp.add, running[1], grads)), None)
    initial = (jnp.zeros((), jnp.float32), jax.tree.map(jnp.zeros_like, params))
    (loss, grads), _ = lax.scan(group_step, initial, (id_groups, reset_groups, target_groups))
    return (loss, grads[0], grads[1], grads[2], grads[3], grads[4], grads[5])
```

```python
import functools

import jax
import jax.numpy as jnp
from jax import lax
from jax.experimental import pallas as pl
from jax.experimental.pallas import tpu as pltpu
from jax.sharding import PartitionSpec as P

f32 = jnp.float32
bf16 = jnp.bfloat16
MESH = pl.DeviceIdType.MESH
LANES = 128
CHIPS = ((2, 0), (0, 2), (2, 2))
PEERS = ((0, 1), (2, 0), (0, 2), (2, 2), (2, 1), (0, 3), (2, 3), (1, 0), (4, 0), (5, 0), (6, 0))
GROUP = ((0, 1), (2, 0), (0, 2), (2, 2), (2, 1), (0, 3), (2, 3))
OTHERS = (1, 4, 5)
COLUMN = (4, 6, 2)
SPLIT = 2
PIECES = 4


def turn(value, flips):
    for bit in (1, 2, 4):
        if flips & bit:
            value = value + bit - 2 * bit * lax.rem(lax.div(value, bit), 2)
    return value


def dot(a, b):
    return jnp.dot(a, b, preferred_element_type=f32)


def dot_t(a, b):
    return lax.dot_general(a, b, (((1,), (1,)), ((), ())), preferred_element_type=f32)


def t_dot(a, b):
    return lax.dot_general(a, b, (((0,), (0,)), ((), ())), preferred_element_type=f32)


def layer_kernel(
    dims,
    ids_ref,
    rec_ref,
    emb_ref,
    iw_ref,
    gb_ref,
    dec_ref,
    decb_ref,
    out_rec,
    out_iw,
    out_emb,
    out_dec,
    out_small,
    ids_all,
    weights,
    dec_all,
    hid,
    gates,
    cells,
    onehots,
    embedded,
    keeps,
    targets,
    logit_grads,
    pgs,
    pgm,
    carry_c,
    own_part,
    own_sum,
    core_out,
    core_in,
    chip_out,
    chip_in,
    small_acc,
    both,
    acc,
    x_out,
    x_in,
    z_out,
    z_in,
    giw_acc,
    giw_out,
    giw_x_in,
    giw_z_out,
    giw_z_in,
    giw_full,
    emb_part,
    emb_in,
    emb_sums,
    emb_full,
    dec_part,
    dec_in,
    small_all,
    ids_sem,
    wz_sem,
    wx_sem,
    decg_sem,
    decr_sem,
    hid_sem,
    relay_sem,
    core_sem,
    chip_sem,
    gx_sem,
    gz_sem,
    giw_sem,
    emb_sem,
    emb2_sem,
    emb3_sem,
    dsum_sem,
    small_sem,
):
    steps, rows, units, vocab_pad, tokens_all, block = dims
    cols = 4 * units
    part = rows // SPLIT
    d, m = lax.axis_index("dp"), lax.axis_index("mp")
    x_at, z_low, z_high = lax.rem(d, 2), lax.rem(lax.div(d, 2), 2), lax.div(d, 4)
    z_at = lax.div(d, 2)

    def device(flips):
        return (turn(d, flips[0]), turn(m, flips[1]))

    def slot(flips):
        return turn(m, flips[1]) * 2 + turn(z_low, flips[0] // 2)

    own = slot((0, 0))

    def copy(src, dst, sems, at, flips):
        return pltpu.make_async_remote_copy(
            src_ref=src,
            dst_ref=dst,
            send_sem=sems.at[(0,) + at],
            recv_sem=sems.at[(1,) + at],
            device_id=device(flips),
            device_id_type=MESH,
        )

    barrier = pltpu.get_barrier_semaphore()
    for flips in PEERS:
        pl.semaphore_signal(barrier, inc=1, device_id=device(flips), device_id_type=MESH)
    pl.semaphore_wait(barrier, len(PEERS))

    piece = block // PIECES

    def weight_rows(index, p):
        first = p * piece
        side, inside = first // LANES, first % LANES
        return weights.at[
            lax.div(index, 2) * 2 + side,
            pl.ds(pl.multiple_of(lax.rem(index, 2) * LANES + inside, piece), piece),
        ]

    def weight_z(k, p):
        flips = COLUMN[k]
        half = turn(z_low, (flips & 2) // 2)
        return copy(
            rec_ref.at[half, pl.ds(p * piece, piece)], weight_rows(d, p), wz_sem, (k, p), (flips, 0)
        )

    def weight_z_in(k, p):
        spot = weight_rows(turn(d, COLUMN[k]), p)
        return copy(spot, spot, wz_sem, (k, p), (COLUMN[k], 0))

    def weight_x(k, p):
        if k == 3:
            return copy(
                rec_ref.at[z_low, pl.ds(p * piece, piece)],
                weight_rows(d, p),
                wx_sem,
                (k, p),
                (1, 0),
            )
        spot = weight_rows(turn(d, COLUMN[k]), p)
        return copy(spot, spot, wx_sem, (k, p), (1, 0))

    def weight_x_in(k, p):
        flips = 0 if k == 3 else COLUMN[k]
        spot = weight_rows(turn(d, flips + 1), p)
        return copy(spot, spot, wx_sem, (k, p), (1, 0))

    ids_copy = copy(ids_ref, ids_all.at[z_low], ids_sem, (0,), (2, 0))
    ids_copy.start()
    dec_rows = dec_ref.shape[0]
    dec_spot = dec_all.at[
        own, pl.ds(pl.multiple_of(z_high * LANES + x_at * dec_rows, dec_rows), dec_rows)
    ]
    dec_copies = [
        copy(dec_ref, dec_spot, decg_sem, (j,), (flips, 0)) for j, flips in enumerate(OTHERS)
    ]
    for each in dec_copies:
        each.start()
    for p in range(PIECES):
        for k in range(3):
            weight_z(k, p).start()
        weight_x(3, p).start()

    ids_all[z_low] = ids_ref[...]
    dec_spot[...] = dec_ref[...]
    for p in range(PIECES):
        weight_rows(d, p)[...] = rec_ref[z_low, pl.ds(p * piece, piece), :]
    ids_copy.wait_recv()
    ids_now = ids_all[...].reshape(rows, LANES)
    vocab_iota = lax.broadcasted_iota(jnp.int32, (rows, vocab_pad), 1)
    for t in range(steps):
        onehots[t] = (ids_now[:, t : t + 1] == vocab_iota).astype(f32).astype(bf16)
        targets[t] = jnp.broadcast_to(ids_now[:, steps + t : steps + t + 1], (rows, LANES))
        keeps[t] = jnp.broadcast_to(
            (1 - ids_now[:, 2 * steps + t : 2 * steps + t + 1]).astype(f32), (rows, LANES)
        )

    def project(t, _):
        chosen = dot(onehots[t], emb_ref[...]).astype(bf16)
        embedded[t] = chosen
        gates[t] = dot(chosen, iw_ref[z_low]) + gb_ref[z_low]
        return 0

    lax.fori_loop(0, steps, project, 0)

    def span(s):
        return pl.ds(s * part, part)

    def send_hidden(t, s):
        spot = hid.at[own, t, span(s)]
        for j, flips in enumerate(CHIPS + ((0, 1),)):
            copy(spot, spot, hid_sem, (t, s, j), flips).start()

    def hidden_in(t, s, j):
        flips = CHIPS[j] if j < 3 else (0, 1)
        spot = hid.at[slot(flips), t, span(s)]
        return copy(spot, spot, hid_sem, (t, s, j), flips)

    def hidden_relay(t, s, j):
        spot = hid.at[slot(CHIPS[j]), t, span(s)]
        return copy(spot, spot, relay_sem, (t, s, j), (0, 1))

    def relay_in(t, s, j):
        spot = hid.at[slot((CHIPS[j][0], CHIPS[j][1] + 1)), t, span(s)]
        return copy(spot, spot, relay_sem, (t, s, j), (0, 1))

    def relay(t, s):
        for j in range(3):
            hidden_in(t, s, j).wait_recv()
            hidden_relay(t, s, j).start()

    def cell_step(t, s, added):
        here = span(s)
        preact = gates[t, here]
        if added is not None:
            keep = keeps[t, here, :1]
            preact = preact + keep * added
        in_gate = jax.nn.sigmoid(preact[:, :units])
        forget = jax.nn.sigmoid(preact[:, units : 2 * units])
        candidate = jnp.tanh(preact[:, 2 * units : 3 * units])
        out_gate = jax.nn.sigmoid(preact[:, 3 * units :])
        cell = in_gate * candidate
        if added is not None:
            cell = forget * keep * cells[t - 1, here] + cell
        cells[t, here] = cell
        hid[own, t, here] = (out_gate * jnp.tanh(cell)).astype(bf16)
        send_hidden(t, s)
        gates[t, here, :units] = in_gate
        gates[t, here, units : 2 * units] = forget
        gates[t, here, 2 * units : 3 * units] = candidate
        gates[t, here, 3 * units :] = out_gate

    for s in range(SPLIT):
        cell_step(0, s, None)

    for j, flips in enumerate(OTHERS):
        at = turn(z_high, flips // 4) * LANES + turn(x_at, flips % 2) * dec_rows
        spot = dec_all.at[own, pl.ds(pl.multiple_of(at, dec_rows), dec_rows)]
        copy(spot, spot, decg_sem, (j,), (flips, 0)).wait_recv()
    dec_own = dec_all.at[own]
    dec_sends = [
        copy(dec_own, dec_own, decr_sem, (j,), flips) for j, flips in enumerate(CHIPS + ((0, 1),))
    ]
    for each in dec_sends:
        each.start()

    def passing(p):
        for k in range(3):
            weight_z_in(k, p).wait_recv()
            weight_x(k, p).start()

    passing(0)
    for s in range(SPLIT):
        relay(0, s)
    passing(1)
    dec_relays = []
    for j in range(3):
        spot = dec_all.at[slot(CHIPS[j])]
        copy(spot, spot, decr_sem, (j,), CHIPS[j]).wait_recv()
        each = copy(spot, spot, decr_sem, (4 + j,), (0, 1))
        each.start()
        dec_relays.append(each)
    for p in range(2, PIECES):
        passing(p)
    spot = dec_all.at[slot((0, 1))]
    copy(spot, spot, decr_sem, (3,), (0, 1)).wait_recv()
    for j in range(3):
        spot = dec_all.at[slot((CHIPS[j][0], CHIPS[j][1] + 1))]
        copy(spot, spot, decr_sem, (4 + j,), (0, 1)).wait_recv()
    for p in range(PIECES):
        for k in (3, 0, 1, 2):
            weight_x_in(k, p).wait_recv()

    def add_member(total, t, s, flips):
        at = slot(flips)
        more = dot(hid[at, t, span(s)], weights[at])
        return more if total is None else total + more

    def gather_hidden(t, s):
        relay(t, s)
        total = add_member(None, t, s, (0, 0))
        for j in range(3):
            total = add_member(total, t, s, CHIPS[j])
        return finish_hidden(t, s, total)

    def finish_hidden(t, s, total):
        hidden_in(t, s, 3).wait_recv()
        total = add_member(total, t, s, (0, 1))
        for j in range(3):
            relay_in(t, s, j).wait_recv()
            total = add_member(total, t, s, (CHIPS[j][0], CHIPS[j][1] + 1))
        return total

    vocab_part = lax.broadcasted_iota(jnp.int32, (part, vocab_pad), 1)
    small_acc[...] = jnp.zeros_like(small_acc)

    def decode(t, s):
        here = span(s)
        logits = decb_ref[...]
        for at in range(8):
            logits = logits + dot(hid[at, t, here], dec_all[at])
        top = jnp.max(logits, axis=1, keepdims=True)
        exps = jnp.exp(logits - top)
        total = jnp.sum(exps, axis=1, keepdims=True)
        hot = targets[t, here, :1] == vocab_part
        picked = jnp.sum(jnp.where(hot, logits, 0.0), axis=1, keepdims=True)
        lost = top + jnp.log(total) - picked
        grad = ((exps / total - jnp.where(hot, 1.0, 0.0)) / tokens_all).astype(bf16)
        logit_grads[t, here] = grad
        small_acc[0:1, :] += jnp.sum(grad.astype(f32), axis=0, keepdims=True)
        small_acc[1:2, :] += jnp.broadcast_to(
            jnp.sum(lost, axis=0, keepdims=True) / tokens_all, (1, vocab_pad)
        )

    def forward(t, _):
        for s in range(SPLIT):
            cell_step(t, s, gather_hidden(t - 1, s))
            decode(t - 1, s)
        return 0

    for s in range(SPLIT):
        total = None
        for flips in ((0, 0),) + CHIPS:
            total = add_member(total, 0, s, flips)
        cell_step(1, s, finish_hidden(0, s, total))
        decode(0, s)
    lax.fori_loop(2, steps, forward, 0)

    def cell_back(t, s, carried, first):
        here = span(s)
        hidden_grad = dot_t(logit_grads[t, here], dec_all[own])
        if carried is not None:
            hidden_grad = hidden_grad + carried
        in_gate = gates[t, here, :units]
        forget = gates[t, here, units : 2 * units]
        candidate = gates[t, here, 2 * units : 3 * units]
        out_gate = gates[t, here, 3 * units :]
        squash = jnp.tanh(cells[t, here])
        cell_grad = hidden_grad * out_gate * (1.0 - squash * squash)
        if carried is not None:
            cell_grad = cell_grad + carry_c[here]
        grads = [
            cell_grad * candidate * in_gate * (1.0 - in_gate),
            None,
            cell_grad * in_gate * (1.0 - candidate * candidate),
            hidden_grad * squash * out_gate * (1.0 - out_gate),
        ]
        if first:
            grads[1] = jnp.zeros_like(cell_grad)
        else:
            keep = keeps[t, here, :1]
            grads[1] = cell_grad * (keep * cells[t - 1, here]) * forget * (1.0 - forget)
            carry_c[here] = keep * forget * cell_grad
        for k in range(4):
            pgs[t, here, k * units : (k + 1) * units] = grads[k].astype(bf16)
            if not first:
                pgm[t - 1, here, k * units : (k + 1) * units] = (keep * grads[k]).astype(bf16)

    def core_copy(t, s):
        return copy(core_out.at[t - 1, s], core_in.at[t - 1, s], core_sem, (t - 1, s), (0, 1))

    def chip_copy(t, s, j):
        return copy(
            chip_out.at[t - 1, s, j], chip_in.at[t - 1, s, j], chip_sem, (t - 1, s, j), CHIPS[j]
        )

    def spread(t, s):
        here = span(s)
        grad = pgm[t - 1, here]
        chips = CHIPS + ((0, 0),)
        for j, flips in enumerate(chips):
            core_out[t - 1, s, j] = dot_t(grad, weights[slot((flips[0], flips[1] + 1))]).astype(bf16)
        core_copy(t, s).start()
        for j, flips in enumerate(chips):
            own_part[j] = dot_t(grad, weights[slot(flips)])
        core_copy(t, s).wait_recv()
        for j in range(3):
            chip_out[t - 1, s, j] = (own_part[j] + core_in[t - 1, s, j].astype(f32)).astype(bf16)
            chip_copy(t, s, j).start()
        own_sum[s] = own_part[3] + core_in[t - 1, s, 3].astype(f32)

    def carried_in(t, s):
        total = own_sum[s]
        for j in range(3):
            chip_copy(t + 1, s, j).wait_recv()
            total = total + chip_in[t, s, j].astype(f32)
        return total

    last = steps - 1
    for s in range(SPLIT):
        relay(last, s)
    for s in range(SPLIT):
        hidden_in(last, s, 3).wait_recv()
        for j in range(3):
            relay_in(last, s, j).wait_recv()
        decode(last, s)
        cell_back(last, s, None, False)
        spread(last, s)

    def backward(i, _):
        t = last - i
        for s in range(SPLIT):
            cell_back(t, s, carried_in(t, s), False)
            spread(t, s)
        return 0

    lax.fori_loop(1, last, backward, 0)

    far = (2, 3, 1, 0)

    def x_copy(k, side):
        return copy(x_out.at[k, side], x_in.at[k, side], gx_sem, (k, side), (1, 0))

    def z_copy(k, side):
        return copy(z_out.at[k, side], z_in.at[k, side], gz_sem, (k, side), (far[k] * 2, 0))

    used = (steps - 1) * rows

    def weight_grad(k):
        block_z = turn(z_at, far[k])

        def one(side, _):
            at = block_z * 2 + side
            both[...] = t_dot(
                hid[at, 0 : steps - 1].reshape(used, units), pgm[...].reshape(used, cols)
            ).reshape(2, LANES, cols)
            x_out[k, side] = both[1 - x_at].astype(bf16)
            x_copy(k, side).start()
            acc[k, side] = both[x_at]
            return 0

        lax.fori_loop(0, 2, one, 0)

    def pass_z(k, side):
        x_copy(k, side).wait_recv()
        total = acc[k, side] + x_in[k, side].astype(f32)
        if k < 3:
            z_out[k, side] = total.astype(bf16)
            z_copy(k, side).start()
        else:
            acc[k, side] = total

    weight_grad(0)
    weight_grad(1)
    weight_grad(2)
    weight_grad(3)

    for s in range(SPLIT):
        cell_back(0, s, carried_in(0, s), True)
    tokens = steps * rows
    flat_grads = pgs[...].reshape(tokens, cols)
    giw_rows = giw_acc.shape[0]
    giw_acc[...] = t_dot(embedded[...].reshape(tokens, LANES), flat_grads)[:giw_rows]
    for k in range(2):
        at = pl.multiple_of((1 - x_at) * (2 * units) + k * units, units)
        giw_out[k] = giw_acc[:, pl.ds(at, units)].astype(bf16)
    giw_x = copy(giw_out, giw_x_in, giw_sem, (0,), (1, 0))
    giw_x.start()

    def dec_block(flips):
        return turn(z_high, flips // 4) * 2 + turn(x_at, flips % 2)

    dec_total = t_dot(hid[own].reshape(tokens, units), logit_grads[...].reshape(tokens, vocab_pad))
    dec_part[...] = dec_total.reshape(4, dec_rows, vocab_pad)
    dsum = [
        copy(dec_part.at[dec_block(flips)], dec_in.at[dec_block(0)], dsum_sem, (j,), (flips, 0))
        for j, flips in enumerate(OTHERS)
    ]
    for each in dsum:
        each.start()
    dec_in[dec_block(0)] = dec_part[dec_block(0)]
    small_all[dec_block(0)] = small_acc[...]
    smalls = [
        copy(small_acc, small_all.at[dec_block(0)], small_sem, (j,), (flips, 0))
        for j, flips in enumerate(OTHERS)
    ]
    for each in smalls:
        each.start()

    by_token = dot_t(flat_grads, iw_ref[z_low])
    high = by_token.astype(bf16)
    low = (by_token - high.astype(f32)).astype(bf16)
    flat_hot = onehots[...].reshape(tokens, vocab_pad)
    emb_rows = emb_full.shape[1]
    emb_part[...] = (t_dot(flat_hot, high) + t_dot(flat_hot, low))[: 8 * emb_rows].reshape(
        8, emb_rows, LANES
    )
    emb_copies = [
        copy(emb_part.at[slot(flips)], emb_in.at[own], emb_sem, (j,), flips)
        for j, flips in enumerate(GROUP)
    ]
    for each in emb_copies:
        each.start()
    emb_in[own] = emb_part[own]

    pass_z(0, 0)

    giw_x.wait_recv()
    for k in range(2):
        at = pl.multiple_of(x_at * (2 * units) + k * units, units)
        giw_acc[:, pl.ds(at, units)] += giw_x_in[k].astype(f32)
    giw_z_out[...] = giw_acc[
        :, pl.ds(pl.multiple_of(x_at * (2 * units) + (1 - z_high) * units, units), units)
    ].astype(bf16)
    giw_z = copy(giw_z_out, giw_z_in, giw_sem, (1,), (4, 0))
    giw_z.start()
    pass_z(0, 1)
    for j, flips in enumerate(GROUP):
        copy(emb_part.at[own], emb_in.at[slot(flips)], emb_sem, (j,), flips).wait_recv()
    total = emb_in[0]
    for at in range(1, 8):
        total = total + emb_in[at]
    emb_sums[dec_block(0)] = total
    emb2 = [
        copy(
            emb_sums.at[dec_block(0)], emb_sums.at[dec_block(0)], emb2_sem, (j,), (flips, 0)
        )
        for j, flips in enumerate(OTHERS)
    ]
    for each in emb2:
        each.start()

    giw_z.wait_recv()
    gate_at = x_at * 2 + z_high
    giw_full[z_low, gate_at] = (
        giw_acc[:, pl.ds(pl.multiple_of(gate_at * units, units), units)] + giw_z_in[...].astype(f32)
    ).astype(bf16)
    spot = giw_full.at[z_low, gate_at]
    giw_back_z = copy(spot, spot, giw_sem, (2,), (4, 0))
    giw_back_z.start()
    pass_z(1, 0)
    for j, flips in enumerate(OTHERS):
        spot = emb_sums.at[dec_block(flips)]
        copy(spot, spot, emb2_sem, (j,), (flips, 0)).wait_recv()
    emb_full[own] = (emb_sums[0] + emb_sums[1]) + (emb_sums[2] + emb_sums[3])
    emb3 = [
        copy(emb_full.at[own], emb_full.at[own], emb3_sem, (j,), flips)
        for j, flips in enumerate(GROUP)
    ]
    for each in emb3:
        each.start()
    spot = giw_full.at[z_low, x_at * 2 + 1 - z_high]
    copy(spot, spot, giw_sem, (2,), (4, 0)).wait_recv()
    spot = giw_full.at[z_low, pl.ds(x_at * 2, 2)]
    giw_back_x = copy(spot, spot, giw_sem, (3,), (1, 0))
    giw_back_x.start()
    pass_z(1, 1)
    spot = giw_full.at[z_low, pl.ds((1 - x_at) * 2, 2)]
    copy(spot, spot, giw_sem, (3,), (1, 0)).wait_recv()
    spot = giw_full.at[z_low]
    giw_side = copy(spot, spot, giw_sem, (4,), (2, 0))
    giw_side.start()
    for j, flips in enumerate(OTHERS):
        copy(
            dec_part.at[dec_block(0)], dec_in.at[dec_block(flips)], dsum_sem, (j,), (flips, 0)
        ).wait_recv()
        spot = small_all.at[dec_block(flips)]
        copy(small_acc, spot, small_sem, (j,), (flips, 0)).wait_recv()
    out_dec[...] = (dec_in[0] + dec_in[1]) + (dec_in[2] + dec_in[3])
    out_small[...] = (small_all[0] + small_all[1]) + (small_all[2] + small_all[3])
    pass_z(2, 0)
    pass_z(2, 1)
    for j, flips in enumerate(GROUP):
        spot = emb_full.at[slot(flips)]
        copy(spot, spot, emb3_sem, (j,), flips).wait_recv()
    out_emb[...] = emb_full[...]
    spot = giw_full.at[1 - z_low]
    copy(spot, spot, giw_sem, (4,), (2, 0)).wait_recv()
    runs = units // LANES

    def scatter(ref, here, side, gate, value):
        for run in range(runs):
            at = pl.multiple_of(gate * 2 * units + run * 2 * LANES + side * LANES, LANES)
            ref[here, pl.ds(at, LANES)] = value[:, run * LANES : (run + 1) * LANES]

    for side in range(2):
        for gate in range(4):
            scatter(out_iw, slice(None), side, gate, giw_full[side, gate].astype(f32))
    pass_z(3, 0)
    pass_z(3, 1)
    for side in range(2):
        here = pl.ds(side * LANES, LANES)
        z_copy(0, side).wait_recv()
        for gate in range(4):
            mine = slice(gate * units, (gate + 1) * units)
            scatter(
                out_rec,
                here,
                z_low,
                gate,
                acc[3, side, :, mine] + z_in[0, side, :, mine].astype(f32),
            )
        z_copy(1, side).wait_recv()
        z_copy(2, side).wait_recv()
        for gate in range(4):
            mine = slice(gate * units, (gate + 1) * units)
            scatter(
                out_rec,
                here,
                1 - z_low,
                gate,
                z_in[1, side, :, mine].astype(f32) + z_in[2, side, :, mine].astype(f32),
            )

    ids_copy.wait_send()
    for each in dec_copies + dec_sends + dec_relays:
        each.wait_send()
    for p in range(PIECES):
        for k in range(3):
            weight_z(k, p).wait_send()
        for k in range(4):
            weight_x(k, p).wait_send()

    def sent(t, _):
        for s in range(SPLIT):
            for j in range(3):
                hidden_in(t, s, j).wait_send()
                hidden_relay(t, s, j).wait_send()
            hidden_in(t, s, 3).wait_send()
        return 0

    lax.fori_loop(0, steps, sent, 0)

    def sent_back(t, _):
        for s in range(SPLIT):
            core_copy(t, s).wait_send()
            for j in range(3):
                chip_copy(t, s, j).wait_send()
        return 0

    lax.fori_loop(1, steps, sent_back, 0)
    for side in range(2):
        for k in range(4):
            x_copy(k, side).wait_send()
        for k in range(3):
            z_copy(k, side).wait_send()
    for each in [giw_x, giw_z, giw_back_z, giw_back_x, giw_side]:
        each.wait_send()
    for each in emb_copies + emb2 + emb3 + dsum + smalls:
        each.wait_send()


def grouped(
    char_ids,
    next_chars,
    resets,
    embedding,
    input_weight,
    recurrent_weight,
    gate_bias,
    decoder_weight,
    decoder_bias,
):
    data_count = lax.axis_size("dp")
    row_count, steps = char_ids.shape
    vocab, width = embedding.shape
    local_units = input_weight.shape[2]
    block = recurrent_weight.shape[0]
    units = local_units // 2
    cols = 4 * units
    runs = units // LANES
    rows = 2 * row_count
    dec_rows = decoder_weight.shape[2]
    vocab_pad = pl.cdiv(vocab, LANES) * LANES
    tokens_all = row_count * steps * data_count
    part = rows // SPLIT
    emb_rows = pl.cdiv(vocab, 64) * 8
    giw_rows = pl.cdiv(width + 1, 16) * 16

    ids = jnp.pad(
        jnp.concatenate([char_ids, next_chars, resets], axis=1), ((0, 0), (0, LANES - 3 * steps))
    )
    rec = (
        recurrent_weight.reshape(block, 4, runs, 2, LANES)
        .transpose(3, 0, 1, 2, 4)
        .reshape(2, block, cols)
    )
    emb = jnp.concatenate([embedding, jnp.ones((vocab, 1), bf16)], axis=1)
    emb = jnp.pad(emb, ((0, vocab_pad - vocab), (0, LANES - width - 1)))
    iw = (
        input_weight.reshape(width, 4, runs, 2, LANES)
        .transpose(3, 0, 1, 2, 4)
        .reshape(2, width, cols)
    )
    iw = jnp.pad(iw, ((0, 0), (0, LANES - width), (0, 0)))
    gate_b = gate_bias.reshape(4, runs, 2, LANES).transpose(2, 0, 1, 3).reshape(2, 1, cols)
    dec = jnp.pad(decoder_weight.reshape(dec_rows, vocab), ((0, 0), (0, vocab_pad - vocab)))
    dec_b = jnp.pad(
        decoder_bias.reshape(1, vocab), ((0, 0), (0, vocab_pad - vocab)), constant_values=-1e30
    )

    vmem = pl.BlockSpec(memory_space=pltpu.VMEM)
    dims = (steps, rows, units, vocab_pad, tokens_all, block)

    def sems(*shape):
        return pltpu.SemaphoreType.DMA((2,) + shape)

    out_rec, out_iw, out_emb, out_dec, out_small = pl.pallas_call(
        functools.partial(layer_kernel, dims),
        out_shape=[
            jax.ShapeDtypeStruct((block, 2 * cols), f32),
            jax.ShapeDtypeStruct((giw_rows, 2 * cols), f32),
            jax.ShapeDtypeStruct((8, emb_rows, LANES), f32),
            jax.ShapeDtypeStruct((dec_rows, vocab_pad), f32),
            jax.ShapeDtypeStruct((8, vocab_pad), f32),
        ],
        in_specs=[vmem] * 7,
        out_specs=[vmem] * 5,
        scratch_shapes=[
            pltpu.VMEM((2, row_count, LANES), jnp.int32),
            pltpu.VMEM((8, units, cols), bf16),
            pltpu.VMEM((8, units, vocab_pad), bf16),
            pltpu.VMEM((8, steps, rows, units), bf16),
            pltpu.VMEM((steps, rows, cols), f32),
            pltpu.VMEM((steps, rows, units), f32),
            pltpu.VMEM((steps, rows, vocab_pad), bf16),
            pltpu.VMEM((steps, rows, LANES), bf16),
            pltpu.VMEM((steps, rows, LANES), f32),
            pltpu.VMEM((steps, rows, LANES), jnp.int32),
            pltpu.VMEM((steps, rows, vocab_pad), bf16),
            pltpu.VMEM((steps, rows, cols), bf16),
            pltpu.VMEM((steps - 1, rows, cols), bf16),
            pltpu.VMEM((rows, units), f32),
            pltpu.VMEM((4, part, units), f32),
            pltpu.VMEM((SPLIT, part, units), f32),
            pltpu.VMEM((steps - 1, SPLIT, 4, part, units), bf16),
            pltpu.VMEM((steps - 1, SPLIT, 4, part, units), bf16),
            pltpu.VMEM((steps - 1, SPLIT, 3, part, units), bf16),
            pltpu.VMEM((steps - 1, SPLIT, 3, part, units), bf16),
            pltpu.VMEM((8, vocab_pad), f32),
            pltpu.VMEM((2, LANES, cols), f32),
            pltpu.VMEM((4, 2, LANES, cols), f32),
            pltpu.VMEM((4, 2, LANES, cols), bf16),
            pltpu.VMEM((4, 2, LANES, cols), bf16),
            pltpu.VMEM((3, 2, LANES, cols), bf16),
            pltpu.VMEM((3, 2, LANES, cols), bf16),
            pltpu.VMEM((giw_rows, cols), f32),
            pltpu.VMEM((2, giw_rows, units), bf16),
            pltpu.VMEM((2, giw_rows, units), bf16),
            pltpu.VMEM((giw_rows, units), bf16),
            pltpu.VMEM((giw_rows, units), bf16),
            pltpu.VMEM((2, 4, giw_rows, units), bf16),
            pltpu.VMEM((8, emb_rows, LANES), f32),
            pltpu.VMEM((8, emb_rows, LANES), f32),
            pltpu.VMEM((4, emb_rows, LANES), f32),
            pltpu.VMEM((8, emb_rows, LANES), f32),
            pltpu.VMEM((4, dec_rows, vocab_pad), f32),
            pltpu.VMEM((4, dec_rows, vocab_pad), f32),
            pltpu.VMEM((4, 8, vocab_pad), f32),
            sems(1),
            sems(3, PIECES),
            sems(4, PIECES),
            sems(3),
            sems(7),
            sems(steps, SPLIT, 4),
            sems(steps, SPLIT, 3),
            sems(steps - 1, SPLIT),
            sems(steps - 1, SPLIT, 3),
            sems(4, 2),
            sems(3, 2),
            sems(5),
            sems(7),
            sems(3),
            sems(7),
            sems(3),
            sems(3),
        ],
        compiler_params=pltpu.CompilerParams(
            collective_id=0, has_side_effects=True, vmem_limit_bytes=62 << 20
        ),
    )(ids, rec, emb, iw, gate_b, dec, dec_b)

    rec_grad = out_rec.reshape(recurrent_weight.shape)
    in_grad = out_iw[:width].reshape(input_weight.shape)
    bias_grad = out_iw[width].reshape(gate_bias.shape)
    emb_grad = out_emb.reshape(8 * emb_rows, LANES)[:vocab, :width]
    dec_grad = out_dec[:, :vocab].reshape(decoder_weight.shape)
    return (
        out_small[1, 0],
        emb_grad,
        in_grad,
        rec_grad,
        bias_grad,
        dec_grad,
        out_small[0, :vocab],
    )


def on_device(
    char_ids,
    next_chars,
    resets,
    embedding,
    input_weight,
    recurrent_weight,
    gate_bias,
    decoder_weight,
    decoder_bias,
):
    highest = lax.Precision.HIGHEST
    data_count = lax.axis_size("dp")
    row_count, step_count = char_ids.shape
    vocab_size, width_in = embedding.shape
    local_units = input_weight.shape[2]
    gate_cols = 4 * local_units
    tokens_here = row_count * step_count
    tokens_all = tokens_here * data_count
    gathered_rec, gathered_dec = (
        lax.all_gather(recurrent_weight, "dp", axis=0, tiled=True),
        lax.all_gather(decoder_weight, "dp", axis=1, tiled=True),
    )
    hidden_total = gathered_rec.shape[0]
    rec_matrix = gathered_rec.reshape(hidden_total, gate_cols)
    dec_matrix = gathered_dec.reshape(local_units, vocab_size)
    time_ids = char_ids.T
    keep_mask = (1 - resets.T).astype(f32)
    proj_table = jnp.dot(
        embedding, input_weight.reshape(width_in, gate_cols), preferred_element_type=f32
    )
    projected = jnp.take(proj_table, time_ids, axis=0) + gate_bias.reshape(gate_cols)

    def forward_step(state_pair, inputs):
        hidden_loc, cell_state = state_pair
        proj_now, keep_now = inputs
        hidden_full = lax.all_gather(hidden_loc, "mp", axis=1, tiled=True)
        previous = hidden_full * keep_now[:, None].astype(bf16)
        preact = proj_now + jnp.dot(previous, rec_matrix, preferred_element_type=f32)
        gate_vals = preact.reshape(row_count, 4, local_units)
        in_gate = jax.nn.sigmoid(gate_vals[:, 0])
        forget_gate = jax.nn.sigmoid(gate_vals[:, 1])
        cell_gate = jnp.tanh(gate_vals[:, 2])
        out_gate = jax.nn.sigmoid(gate_vals[:, 3])
        new_cell = forget_gate * cell_state * keep_now[:, None] + in_gate * cell_gate
        new_hidden = (out_gate * jnp.tanh(new_cell)).astype(bf16)
        return ((new_hidden, new_cell), (previous, preact, new_cell, new_hidden))

    first_state = (
        jnp.zeros((row_count, local_units), bf16),
        jnp.zeros((row_count, local_units), f32),
    )
    _, (prevs, preacts, cells, hiddens) = lax.scan(
        forward_step, first_state, (projected, keep_mask)
    )
    flat_hidden = hiddens.reshape(tokens_here, local_units)
    partial_value = jnp.dot(flat_hidden, dec_matrix, preferred_element_type=f32)
    flat_targets = next_chars.T.reshape(tokens_here)
    logit_rows = lax.psum(partial_value, "mp")
    shifted_in = logit_rows + decoder_bias
    row_max = jnp.max(shifted_in, axis=1)
    exp_total = jnp.sum(jnp.exp(shifted_in - row_max[:, None]), axis=1)
    log_total = row_max + jnp.log(exp_total)
    softmax_out = jnp.exp(shifted_in - log_total[:, None])
    onehot = (flat_targets[:, None] == jnp.arange(vocab_size, dtype=jnp.int32)[None, :]).astype(f32)
    picked = jnp.sum(shifted_in * onehot, axis=1)
    grad_rows = ((softmax_out - onehot) / tokens_all).astype(bf16)
    local_loss = jnp.sum(log_total - picked) / tokens_all
    loss_part = jnp.where(lax.axis_index("mp") == 0, local_loss, jnp.zeros((), f32))
    out_grads = jnp.dot(grad_rows, dec_matrix.T, preferred_element_type=f32).reshape(
        step_count, row_count, local_units
    )
    dec_bias_part = jnp.sum(grad_rows.astype(f32), axis=0)
    columns = flat_hidden
    dec_grad = lax.psum_scatter(
        lax.dot_general(columns, grad_rows, (((0,), (0,)), ((), ())), preferred_element_type=f32),
        "dp",
        scatter_dimension=0,
        tiled=True,
    ).reshape(decoder_weight.shape)
    prev_cells = (
        jnp.concatenate([jnp.zeros((1, row_count, local_units), f32), cells[:-1]], axis=0)
        * keep_mask[:, :, None]
    )

    def backward_step(state_pair, inputs):
        carry_hidden, carry_cell = state_pair
        preact, cell_state, prev_cell, hidden_out, keep_now = inputs
        gate_vals = preact.reshape(row_count, 4, local_units)
        in_gate = jax.nn.sigmoid(gate_vals[:, 0])
        forget_gate = jax.nn.sigmoid(gate_vals[:, 1])
        cell_gate = jnp.tanh(gate_vals[:, 2])
        out_gate = jax.nn.sigmoid(gate_vals[:, 3])
        hidden_grad = hidden_out + carry_hidden
        squash = jnp.tanh(cell_state)
        cell_grad = hidden_grad * out_gate * (1.0 - squash * squash) + carry_cell
        grad_in = cell_grad * cell_gate * in_gate * (1.0 - in_gate)
        grad_forget = cell_grad * prev_cell * forget_gate * (1.0 - forget_gate)
        grad_cand = cell_grad * in_gate * (1.0 - cell_gate * cell_gate)
        grad_out = hidden_grad * squash * out_gate * (1.0 - out_gate)
        preact_grad = (
            jnp.stack([grad_in, grad_forget, grad_cand, grad_out], axis=1)
            .reshape(row_count, gate_cols)
            .astype(bf16)
        )
        back_term = lax.dot_general(
            preact_grad, rec_matrix, (((1,), (1,)), ((), ())), preferred_element_type=f32
        )
        next_hidden = (
            lax.psum_scatter(back_term, "mp", scatter_dimension=1, tiled=True) * keep_now[:, None]
        )
        next_cell = cell_grad * forget_gate * keep_now[:, None]
        return ((next_hidden, next_cell), preact_grad)

    zero_rows = jnp.zeros((row_count, local_units), f32)
    _, preact_grads = lax.scan(
        backward_step,
        (zero_rows, zero_rows),
        (preacts, cells, prev_cells, out_grads, keep_mask),
        reverse=True,
    )
    flat_prev = prevs.reshape(tokens_here, hidden_total)
    flat_pgrad = preact_grads.reshape(tokens_here, gate_cols)
    columns = flat_prev
    rec_grad = lax.psum_scatter(
        lax.dot_general(columns, flat_pgrad, (((0,), (0,)), ((), ())), preferred_element_type=f32),
        "dp",
        scatter_dimension=0,
        tiled=True,
    ).reshape(recurrent_weight.shape)
    onehot_ids = (
        time_ids.reshape(tokens_here)[:, None] == jnp.arange(vocab_size, dtype=jnp.int32)[None, :]
    ).astype(bf16)
    table_part = lax.dot_general(
        onehot_ids, flat_pgrad, (((0,), (0,)), ((), ())), preferred_element_type=f32
    )
    table_sum, dec_bias_grad, loss_data = lax.psum((table_part, dec_bias_part, loss_part), "dp")
    in_grad = jnp.dot(embedding.astype(f32).T, table_sum, precision=highest).reshape(
        width_in, 4, local_units
    )
    bias_grad = jnp.sum(table_sum, axis=0).reshape(4, local_units)
    emb_part = lax.dot_general(
        table_sum,
        input_weight.reshape(width_in, gate_cols).astype(f32),
        (((1,), (1,)), ((), ())),
        precision=highest,
    )
    emb_grad, loss = lax.psum((emb_part, loss_data), "mp")
    return (loss, emb_grad, in_grad, rec_grad, bias_grad, dec_grad, dec_bias_grad)


def solution(mesh):
    in_specs = (
        P("dp", None),
        P("dp", None),
        P("dp", None),
        P(),
        P(None, None, "mp"),
        P("dp", None, "mp"),
        P(None, "mp"),
        P("mp", "dp", None, None),
        P(),
    )
    out_specs = (
        P(),
        P(),
        P(None, None, "mp"),
        P("dp", None, "mp"),
        P(None, "mp"),
        P("mp", "dp", None, None),
        P(),
    )
    fits = (mesh.shape["dp"], mesh.shape["mp"]) == (8, 4)
    return jax.shard_map(
        grouped if fits else on_device,
        mesh=mesh,
        in_specs=in_specs,
        out_specs=out_specs,
        check_vma=False,
    )
```

```python
import functools

import jax
import jax.numpy as jnp
from jax import lax
from jax.experimental import pallas as pl
from jax.experimental.pallas import tpu as pltpu
from jax.sharding import PartitionSpec as P

f32 = jnp.float32
bf16 = jnp.bfloat16
MESH = pl.DeviceIdType.MESH
LANES = 128
CHIPS = ((2, 0), (0, 2), (2, 2))
PEERS = ((0, 1), (2, 0), (0, 2), (2, 2), (2, 1), (0, 3), (2, 3), (1, 0), (4, 0), (5, 0), (6, 0))
GROUP = ((0, 1), (2, 0), (0, 2), (2, 2), (2, 1), (0, 3), (2, 3))
OTHERS = (1, 4, 5)
COLUMN = (4, 6, 2)
SPLIT = 2
PIECES = 8
SUB = 2


def turn(value, flips):
    for bit in (1, 2, 4):
        if flips & bit:
            value = value + bit - 2 * bit * lax.rem(lax.div(value, bit), 2)
    return value


def dot(a, b):
    return jnp.dot(a, b, preferred_element_type=f32)


def dot_t(a, b):
    return lax.dot_general(a, b, (((1,), (1,)), ((), ())), preferred_element_type=f32)


def t_dot(a, b):
    return lax.dot_general(a, b, (((0,), (0,)), ((), ())), preferred_element_type=f32)


def layer_kernel(
    dims,
    chars_ref,
    nexts_ref,
    resets_ref,
    emb_ref,
    iw_ref,
    rec_ref,
    gb_ref,
    dec_ref,
    decb_ref,
    out_loss,
    out_emb,
    out_iw,
    out_rec,
    out_gb,
    out_dec,
    out_decb,
    ids_rows,
    ids_cols,
    rec_halves,
    weights,
    emb_pad,
    iw_pads,
    gb_pads,
    dec_pad,
    decb_pad,
    dec_all,
    hid,
    gates,
    cells,
    onehots,
    embedded,
    keeps,
    targets,
    logit_grads,
    pgs,
    pgm,
    carry_c,
    pg_now,
    pg_out,
    pgm_out,
    pgm_now,
    own_sum,
    chip_out,
    chip_in,
    small_acc,
    small_pair,
    both,
    acc,
    x_out,
    x_in,
    z_out,
    z_in,
    giw_acc,
    giw_out,
    giw_x_in,
    giw_z_out,
    giw_z_in,
    giw_full,
    emb_part,
    emb_in,
    emb_sums,
    emb_full,
    dec_part,
    dec_x_out,
    dec_x_in,
    dec_z_out,
    dec_z_in,
    ids_sem,
    wz_sem,
    wx_sem,
    wc_sem,
    iw_sem,
    decg_sem,
    decr_sem,
    hid_sem,
    hidc_sem,
    lg_sem,
    pg_sem,
    pgm_sem,
    small_sem,
    chip_sem,
    gx_sem,
    gz_sem,
    giw_sem,
    emb_sem,
    emb2_sem,
    emb3_sem,
    dsum_sem,
):
    steps, rows, units, vocab, vocab_pad, tokens_all, block = dims
    cols = 4 * units
    half = rows // 2
    part = half // SPLIT
    d, m = lax.axis_index("dp"), lax.axis_index("mp")
    x_at, z_low, z_high = lax.rem(d, 2), lax.rem(lax.div(d, 2), 2), lax.div(d, 4)
    z_at = lax.div(d, 2)
    core, y_at = lax.rem(m, 2), lax.div(m, 2)

    def device(flips):
        return (turn(d, flips[0]), turn(m, flips[1]))

    def slot(flips):
        return turn(z_low, flips[0] // 2) * 4 + turn(m, flips[1])

    def chip(flips):
        return pl.ds(turn(z_low, flips[0] // 2) * 4 + turn(y_at, flips[1] // 2) * 2, 2)

    own = slot((0, 0))

    def copy(src, dst, sems, at, flips):
        return pltpu.make_async_remote_copy(
            src_ref=src,
            dst_ref=dst,
            send_sem=sems.at[(0,) + at],
            recv_sem=sems.at[(1,) + at],
            device_id=device(flips),
            device_id_type=MESH,
        )

    barrier = pltpu.get_barrier_semaphore()
    for flips in PEERS:
        pl.semaphore_signal(barrier, inc=1, device_id=device(flips), device_id_type=MESH)
    pl.semaphore_wait(barrier, len(PEERS))

    piece = block // PIECES

    def weight_rows(index, p):
        first = p * piece
        side, inside = first // LANES, first % LANES
        return weights.at[
            core,
            side * 4 + lax.div(index, 2),
            pl.ds(pl.multiple_of(lax.rem(index, 2) * LANES + inside, piece), piece),
        ]

    def weight_core(index, at, p):
        spot = weight_rows(index, p)
        return copy(spot, spot, wc_sem, (at, p), (0, 1))

    def block_of(at):
        return turn(d, (0, 4, 6, 2)[at % 4] + at // 4)

    def weight_z(k, p):
        flips = COLUMN[k]
        half = turn(z_low, (flips & 2) // 2)
        return copy(
            rec_halves.at[half, pl.ds(p * piece, piece)], weight_rows(d, p), wz_sem, (k, p), (flips, 0)
        )

    def weight_z_in(k, p):
        spot = weight_rows(turn(d, COLUMN[k]), p)
        return copy(spot, spot, wz_sem, (k, p), (COLUMN[k], 0))

    def weight_x(k, p):
        if k == 3:
            return copy(
                rec_halves.at[z_low, pl.ds(p * piece, piece)],
                weight_rows(d, p),
                wx_sem,
                (k, p),
                (1, 0),
            )
        spot = weight_rows(turn(d, COLUMN[k]), p)
        return copy(spot, spot, wx_sem, (k, p), (1, 0))

    def weight_x_in(k, p):
        flips = 0 if k == 3 else COLUMN[k]
        spot = weight_rows(turn(d, flips + 1), p)
        return copy(spot, spot, wx_sem, (k, p), (1, 0))

    runs = units // LANES
    width = iw_ref.shape[1]
    dec_rows = dec_ref.shape[0]
    vocab_rows = emb_pad.shape[0]

    def dec_spot(flips):
        at = turn(z_high, flips // 4) * LANES + turn(x_at, flips % 2) * dec_rows
        return dec_all.at[own, pl.ds(pl.multiple_of(at, dec_rows), dec_rows)]

    ids_rows[z_low, 0:steps] = chars_ref[...]
    ids_rows[z_low, 8 : 8 + steps] = nexts_ref[...]
    ids_rows[z_low, 16 : 16 + steps] = resets_ref[...]
    ids_copy = copy(ids_rows.at[z_low], ids_rows.at[z_low], ids_sem, (0,), (2, 0))
    ids_copy.start()
    for p in range(PIECES):
        here = slice(p * piece, (p + 1) * piece)
        for gate in range(4):
            for run in range(runs):
                for side in range(2):
                    at = (run * 2 + side) * LANES
                    to = gate * units + run * LANES
                    rec_halves[side, here, to : to + LANES] = rec_ref[gate, here, at : at + LANES]
        for k in range(3):
            weight_z(k, p).start()
        weight_x(3, p).start()
        if p == 0:
            dec_pad[...] = jnp.zeros_like(dec_pad)
            dec_pad[:, :vocab] = dec_ref[...]
            dec_z = copy(dec_pad, dec_spot(0), decg_sem, (0,), (4, 0))
            dec_z.start()
            dec_x = [copy(dec_pad, dec_spot(0), decg_sem, (1,), (1, 0))]
            dec_x[0].start()

    def weight_round(p):
        for k in range(3):
            weight_z_in(k, p).wait_recv()
            weight_x(k, p).start()
            weight_core(block_of(1 + k), 1 + k, p).start()
        if p:
            weight_over_x(p - 1)

    def weight_over_x(p):
        for k in (3, 0, 1, 2):
            weight_x_in(k, p).wait_recv()
            at = 4 if k == 3 else 5 + k
            weight_core(block_of(at), at, p).start()

    for p in range(PIECES):
        weight_rows(d, p)[...] = rec_halves[z_low, pl.ds(p * piece, piece)]
        weight_core(block_of(0), 0, p).start()
    dec_spot(0)[...] = dec_pad[...]
    emb_pad[...] = jnp.zeros_like(emb_pad)
    emb_pad[:vocab, :width] = emb_ref[...]
    ones_at = lax.broadcasted_iota(jnp.int32, emb_pad.shape, 1) == width
    emb_pad[...] = jnp.where(ones_at, 1.0, emb_pad[...].astype(f32)).astype(bf16)
    iw_pads[core] = jnp.zeros(iw_pads.shape[1:], bf16)

    def half_lanes(run):
        return pl.ds(pl.multiple_of((run * 2 + z_low) * LANES, LANES), LANES)

    for gate in range(4):
        for run in range(runs):
            to = gate * units + run * LANES
            iw_pads[core, :width, to : to + LANES] = iw_ref[gate, :, half_lanes(run)]
            gb_pads[core, :, to : to + LANES] = gb_ref[gate : gate + 1, half_lanes(run)]
    iw_copies = [
        copy(ref.at[core], ref.at[core], iw_sem, (k,), (0, 1))
        for k, ref in enumerate((iw_pads, gb_pads))
    ]
    for each in iw_copies:
        each.start()
    decb_pad[...] = jnp.full(decb_pad.shape, -1e30, f32)
    decb_pad[:, :vocab] = decb_ref[...]
    ids_copy.wait_recv()
    ids_cols[...] = ids_rows[core].T
    vocab_iota = lax.broadcasted_iota(jnp.int32, (vocab_rows, rows), 0)

    def read_ids(t):
        now = jnp.concatenate([ids_rows[0, t : t + 1], ids_rows[1, t : t + 1]], axis=1)
        onehots[t] = (vocab_iota == now).astype(f32).astype(bf16)
        targets[t] = jnp.broadcast_to(ids_cols[:, 8 + t : 9 + t], (half, LANES))
        keeps[t] = jnp.broadcast_to((1 - ids_cols[:, 16 + t : 17 + t]).astype(f32), (half, LANES))

    def project(t):
        read_ids(t)
        chosen = t_dot(onehots[t], emb_pad[...]).astype(bf16)
        embedded[t] = chosen
        mine = embedded[t, pl.ds(pl.multiple_of(core * half, half), half)]
        for c in range(2):
            gates[t, c] = dot(mine, iw_pads[c]) + gb_pads[c]

    for k, ref in enumerate((iw_pads, gb_pads)):
        copy(ref.at[1 - core], ref.at[1 - core], iw_sem, (k,), (0, 1)).wait_recv()
    project(0)

    def span(s):
        return pl.ds(s * part, part)

    def wide(s):
        return pl.ds(pl.multiple_of(core * half + s * part, part), part)

    def hidden_copy(t, s, j):
        spot = hid.at[chip((0, 0)), t, wide(s)]
        return copy(spot, spot, hid_sem, (t, s, j), CHIPS[j])

    def hidden_in(t, s, j):
        spot = hid.at[chip(CHIPS[j]), t, wide(s)]
        return copy(spot, spot, hid_sem, (t, s, j), CHIPS[j])

    def hidden_core(t, s):
        spot = hid.at[:, t, wide(s)]
        return copy(spot, spot, hidc_sem, (t, s), (0, 1))

    def hidden_core_in(t, s):
        rows_there = pl.ds(pl.multiple_of((1 - core) * half + s * part, part), part)
        spot = hid.at[:, t, rows_there]
        return copy(spot, spot, hidc_sem, (t, s), (0, 1))

    def cell_step(t, s, added):
        here = span(s)
        if added is not None:
            keep = keeps[t, here, :1]
        for c in range(2):
            preact = gates[t, c, here]
            if added is not None:
                preact = preact + keep * added[c]
            in_gate = jax.nn.sigmoid(preact[:, :units])
            forget = jax.nn.sigmoid(preact[:, units : 2 * units])
            candidate = jnp.tanh(preact[:, 2 * units : 3 * units])
            out_gate = jax.nn.sigmoid(preact[:, 3 * units :])
            cell = in_gate * candidate
            if added is not None:
                cell = forget * keep * cells[t - 1, c, here] + cell
            cells[t, c, here] = cell
            hid[z_low * 4 + y_at * 2 + c, t, wide(s)] = (out_gate * jnp.tanh(cell)).astype(bf16)
            gates[t, c, here, :units] = in_gate
            gates[t, c, here, units : 2 * units] = forget
            gates[t, c, here, 2 * units : 3 * units] = candidate
            gates[t, c, here, 3 * units :] = out_gate
        for j in (2, 0, 1):
            hidden_copy(t, s, j).start()

    for s in range(SPLIT):
        cell_step(0, s, None)

    weight_round(0)
    project(1)
    project(2)
    weight_round(1)
    spot = dec_spot(4)
    copy(spot, spot, decg_sem, (0,), (4, 0)).wait_recv()
    dec_x.append(copy(spot, spot, decg_sem, (2,), (1, 0)))
    dec_x[1].start()
    project(3)
    weight_round(2)
    project(4)
    project(5)
    weight_round(3)
    for j, flips in enumerate((1, 5)):
        spot = dec_spot(flips)
        copy(spot, spot, decg_sem, (1 + j,), (1, 0)).wait_recv()
    dec_own = dec_all.at[own]
    dec_sends = [
        copy(dec_own, dec_own, decr_sem, (j,), flips) for j, flips in enumerate(CHIPS + ((0, 1),))
    ]
    for each in dec_sends:
        each.start()
    weight_round(4)
    weight_round(5)
    dec_relays = []
    for j in range(3):
        spot = dec_all.at[slot(CHIPS[j])]
        copy(spot, spot, decr_sem, (j,), CHIPS[j]).wait_recv()
        each = copy(spot, spot, decr_sem, (4 + j,), (0, 1))
        each.start()
        dec_relays.append(each)
    for p in range(6, PIECES):
        weight_round(p)
    spot = dec_all.at[slot((0, 1))]
    copy(spot, spot, decr_sem, (3,), (0, 1)).wait_recv()
    for j in range(3):
        spot = dec_all.at[slot((CHIPS[j][0], CHIPS[j][1] + 1))]
        copy(spot, spot, decr_sem, (4 + j,), (0, 1)).wait_recv()
    weight_over_x(PIECES - 1)
    for p in range(PIECES):
        for at in range(8):
            spot = weights.at[
                1 - core,
                (p * piece // LANES) * 4 + lax.div(block_of(at), 2),
                pl.ds(
                    pl.multiple_of(
                        lax.rem(block_of(at), 2) * LANES + p * piece % LANES, piece
                    ),
                    piece,
                ),
            ]
            copy(spot, spot, wc_sem, (at, p), (0, 1)).wait_recv()

    def add_chip(total, t, s, flips):
        first = turn(z_low, flips[0] // 2) * 4 + turn(y_at, flips[1] // 2) * 2
        for k in range(2):
            some = hid[first + k, t, wide(s)]
            for c in range(2):
                more = dot(some, weights[c, first + k])
                total[c] = more if total[c] is None else total[c] + more

    def gather_hidden(t, s):
        total = [None, None]
        add_chip(total, t, s, (0, 0))
        for j in range(3):
            hidden_in(t, s, j).wait_recv()
            add_chip(total, t, s, CHIPS[j])
        hidden_core(t, s).start()
        return total

    vocab_part = lax.broadcasted_iota(jnp.int32, (part, vocab_pad), 1)
    last_lane = lax.broadcasted_iota(jnp.int32, (1, vocab_pad), 1) == vocab_pad - 1
    small_acc[...] = jnp.zeros_like(small_acc)

    def lg_copy(t, s):
        spot = logit_grads.at[t, wide(s)]
        return copy(spot, spot, lg_sem, (t, s), (0, 1))

    def decode(t, s):
        here = span(s)
        logits = decb_pad[...]
        for at in range(8):
            logits = logits + dot(hid[at, t, wide(s)], dec_all[at])
        top = jnp.max(logits, axis=1, keepdims=True)
        exps = jnp.exp(logits - top)
        total = jnp.sum(exps, axis=1, keepdims=True)
        hot = targets[t, here, :1] == vocab_part
        picked = jnp.sum(jnp.where(hot, logits, 0.0), axis=1, keepdims=True)
        lost = top + jnp.log(total) - picked
        grad = ((exps / total - jnp.where(hot, 1.0, 0.0)) / tokens_all).astype(bf16)
        logit_grads[t, wide(s)] = grad
        lg_copy(t, s).start()
        small_acc[...] += jnp.sum(grad.astype(f32), axis=0, keepdims=True) + jnp.where(
            last_lane, jnp.sum(lost, axis=0, keepdims=True) / tokens_all, 0.0
        )

    def forward(t, _):
        for s in range(SPLIT):
            cell_step(t, s, gather_hidden(t - 1, s))
            decode(t - 1, s)
        return 0

    lax.fori_loop(1, steps, forward, 0)

    def pg_copy(t, s):
        return copy(pg_out.at[t, span(s)], pgs.at[t, wide(s)], pg_sem, (t, s), (0, 1))

    def pgm_copy(t, s):
        return copy(
            pgm_out.at[t - 1, span(s)], pgm.at[t - 1, wide(s)], pgm_sem, (t - 1, s), (0, 1)
        )

    def cell_back(t, s, carried, first):
        here = span(s)
        if not first:
            keep = keeps[t, here, :1]
        for c in range(2):
            hidden_grad = dot_t(logit_grads[t, wide(s)], dec_all[z_low * 4 + y_at * 2 + c])
            if carried is not None:
                hidden_grad = hidden_grad + carried[:, c * units : (c + 1) * units]
            in_gate = gates[t, c, here, :units]
            forget = gates[t, c, here, units : 2 * units]
            candidate = gates[t, c, here, 2 * units : 3 * units]
            out_gate = gates[t, c, here, 3 * units :]
            squash = jnp.tanh(cells[t, c, here])
            cell_grad = hidden_grad * out_gate * (1.0 - squash * squash)
            if carried is not None:
                cell_grad = cell_grad + carry_c[c, here]
            grads = [
                cell_grad * candidate * in_gate * (1.0 - in_gate),
                None,
                cell_grad * in_gate * (1.0 - candidate * candidate),
                hidden_grad * squash * out_gate * (1.0 - out_gate),
            ]
            if first:
                grads[1] = jnp.zeros_like(cell_grad)
            else:
                grads[1] = cell_grad * (keep * cells[t - 1, c, here]) * forget * (1.0 - forget)
                carry_c[c, here] = keep * forget * cell_grad
            for k in range(4):
                pg_now[c, here, k * units : (k + 1) * units] = grads[k].astype(bf16)
                if not first:
                    pgm_now[c, here, k * units : (k + 1) * units] = (keep * grads[k]).astype(bf16)

    def share(t, s, first):
        here = span(s)
        pgs[t, wide(s)] = pg_now[core, here]
        pg_out[t, here] = pg_now[1 - core, here]
        if not first:
            pgm[t - 1, wide(s)] = pgm_now[core, here]
            pgm_out[t - 1, here] = pgm_now[1 - core, here]
            pgm_copy(t, s).start()
        pg_copy(t, s).start()

    def chip_copy(t, s, j):
        return copy(
            chip_out.at[t - 1, s, j], chip_in.at[t - 1, s, j], chip_sem, (t - 1, s, j), CHIPS[j]
        )

    def spread(t, s):
        here = span(s)
        for j in (2, 0, 1, 3):
            flips = CHIPS[j] if j < 3 else (0, 0)
            first = turn(z_low, flips[0] // 2) * 4 + turn(y_at, flips[1] // 2) * 2
            for k in range(2):
                part_sum = dot_t(pgm_now[0, here], weights[0, first + k]) + dot_t(
                    pgm_now[1, here], weights[1, first + k]
                )
                lanes = slice(k * units, (k + 1) * units)
                if j < 3:
                    chip_out[t - 1, s, j, :, lanes] = part_sum.astype(bf16)
                else:
                    own_sum[s, :, lanes] = part_sum
            if j < 3:
                chip_copy(t, s, j).start()

    def carried_in(t, s):
        total = own_sum[s]
        for j in range(3):
            chip_copy(t + 1, s, j).wait_recv()
            total = total + chip_in[t, s, j].astype(f32)
        return total

    last = steps - 1
    for s in range(SPLIT):
        for j in range(3):
            hidden_in(last, s, j).wait_recv()
        hidden_core(last, s).start()
        decode(last, s)
        cell_back(last, s, None, False)
        spread(last, s)
        share(last, s, False)

    def backward(i, _):
        t = last - i
        for s in range(SPLIT):
            cell_back(t, s, carried_in(t, s), False)
            spread(t, s)
            share(t, s, False)
        return 0

    lax.fori_loop(1, last, backward, 0)

    far = (2, 3, 1, 0)

    piece_rows = LANES // SUB

    def x_copy(k, side, sub):
        here = pl.ds(sub * piece_rows, piece_rows)
        return copy(
            x_out.at[k, side, here], x_in.at[k, side, here], gx_sem, (k, side, sub), (1, 0)
        )

    def z_copy(k, side, sub):
        here = pl.ds(sub * piece_rows, piece_rows)
        return copy(
            z_out.at[k, side, here], z_in.at[k, side, here], gz_sem, (k, side, sub), (far[k] * 2, 0)
        )

    used = (steps - 1) * rows

    def from_core(t, first):
        for s in range(SPLIT):
            hidden_core_in(t, s).wait_recv()
            rows_there = pl.ds(pl.multiple_of((1 - core) * half + s * part, part), part)
            spot = logit_grads.at[t, rows_there]
            copy(spot, spot, lg_sem, (t, s), (0, 1)).wait_recv()
            spot = pgs.at[t, rows_there]
            copy(spot, spot, pg_sem, (t, s), (0, 1)).wait_recv()
            if not first:
                spot = pgm.at[t - 1, rows_there]
                copy(spot, spot, pgm_sem, (t - 1, s), (0, 1)).wait_recv()

    def all_from_core(t, _):
        from_core(t, False)
        return 0

    lax.fori_loop(1, steps, all_from_core, 0)
    hidden_0 = [hidden_core_in(0, s) for s in range(SPLIT)]
    for each in hidden_0:
        each.wait_recv()

    def weight_grad(k, side):
        at = side * 4 + turn(z_at, far[k])
        both[...] = t_dot(
            hid[at, 0 : steps - 1].reshape(used, units), pgm[...].reshape(used, cols)
        ).reshape(2, LANES, cols)
        x_out[k, side] = both[1 - x_at].astype(bf16)
        acc[k, side] = both[x_at]

    order = [(k, side, sub) for k in range(4) for side in range(2) for sub in range(SUB)]

    def send_x(first, last):
        for spot in order[first:last]:
            x_copy(*spot).start()

    def pass_z(at):
        k, side, sub = order[at]
        here = pl.ds(sub * piece_rows, piece_rows)
        x_copy(k, side, sub).wait_recv()
        total = acc[k, side, here] + x_in[k, side, here].astype(f32)
        if k == 3:
            acc[k, side, here] = total
            return
        z_out[k, side, here] = total.astype(bf16)
        if at in range(2, 4 * SUB):
            z_copy(*order[at - 2]).wait_send()
        z_copy(k, side, sub).start()

    weight_grad(0, 0)
    send_x(0, SUB)
    weight_grad(0, 1)
    send_x(SUB, 2 * SUB)
    weight_grad(1, 0)
    weight_grad(1, 1)
    pass_z(0)

    for s in range(SPLIT):
        cell_back(0, s, carried_in(0, s), True)
        share(0, s, True)
    small_pair[core] = small_acc[...]
    small_copy = copy(small_pair.at[core], small_pair.at[core], small_sem, (0,), (0, 1))
    small_copy.start()
    for s in range(SPLIT):
        rows_there = pl.ds(pl.multiple_of((1 - core) * half + s * part, part), part)
        spot = logit_grads.at[0, rows_there]
        copy(spot, spot, lg_sem, (0, s), (0, 1)).wait_recv()
        spot = pgs.at[0, rows_there]
        copy(spot, spot, pg_sem, (0, s), (0, 1)).wait_recv()
    spot = small_pair.at[1 - core]
    copy(spot, spot, small_sem, (0,), (0, 1)).wait_recv()
    tokens = steps * rows
    giw_rows = giw_acc.shape[0]
    giw_acc[...] = t_dot(
        embedded[...].reshape(tokens, LANES), pgs[...].reshape(tokens, cols)
    )[:giw_rows]
    for k in range(2):
        at = pl.multiple_of((1 - x_at) * (2 * units) + k * units, units)
        giw_out[k] = giw_acc[:, pl.ds(at, units)].astype(bf16)
    giw_x = copy(giw_out, giw_x_in, giw_sem, (0,), (1, 0))
    giw_x.start()
    dec_part[...] = t_dot(
        hid[own].reshape(tokens, units), logit_grads[...].reshape(tokens, vocab_pad)
    ).reshape(2, 2, dec_rows, vocab_pad)
    for k in range(2):
        dec_x_out[k] = dec_part[k, 1 - x_at].astype(bf16)
    dsum_x = copy(dec_x_out, dec_x_in, dsum_sem, (0,), (1, 0))
    dsum_x.start()
    send_x(2 * SUB, 3 * SUB)
    pass_z(1)

    emb_rows = emb_full.shape[1]
    by_char = jnp.zeros((vocab_rows, 2 * LANES), f32)
    for t in range(steps):
        by_token = dot_t(pgs[t], iw_pads[core])
        high = by_token.astype(bf16)
        low = (by_token - high.astype(f32)).astype(bf16)
        by_char = by_char + dot(onehots[t], jnp.concatenate([high, low], axis=1))
    emb_part[...] = (by_char[:, :LANES] + by_char[:, LANES:]).reshape(8, emb_rows, LANES)
    emb_copies = [
        copy(emb_part.at[slot(flips)], emb_in.at[own], emb_sem, (j,), flips)
        for j, flips in enumerate(GROUP)
    ]
    for each in emb_copies:
        each.start()
    emb_in[own] = emb_part[own]
    pass_z(2)
    send_x(3 * SUB, 4 * SUB)

    giw_x.wait_recv()
    for k in range(2):
        at = pl.multiple_of(x_at * (2 * units) + k * units, units)
        giw_acc[:, pl.ds(at, units)] += giw_x_in[k].astype(f32)
    giw_z_out[...] = giw_acc[
        :, pl.ds(pl.multiple_of(x_at * (2 * units) + (1 - z_high) * units, units), units)
    ].astype(bf16)
    giw_z = copy(giw_z_out, giw_z_in, giw_sem, (1,), (4, 0))
    giw_z.start()
    dsum_x.wait_recv()
    dec_z_out[...] = (
        dec_part[1 - z_high, x_at] + dec_x_in[1 - z_high].astype(f32)
    ).astype(bf16)
    dsum_z = copy(dec_z_out, dec_z_in, dsum_sem, (1,), (4, 0))
    dsum_z.start()
    for j, flips in enumerate(GROUP):
        spot = emb_in.at[slot(flips)]
        copy(spot, spot, emb_sem, (j,), flips).wait_recv()
    total = emb_in[0]
    for at in range(1, 8):
        total = total + emb_in[at]

    def place(flips):
        return turn(z_high, flips // 4) * 2 + turn(x_at, flips % 2)

    emb_sums[place(0), :emb_rows] = total
    smalls = small_pair[0] + small_pair[1]
    for k in range(vocab_pad // LANES):
        emb_sums[place(0), emb_rows + k : emb_rows + k + 1] = smalls[
            :, k * LANES : (k + 1) * LANES
        ]
    spot = emb_sums.at[place(0)]
    emb2 = [copy(spot, spot, emb2_sem, (j,), (flips, 0)) for j, flips in enumerate(OTHERS)]
    for each in emb2:
        each.start()
    pass_z(3)
    weight_grad(2, 0)
    weight_grad(2, 1)
    send_x(4 * SUB, 5 * SUB)
    weight_grad(3, 0)
    weight_grad(3, 1)

    giw_z.wait_recv()
    gate_at = x_at * 2 + z_high
    giw_full[z_low, gate_at] = (
        giw_acc[:, pl.ds(pl.multiple_of(gate_at * units, units), units)] + giw_z_in[...].astype(f32)
    ).astype(bf16)
    spot = giw_full.at[z_low, gate_at]
    giw_back_z = copy(spot, spot, giw_sem, (2,), (4, 0))
    giw_back_z.start()
    pass_z(4)
    send_x(5 * SUB, 6 * SUB)
    for j, flips in enumerate(OTHERS):
        spot = emb_sums.at[place(flips)]
        copy(spot, spot, emb2_sem, (j,), (flips, 0)).wait_recv()
    sums = (emb_sums[0] + emb_sums[1]) + (emb_sums[2] + emb_sums[3])
    emb_full[own] = sums[:emb_rows]
    spot = emb_full.at[own]
    emb3 = [copy(spot, spot, emb3_sem, (j,), flips) for j, flips in enumerate(GROUP)]
    for each in emb3:
        each.start()
    for k in range(vocab_pad // LANES):
        lanes = slice(k * LANES, min(vocab, (k + 1) * LANES))
        out_decb[:, lanes] = sums[emb_rows + k : emb_rows + k + 1, : lanes.stop - lanes.start]
    k = vocab_pad // LANES - 1
    out_loss[...] = sums[emb_rows + k : emb_rows + k + 1, LANES - 1 :]
    pass_z(5)
    spot = giw_full.at[z_low, x_at * 2 + 1 - z_high]
    copy(spot, spot, giw_sem, (2,), (4, 0)).wait_recv()
    spot = giw_full.at[z_low, pl.ds(x_at * 2, 2)]
    giw_back_x = copy(spot, spot, giw_sem, (3,), (1, 0))
    giw_back_x.start()
    send_x(6 * SUB, 8 * SUB)
    pass_z(6)
    dsum_z.wait_recv()
    total = dec_part[z_high, x_at] + dec_x_in[z_high].astype(f32) + dec_z_in[...].astype(f32)
    out_dec[...] = total[:, :vocab]
    spot = giw_full.at[z_low, pl.ds((1 - x_at) * 2, 2)]
    copy(spot, spot, giw_sem, (3,), (1, 0)).wait_recv()
    spot = giw_full.at[z_low]
    giw_side = copy(spot, spot, giw_sem, (4,), (2, 0))
    giw_side.start()
    pass_z(7)
    for j, flips in enumerate(GROUP):
        spot = emb_full.at[slot(flips)]
        copy(spot, spot, emb3_sem, (j,), flips).wait_recv()
    out_emb[...] = emb_full[...].reshape(vocab_rows, LANES)[:vocab, :width]
    for at in range(4 * SUB, 6 * SUB):
        pass_z(at)
    spot = giw_full.at[1 - z_low]
    copy(spot, spot, giw_sem, (4,), (2, 0)).wait_recv()
    for side in range(2):
        for gate in range(4):
            value = giw_full[side, gate].astype(f32)
            for run in range(runs):
                to = slice((run * 2 + side) * LANES, (run * 2 + side + 1) * LANES)
                lanes = slice(run * LANES, (run + 1) * LANES)
                out_iw[gate, :, to] = value[:width, lanes]
                out_gb[gate : gate + 1, to] = value[width : width + 1, lanes]
    for at in range(6 * SUB, 8 * SUB):
        pass_z(at)

    def scatter(here, side, gate, value):
        for run in range(runs):
            at = pl.multiple_of(gate * 2 * units + run * 2 * LANES + side * LANES, LANES)
            out_rec[here, pl.ds(at, LANES)] = value[:, run * LANES : (run + 1) * LANES]

    for side in range(2):
        for sub in range(SUB):
            z_copy(0, side, sub).wait_recv()
            z_copy(1, side, sub).wait_recv()
            z_copy(2, side, sub).wait_recv()
            here = pl.ds(side * LANES + sub * piece_rows, piece_rows)
            mine = pl.ds(sub * piece_rows, piece_rows)
            for gate in range(4):
                lanes = slice(gate * units, (gate + 1) * units)
                scatter(
                    here,
                    z_low,
                    gate,
                    acc[3, side, mine, lanes] + z_in[0, side, mine, lanes].astype(f32),
                )
                scatter(
                    here,
                    1 - z_low,
                    gate,
                    z_in[1, side, mine, lanes].astype(f32) + z_in[2, side, mine, lanes].astype(f32),
                )

    ids_copy.wait_send()
    dec_z.wait_send()
    for each in dec_x + dec_sends + dec_relays + iw_copies + [small_copy]:
        each.wait_send()
    for p in range(PIECES):
        for at in range(8):
            weight_core(block_of(at), at, p).wait_send()
        for k in range(3):
            weight_z(k, p).wait_send()
        for k in range(4):
            weight_x(k, p).wait_send()

    def sent(t, _):
        for s in range(SPLIT):
            for j in range(3):
                hidden_copy(t, s, j).wait_send()
            hidden_core(t, s).wait_send()
            lg_copy(t, s).wait_send()
            pg_copy(t, s).wait_send()
        return 0

    lax.fori_loop(0, steps, sent, 0)

    def sent_back(t, _):
        for s in range(SPLIT):
            pgm_copy(t, s).wait_send()
            for j in range(3):
                chip_copy(t, s, j).wait_send()
        return 0

    lax.fori_loop(1, steps, sent_back, 0)
    for at, spot in enumerate(order):
        x_copy(*spot).wait_send()
        if spot[0] < 3 and at not in range(4 * SUB - 2):
            z_copy(*spot).wait_send()
    for each in [giw_x, giw_z, giw_back_z, giw_back_x, giw_side, dsum_x, dsum_z]:
        each.wait_send()
    for each in emb_copies + emb2 + emb3:
        each.wait_send()


def grouped(
    char_ids,
    next_chars,
    resets,
    embedding,
    input_weight,
    recurrent_weight,
    gate_bias,
    decoder_weight,
    decoder_bias,
):
    data_count = lax.axis_size("dp")
    row_count, steps = char_ids.shape
    vocab, width = embedding.shape
    local_units = input_weight.shape[2]
    block = recurrent_weight.shape[0]
    units = local_units // 2
    cols = 4 * units
    rows = 2 * row_count
    dec_rows = decoder_weight.shape[2]
    vocab_pad = pl.cdiv(vocab, LANES) * LANES
    tokens_all = row_count * steps * data_count
    half = rows // 2
    part = half // SPLIT
    emb_rows = pl.cdiv(vocab, 64) * 8
    giw_rows = pl.cdiv(width + 1, 16) * 16

    vocab_rows = 8 * emb_rows
    by_gate = recurrent_weight.transpose(1, 0, 2)
    in_by_gate = input_weight.transpose(1, 0, 2)
    dec = decoder_weight.reshape(dec_rows, vocab)

    vmem = pl.BlockSpec(memory_space=pltpu.VMEM)
    dims = (steps, rows, units, vocab, vocab_pad, tokens_all, block)

    def sems(*shape):
        return pltpu.SemaphoreType.DMA((2,) + shape)

    loss, emb_grad, in_grad, rec_grad, bias_grad, dec_grad, dec_bias_grad = pl.pallas_call(
        functools.partial(layer_kernel, dims),
        out_shape=[
            jax.ShapeDtypeStruct((1, 1), f32),
            jax.ShapeDtypeStruct((vocab, width), f32),
            jax.ShapeDtypeStruct((4, width, local_units), f32),
            jax.ShapeDtypeStruct((block, 2 * cols), f32),
            jax.ShapeDtypeStruct((4, local_units), f32),
            jax.ShapeDtypeStruct((dec_rows, vocab), f32),
            jax.ShapeDtypeStruct((1, vocab), f32),
        ],
        in_specs=[vmem] * 9,
        out_specs=[vmem] * 7,
        scratch_shapes=[
            pltpu.VMEM((2, LANES, row_count), jnp.int32),
            pltpu.VMEM((row_count, LANES), jnp.int32),
            pltpu.VMEM((2, block, cols), bf16),
            pltpu.VMEM((2, 8, units, cols), bf16),
            pltpu.VMEM((vocab_rows, LANES), bf16),
            pltpu.VMEM((2, LANES, cols), bf16),
            pltpu.VMEM((2, 1, cols), f32),
            pltpu.VMEM((dec_rows, vocab_pad), bf16),
            pltpu.VMEM((1, vocab_pad), f32),
            pltpu.VMEM((8, units, vocab_pad), bf16),
            pltpu.VMEM((8, steps, rows, units), bf16),
            pltpu.VMEM((steps, 2, half, cols), f32),
            pltpu.VMEM((steps, 2, half, units), f32),
            pltpu.VMEM((steps, vocab_rows, rows), bf16),
            pltpu.VMEM((steps, rows, LANES), bf16),
            pltpu.VMEM((steps, half, LANES), f32),
            pltpu.VMEM((steps, half, LANES), jnp.int32),
            pltpu.VMEM((steps, rows, vocab_pad), bf16),
            pltpu.VMEM((steps, rows, cols), bf16),
            pltpu.VMEM((steps - 1, rows, cols), bf16),
            pltpu.VMEM((2, half, units), f32),
            pltpu.VMEM((2, half, cols), bf16),
            pltpu.VMEM((steps, half, cols), bf16),
            pltpu.VMEM((steps - 1, half, cols), bf16),
            pltpu.VMEM((2, half, cols), bf16),
            pltpu.VMEM((SPLIT, part, 2 * units), f32),
            pltpu.VMEM((steps - 1, SPLIT, 3, part, 2 * units), bf16),
            pltpu.VMEM((steps - 1, SPLIT, 3, part, 2 * units), bf16),
            pltpu.VMEM((1, vocab_pad), f32),
            pltpu.VMEM((2, 1, vocab_pad), f32),
            pltpu.VMEM((2, LANES, cols), f32),
            pltpu.VMEM((4, 2, LANES, cols), f32),
            pltpu.VMEM((4, 2, LANES, cols), bf16),
            pltpu.VMEM((4, 2, LANES, cols), bf16),
            pltpu.VMEM((3, 2, LANES, cols), bf16),
            pltpu.VMEM((3, 2, LANES, cols), bf16),
            pltpu.VMEM((giw_rows, cols), f32),
            pltpu.VMEM((2, giw_rows, units), bf16),
            pltpu.VMEM((2, giw_rows, units), bf16),
            pltpu.VMEM((giw_rows, units), bf16),
            pltpu.VMEM((giw_rows, units), bf16),
            pltpu.VMEM((2, 4, giw_rows, units), bf16),
            pltpu.VMEM((8, emb_rows, LANES), f32),
            pltpu.VMEM((8, emb_rows, LANES), f32),
            pltpu.VMEM((4, emb_rows + 8, LANES), f32),
            pltpu.VMEM((8, emb_rows, LANES), f32),
            pltpu.VMEM((2, 2, dec_rows, vocab_pad), f32),
            pltpu.VMEM((2, dec_rows, vocab_pad), bf16),
            pltpu.VMEM((2, dec_rows, vocab_pad), bf16),
            pltpu.VMEM((dec_rows, vocab_pad), bf16),
            pltpu.VMEM((dec_rows, vocab_pad), bf16),
            sems(1),
            sems(3, PIECES),
            sems(4, PIECES),
            sems(8, PIECES),
            sems(2),
            sems(3),
            sems(7),
            sems(steps, SPLIT, 3),
            sems(steps, SPLIT),
            sems(steps, SPLIT),
            sems(steps, SPLIT),
            sems(steps - 1, SPLIT),
            sems(1),
            sems(steps - 1, SPLIT, 3),
            sems(4, 2, SUB),
            sems(3, 2, SUB),
            sems(5),
            sems(7),
            sems(3),
            sems(7),
            sems(2),
        ],
        compiler_params=pltpu.CompilerParams(
            collective_id=0, has_side_effects=True, vmem_limit_bytes=62 << 20
        ),
    )(
        char_ids.T,
        next_chars.T,
        resets.T,
        embedding,
        in_by_gate,
        by_gate,
        gate_bias,
        dec,
        decoder_bias.reshape(1, vocab),
    )
    return (
        loss.reshape(()),
        emb_grad,
        in_grad.transpose(1, 0, 2),
        rec_grad.reshape(recurrent_weight.shape),
        bias_grad,
        dec_grad.reshape(decoder_weight.shape),
        dec_bias_grad.reshape(vocab),
    )


def on_device(
    char_ids,
    next_chars,
    resets,
    embedding,
    input_weight,
    recurrent_weight,
    gate_bias,
    decoder_weight,
    decoder_bias,
):
    highest = lax.Precision.HIGHEST
    data_count = lax.axis_size("dp")
    row_count, step_count = char_ids.shape
    vocab_size, width_in = embedding.shape
    local_units = input_weight.shape[2]
    gate_cols = 4 * local_units
    tokens_here = row_count * step_count
    tokens_all = tokens_here * data_count
    gathered_rec, gathered_dec = (
        lax.all_gather(recurrent_weight, "dp", axis=0, tiled=True),
        lax.all_gather(decoder_weight, "dp", axis=1, tiled=True),
    )
    hidden_total = gathered_rec.shape[0]
    rec_matrix = gathered_rec.reshape(hidden_total, gate_cols)
    dec_matrix = gathered_dec.reshape(local_units, vocab_size)
    time_ids = char_ids.T
    keep_mask = (1 - resets.T).astype(f32)
    proj_table = jnp.dot(
        embedding, input_weight.reshape(width_in, gate_cols), preferred_element_type=f32
    )
    projected = jnp.take(proj_table, time_ids, axis=0) + gate_bias.reshape(gate_cols)

    def forward_step(state_pair, inputs):
        hidden_loc, cell_state = state_pair
        proj_now, keep_now = inputs
        hidden_full = lax.all_gather(hidden_loc, "mp", axis=1, tiled=True)
        previous = hidden_full * keep_now[:, None].astype(bf16)
        preact = proj_now + jnp.dot(previous, rec_matrix, preferred_element_type=f32)
        gate_vals = preact.reshape(row_count, 4, local_units)
        in_gate = jax.nn.sigmoid(gate_vals[:, 0])
        forget_gate = jax.nn.sigmoid(gate_vals[:, 1])
        cell_gate = jnp.tanh(gate_vals[:, 2])
        out_gate = jax.nn.sigmoid(gate_vals[:, 3])
        new_cell = forget_gate * cell_state * keep_now[:, None] + in_gate * cell_gate
        new_hidden = (out_gate * jnp.tanh(new_cell)).astype(bf16)
        return ((new_hidden, new_cell), (previous, preact, new_cell, new_hidden))

    first_state = (
        jnp.zeros((row_count, local_units), bf16),
        jnp.zeros((row_count, local_units), f32),
    )
    _, (prevs, preacts, cells, hiddens) = lax.scan(
        forward_step, first_state, (projected, keep_mask)
    )
    flat_hidden = hiddens.reshape(tokens_here, local_units)
    partial_value = jnp.dot(flat_hidden, dec_matrix, preferred_element_type=f32)
    flat_targets = next_chars.T.reshape(tokens_here)
    logit_rows = lax.psum(partial_value, "mp")
    shifted_in = logit_rows + decoder_bias
    row_max = jnp.max(shifted_in, axis=1)
    exp_total = jnp.sum(jnp.exp(shifted_in - row_max[:, None]), axis=1)
    log_total = row_max + jnp.log(exp_total)
    softmax_out = jnp.exp(shifted_in - log_total[:, None])
    onehot = (flat_targets[:, None] == jnp.arange(vocab_size, dtype=jnp.int32)[None, :]).astype(f32)
    picked = jnp.sum(shifted_in * onehot, axis=1)
    grad_rows = ((softmax_out - onehot) / tokens_all).astype(bf16)
    local_loss = jnp.sum(log_total - picked) / tokens_all
    loss_part = jnp.where(lax.axis_index("mp") == 0, local_loss, jnp.zeros((), f32))
    out_grads = jnp.dot(grad_rows, dec_matrix.T, preferred_element_type=f32).reshape(
        step_count, row_count, local_units
    )
    dec_bias_part = jnp.sum(grad_rows.astype(f32), axis=0)
    columns = flat_hidden
    dec_grad = lax.psum_scatter(
        lax.dot_general(columns, grad_rows, (((0,), (0,)), ((), ())), preferred_element_type=f32),
        "dp",
        scatter_dimension=0,
        tiled=True,
    ).reshape(decoder_weight.shape)
    prev_cells = (
        jnp.concatenate([jnp.zeros((1, row_count, local_units), f32), cells[:-1]], axis=0)
        * keep_mask[:, :, None]
    )

    def backward_step(state_pair, inputs):
        carry_hidden, carry_cell = state_pair
        preact, cell_state, prev_cell, hidden_out, keep_now = inputs
        gate_vals = preact.reshape(row_count, 4, local_units)
        in_gate = jax.nn.sigmoid(gate_vals[:, 0])
        forget_gate = jax.nn.sigmoid(gate_vals[:, 1])
        cell_gate = jnp.tanh(gate_vals[:, 2])
        out_gate = jax.nn.sigmoid(gate_vals[:, 3])
        hidden_grad = hidden_out + carry_hidden
        squash = jnp.tanh(cell_state)
        cell_grad = hidden_grad * out_gate * (1.0 - squash * squash) + carry_cell
        grad_in = cell_grad * cell_gate * in_gate * (1.0 - in_gate)
        grad_forget = cell_grad * prev_cell * forget_gate * (1.0 - forget_gate)
        grad_cand = cell_grad * in_gate * (1.0 - cell_gate * cell_gate)
        grad_out = hidden_grad * squash * out_gate * (1.0 - out_gate)
        preact_grad = (
            jnp.stack([grad_in, grad_forget, grad_cand, grad_out], axis=1)
            .reshape(row_count, gate_cols)
            .astype(bf16)
        )
        back_term = lax.dot_general(
            preact_grad, rec_matrix, (((1,), (1,)), ((), ())), preferred_element_type=f32
        )
        next_hidden = (
            lax.psum_scatter(back_term, "mp", scatter_dimension=1, tiled=True) * keep_now[:, None]
        )
        next_cell = cell_grad * forget_gate * keep_now[:, None]
        return ((next_hidden, next_cell), preact_grad)

    zero_rows = jnp.zeros((row_count, local_units), f32)
    _, preact_grads = lax.scan(
        backward_step,
        (zero_rows, zero_rows),
        (preacts, cells, prev_cells, out_grads, keep_mask),
        reverse=True,
    )
    flat_prev = prevs.reshape(tokens_here, hidden_total)
    flat_pgrad = preact_grads.reshape(tokens_here, gate_cols)
    columns = flat_prev
    rec_grad = lax.psum_scatter(
        lax.dot_general(columns, flat_pgrad, (((0,), (0,)), ((), ())), preferred_element_type=f32),
        "dp",
        scatter_dimension=0,
        tiled=True,
    ).reshape(recurrent_weight.shape)
    onehot_ids = (
        time_ids.reshape(tokens_here)[:, None] == jnp.arange(vocab_size, dtype=jnp.int32)[None, :]
    ).astype(bf16)
    table_part = lax.dot_general(
        onehot_ids, flat_pgrad, (((0,), (0,)), ((), ())), preferred_element_type=f32
    )
    table_sum, dec_bias_grad, loss_data = lax.psum((table_part, dec_bias_part, loss_part), "dp")
    in_grad = jnp.dot(embedding.astype(f32).T, table_sum, precision=highest).reshape(
        width_in, 4, local_units
    )
    bias_grad = jnp.sum(table_sum, axis=0).reshape(4, local_units)
    emb_part = lax.dot_general(
        table_sum,
        input_weight.reshape(width_in, gate_cols).astype(f32),
        (((1,), (1,)), ((), ())),
        precision=highest,
    )
    emb_grad, loss = lax.psum((emb_part, loss_data), "mp")
    return (loss, emb_grad, in_grad, rec_grad, bias_grad, dec_grad, dec_bias_grad)


def solution(mesh):
    in_specs = (
        P("dp", None),
        P("dp", None),
        P("dp", None),
        P(),
        P(None, None, "mp"),
        P("dp", None, "mp"),
        P(None, "mp"),
        P("mp", "dp", None, None),
        P(),
    )
    out_specs = (
        P(),
        P(),
        P(None, None, "mp"),
        P("dp", None, "mp"),
        P(None, "mp"),
        P("mp", "dp", None, None),
        P(),
    )
    fits = (mesh.shape["dp"], mesh.shape["mp"]) == (8, 4)
    return jax.shard_map(
        grouped if fits else on_device,
        mesh=mesh,
        in_specs=in_specs,
        out_specs=out_specs,
        check_vma=False,
    )
```

```python
import functools

import jax
import jax.numpy as jnp
from jax import lax
from jax.experimental import pallas as pl
from jax.experimental.pallas import tpu as pltpu
from jax.sharding import PartitionSpec as P

f32 = jnp.float32
bf16 = jnp.bfloat16
MESH = pl.DeviceIdType.MESH
LANES = 128
CHIPS = ((2, 0), (0, 2), (2, 2))
PEERS = ((0, 1), (2, 0), (0, 2), (2, 2), (2, 1), (0, 3), (2, 3), (1, 0), (4, 0), (5, 0), (6, 0))
GROUP = ((0, 1), (2, 0), (0, 2), (2, 2), (2, 1), (0, 3), (2, 3))
OTHERS = (1, 4, 5)
COLUMN = (4, 6, 2)
SPLIT = 2
PIECES = 8
LAG = 2
EARLY = 3
SUB = 4


def turn(value, flips):
    for bit in (1, 2, 4):
        if flips & bit:
            value = value + bit - 2 * bit * lax.rem(lax.div(value, bit), 2)
    return value


def dot(a, b):
    return jnp.dot(a, b, preferred_element_type=f32)


def dot_t(a, b):
    return lax.dot_general(a, b, (((1,), (1,)), ((), ())), preferred_element_type=f32)


def t_dot(a, b):
    return lax.dot_general(a, b, (((0,), (0,)), ((), ())), preferred_element_type=f32)


def layer_kernel(
    dims,
    chars_ref,
    nexts_ref,
    resets_ref,
    emb_ref,
    iw_ref,
    rec_ref,
    gb_ref,
    dec_ref,
    decb_ref,
    out_loss,
    out_emb,
    out_iw,
    out_rec,
    out_gb,
    out_dec,
    out_decb,
    rec_in,
    iw_in,
    rec_final,
    iw_final,
    gb_final,
    loss_final,
    decb_final,
    dec_final,
    emb_final,
    ids_rows,
    ids_cols,
    rec_halves,
    weights,
    emb_pad,
    iw_pads,
    gb_pads,
    dec_pad,
    decb_pad,
    dec_all,
    hid,
    gates,
    cells,
    onehots,
    embedded,
    keeps,
    targets,
    logit_grads,
    pgs,
    pgm,
    carry_c,
    pg_now,
    pg_out,
    pgm_out,
    pgm_now,
    own_sum,
    chip_out,
    chip_in,
    small_acc,
    small_pair,
    both,
    acc,
    x_out,
    x_in,
    z_out,
    z_in,
    giw_acc,
    giw_out,
    giw_x_in,
    giw_z_out,
    giw_z_in,
    giw_full,
    emb_part,
    emb_in,
    emb_sums,
    emb_full,
    dec_part,
    dec_x_out,
    dec_x_in,
    dec_z_out,
    dec_z_in,
    in_sem,
    out_sem,
    ids_sem,
    wz_sem,
    wx_sem,
    wc_sem,
    iw_sem,
    decg_sem,
    decr_sem,
    hid_sem,
    hidc_sem,
    lg_sem,
    pg_sem,
    pgm_sem,
    small_sem,
    chip_sem,
    gx_sem,
    gz_sem,
    giw_sem,
    emb_sem,
    emb2_sem,
    emb3_sem,
    dsum_sem,
):
    steps, rows, units, vocab, vocab_pad, tokens_all, block = dims
    cols = 4 * units
    half = rows // 2
    part = half // SPLIT
    d, m = lax.axis_index("dp"), lax.axis_index("mp")
    x_at, z_low, z_high = lax.rem(d, 2), lax.rem(lax.div(d, 2), 2), lax.div(d, 4)
    z_at = lax.div(d, 2)
    core, y_at = lax.rem(m, 2), lax.div(m, 2)

    def device(flips):
        return (turn(d, flips[0]), turn(m, flips[1]))

    def slot(flips):
        return turn(z_low, flips[0] // 2) * 4 + turn(m, flips[1])

    def chip(flips):
        return pl.ds(turn(z_low, flips[0] // 2) * 4 + turn(y_at, flips[1] // 2) * 2, 2)

    own = slot((0, 0))

    def copy(src, dst, sems, at, flips):
        return pltpu.make_async_remote_copy(
            src_ref=src,
            dst_ref=dst,
            send_sem=sems.at[(0,) + at],
            recv_sem=sems.at[(1,) + at],
            device_id=device(flips),
            device_id_type=MESH,
        )

    sizes = [block // PIECES] * (PIECES - 1) + [block // PIECES // 2] * 2
    pieces = [(sum(sizes[:p]), size) for p, size in enumerate(sizes)]
    rec_loads = [
        pltpu.make_async_copy(
            rec_ref.at[pl.ds(first, size)], rec_in.at[pl.ds(first, size)], in_sem.at[p]
        )
        for p, (first, size) in enumerate(pieces)
    ]
    iw_load = pltpu.make_async_copy(iw_ref, iw_in, in_sem.at[PIECES + 1])
    for each in rec_loads + [iw_load]:
        each.start()

    barrier = pltpu.get_barrier_semaphore()
    for flips in PEERS:
        pl.semaphore_signal(barrier, inc=1, device_id=device(flips), device_id_type=MESH)
    pl.semaphore_wait(barrier, len(PEERS))


    def weight_rows(index, p):
        first, size = pieces[p]
        side, inside = first // LANES, first % LANES
        return weights.at[
            core,
            side * 4 + lax.div(index, 2),
            :,
            pl.ds(pl.multiple_of(lax.rem(index, 2) * LANES + inside, size), size),
        ]

    def weight_core(index, at, p):
        spot = weight_rows(index, p)
        return copy(spot, spot, wc_sem, (at, p), (0, 1))

    def block_of(at):
        return turn(d, (0, 4, 6, 2)[at % 4] + at // 4)

    def weight_z(k, p):
        flips = COLUMN[k]
        half = turn(z_low, (flips & 2) // 2)
        return copy(
            rec_halves.at[half, :, pl.ds(*pieces[p])], weight_rows(d, p), wz_sem, (k, p), (flips, 0)
        )

    def weight_z_in(k, p):
        spot = weight_rows(turn(d, COLUMN[k]), p)
        return copy(spot, spot, wz_sem, (k, p), (COLUMN[k], 0))

    def weight_x(k, p):
        if k == 3:
            return copy(
                rec_halves.at[z_low, :, pl.ds(*pieces[p])],
                weight_rows(d, p),
                wx_sem,
                (k, p),
                (1, 0),
            )
        spot = weight_rows(turn(d, COLUMN[k]), p)
        return copy(spot, spot, wx_sem, (k, p), (1, 0))

    def weight_x_in(k, p):
        flips = 0 if k == 3 else COLUMN[k]
        spot = weight_rows(turn(d, flips + 1), p)
        return copy(spot, spot, wx_sem, (k, p), (1, 0))

    runs = units // LANES
    width = iw_ref.shape[0]
    dec_rows = dec_ref.shape[0]
    vocab_rows = emb_pad.shape[0]

    def dec_spot(flips):
        at = turn(z_high, flips // 4) * LANES + turn(x_at, flips % 2) * dec_rows
        return dec_all.at[own, pl.ds(pl.multiple_of(at, dec_rows), dec_rows)]

    ids_rows[z_low, 0:steps] = chars_ref[...]
    ids_rows[z_low, 8 : 8 + steps] = nexts_ref[...]
    ids_rows[z_low, 16 : 16 + steps] = resets_ref[...]
    ids_copy = copy(ids_rows.at[z_low], ids_rows.at[z_low], ids_sem, (0,), (2, 0))
    ids_copy.start()

    def weight_start(p):
        for k in range(3):
            weight_z(k, p).start()
        weight_x(3, p).start()

    for p, (first, size) in enumerate(pieces):
        here = slice(first, first + size)
        rec_loads[p].wait()
        for gate in range(4):
            for run in range(runs):
                for side in range(2):
                    at = (run * 2 + side) * LANES
                    to = run * LANES
                    rec_halves[side, gate, here, to : to + LANES] = rec_in[here, gate, at : at + LANES]
        if p < EARLY:
            weight_start(p)
        if p == 0:
            dec_pad[...] = jnp.zeros_like(dec_pad)
            dec_pad[:, :vocab] = dec_ref[...]
            dec_z = copy(dec_pad, dec_spot(0), decg_sem, (0,), (4, 0))
            dec_z.start()
            dec_x = [copy(dec_pad, dec_spot(0), decg_sem, (1,), (1, 0))]
            dec_x[0].start()

    def weight_round(p):
        for k in range(3):
            weight_z_in(k, p).wait_recv()
            weight_x(k, p).start()
            weight_core(block_of(1 + k), 1 + k, p).start()
        if p >= LAG:
            weight_over_x(p - LAG)

    def weights_from_core(which):
        for p in which:
            for at in range(8):
                index = block_of(at)
                first, size = pieces[p]
                inside = first % LANES
                spot = weights.at[
                    1 - core,
                    first // LANES * 4 + lax.div(index, 2),
                    :,
                    pl.ds(pl.multiple_of(lax.rem(index, 2) * LANES + inside, size), size),
                ]
                copy(spot, spot, wc_sem, (at, p), (0, 1)).wait_recv()

    def weight_over_x(p):
        for k in (3, 0, 1, 2):
            weight_x_in(k, p).wait_recv()
            at = 4 if k == 3 else 5 + k
            weight_core(block_of(at), at, p).start()

    for p in range(PIECES + 1):
        weight_rows(d, p)[...] = rec_halves[z_low, :, pl.ds(*pieces[p])]
        weight_core(block_of(0), 0, p).start()
    dec_spot(0)[...] = dec_pad[...]
    emb_pad[...] = jnp.zeros_like(emb_pad)
    emb_pad[:vocab, :width] = emb_ref[...]
    ones_at = lax.broadcasted_iota(jnp.int32, emb_pad.shape, 1) == width
    emb_pad[...] = jnp.where(ones_at, 1.0, emb_pad[...].astype(f32)).astype(bf16)
    iw_pads[core] = jnp.zeros(iw_pads.shape[1:], bf16)
    iw_load.wait()

    def half_lanes(run):
        return pl.ds(pl.multiple_of((run * 2 + z_low) * LANES, LANES), LANES)

    for gate in range(4):
        for run in range(runs):
            to = gate * units + run * LANES
            iw_pads[core, :width, to : to + LANES] = iw_in[:, gate, half_lanes(run)]
            gb_pads[core, :, to : to + LANES] = gb_ref[gate : gate + 1, half_lanes(run)]
    iw_copies = [
        copy(ref.at[core], ref.at[core], iw_sem, (k,), (0, 1))
        for k, ref in enumerate((iw_pads, gb_pads))
    ]
    for each in iw_copies:
        each.start()
    decb_pad[...] = jnp.full(decb_pad.shape, -1e30, f32)
    decb_pad[0, :vocab] = decb_ref[...]
    ids_copy.wait_recv()
    ids_cols[...] = ids_rows[core].T
    vocab_iota = lax.broadcasted_iota(jnp.int32, (vocab_rows, rows), 0)

    def read_ids(t):
        now = jnp.concatenate([ids_rows[0, t : t + 1], ids_rows[1, t : t + 1]], axis=1)
        onehots[t] = (vocab_iota == now).astype(f32).astype(bf16)
        targets[t] = jnp.broadcast_to(ids_cols[:, 8 + t : 9 + t], (half, LANES))
        keeps[t] = jnp.broadcast_to((1 - ids_cols[:, 16 + t : 17 + t]).astype(f32), (half, LANES))

    def project(t):
        read_ids(t)
        chosen = t_dot(onehots[t], emb_pad[...]).astype(bf16)
        embedded[t] = chosen
        mine = embedded[t, pl.ds(pl.multiple_of(core * half, half), half)]
        for c in range(2):
            gates[t, c] = dot(mine, iw_pads[c]) + gb_pads[c]

    for k, ref in enumerate((iw_pads, gb_pads)):
        copy(ref.at[1 - core], ref.at[1 - core], iw_sem, (k,), (0, 1)).wait_recv()
    project(0)

    def span(s):
        return pl.ds(s * part, part)

    def wide(s):
        return pl.ds(pl.multiple_of(core * half + s * part, part), part)

    def hidden_copy(t, s, j):
        spot = hid.at[chip((0, 0)), t, wide(s)]
        return copy(spot, spot, hid_sem, (t, s, j), CHIPS[j])

    def hidden_in(t, s, j):
        spot = hid.at[chip(CHIPS[j]), t, wide(s)]
        return copy(spot, spot, hid_sem, (t, s, j), CHIPS[j])

    def hidden_core(t, s):
        spot = hid.at[:, t, wide(s)]
        return copy(spot, spot, hidc_sem, (t, s), (0, 1))

    def hidden_core_in(t, s):
        rows_there = pl.ds(pl.multiple_of((1 - core) * half + s * part, part), part)
        spot = hid.at[:, t, rows_there]
        return copy(spot, spot, hidc_sem, (t, s), (0, 1))

    def cell_step(t, s, added):
        here = span(s)
        if added is not None:
            keep = keeps[t, here, :1]
        for c in range(2):
            preact = [gates[t, c, here, k * units : (k + 1) * units] for k in range(4)]
            if added is not None:
                preact = [preact[k] + keep * added[c][k] for k in range(4)]
            in_gate = jax.nn.sigmoid(preact[0])
            forget = jax.nn.sigmoid(preact[1])
            candidate = jnp.tanh(preact[2])
            out_gate = jax.nn.sigmoid(preact[3])
            cell = in_gate * candidate
            if added is not None:
                cell = forget * keep * cells[t - 1, c, here] + cell
            cells[t, c, here] = cell
            hid[z_low * 4 + y_at * 2 + c, t, wide(s)] = (out_gate * jnp.tanh(cell)).astype(bf16)
            gates[t, c, here, :units] = in_gate
            gates[t, c, here, units : 2 * units] = forget
            gates[t, c, here, 2 * units : 3 * units] = candidate
            gates[t, c, here, 3 * units :] = out_gate
        for j in (2, 0, 1):
            hidden_copy(t, s, j).start()

    def add_slot(total, t, s, at):
        some = hid[at, t, wide(s)]
        for c in range(2):
            for gate in range(4):
                more = dot(some, weights[c, at, gate])
                total[c][gate] = more if total[c][gate] is None else total[c][gate] + more

    for s in range(SPLIT):
        cell_step(0, s, None)

    for p in range(EARLY, PIECES + 1):
        weight_start(p)
    weight_round(0)
    project(1)
    project(2)
    weight_round(1)
    spot = dec_spot(4)
    copy(spot, spot, decg_sem, (0,), (4, 0)).wait_recv()
    dec_x.append(copy(spot, spot, decg_sem, (2,), (1, 0)))
    dec_x[1].start()
    project(3)
    weight_round(2)
    project(4)
    project(5)
    weight_round(3)
    for j, flips in enumerate((1, 5)):
        spot = dec_spot(flips)
        copy(spot, spot, decg_sem, (1 + j,), (1, 0)).wait_recv()
    dec_own = dec_all.at[own]
    dec_sends = [
        copy(dec_own, dec_own, decr_sem, (j,), flips) for j, flips in enumerate(CHIPS + ((0, 1),))
    ]
    for each in dec_sends:
        each.start()
    weight_round(4)
    weight_round(5)
    weights_from_core(range(PIECES // 2))
    for s in range(SPLIT):
        for j in range(3):
            hidden_in(0, s, j).wait_recv()
        total = [[None] * 4, [None] * 4]
        for at in range(4):
            add_slot(total, 0, s, at)
        for c in range(2):
            for gate in range(4):
                lanes = slice(gate * units, (gate + 1) * units)
                gates[1, c, span(s), lanes] += keeps[1, span(s), :1] * total[c][gate]
    for p in range(6, PIECES + 1):
        weight_round(p)
    for p in range(PIECES + 1 - LAG, PIECES + 1):
        weight_over_x(p)
    weights_from_core(range(PIECES // 2, PIECES + 1))

    dec_relays = []
    for j in range(3):
        spot = dec_all.at[slot(CHIPS[j])]
        copy(spot, spot, decr_sem, (j,), CHIPS[j]).wait_recv()
        dec_relays.append(copy(spot, spot, decr_sem, (4 + j,), (0, 1)))
        dec_relays[-1].start()

    def add_chip(total, t, s, flips):
        first = turn(z_low, flips[0] // 2) * 4 + turn(y_at, flips[1] // 2) * 2
        for k in range(2):
            add_slot(total, t, s, first + k)

    def gather_hidden(t, s):
        total = [[None] * 4, [None] * 4]
        add_chip(total, t, s, (0, 0))
        for j in range(3):
            hidden_in(t, s, j).wait_recv()
            add_chip(total, t, s, CHIPS[j])
        hidden_core(t, s).start()
        return total

    vocab_part = lax.broadcasted_iota(jnp.int32, (part, vocab_pad), 1)
    last_lane = lax.broadcasted_iota(jnp.int32, (1, vocab_pad), 1) == vocab_pad - 1
    small_acc[...] = jnp.zeros_like(small_acc)

    def lg_copy(t, s):
        spot = logit_grads.at[t, wide(s)]
        return copy(spot, spot, lg_sem, (t, s), (0, 1))

    def decode(t, s):
        here = span(s)
        logits = decb_pad[...]
        for at in range(8):
            logits = logits + dot(hid[at, t, wide(s)], dec_all[at])
        top = jnp.max(logits, axis=1, keepdims=True)
        exps = jnp.exp(logits - top)
        total = jnp.sum(exps, axis=1, keepdims=True)
        hot = targets[t, here, :1] == vocab_part
        picked = jnp.sum(jnp.where(hot, logits, 0.0), axis=1, keepdims=True)
        lost = top + jnp.log(total) - picked
        grad = ((exps / total - jnp.where(hot, 1.0, 0.0)) / tokens_all).astype(bf16)
        logit_grads[t, wide(s)] = grad
        lg_copy(t, s).start()
        small_acc[...] += jnp.sum(grad.astype(f32), axis=0, keepdims=True) + jnp.where(
            last_lane, jnp.sum(lost, axis=0, keepdims=True) / tokens_all, 0.0
        )

    def forward(t, _):
        for s in range(SPLIT):
            cell_step(t, s, gather_hidden(t - 1, s))
            decode(t - 1, s)
        return 0

    for s in range(SPLIT):
        total = [[None] * 4, [None] * 4]
        for at in range(4, 8):
            add_slot(total, 0, s, at)
        cell_step(1, s, total)
        hidden_core(0, s).start()
    spot = dec_all.at[slot((0, 1))]
    copy(spot, spot, decr_sem, (3,), (0, 1)).wait_recv()
    for j in range(3):
        spot = dec_all.at[slot((CHIPS[j][0], CHIPS[j][1] + 1))]
        copy(spot, spot, decr_sem, (4 + j,), (0, 1)).wait_recv()
    for s in range(SPLIT):
        decode(0, s)
    lax.fori_loop(2, steps, forward, 0)

    def pg_copy(t, s):
        return copy(pg_out.at[t, span(s)], pgs.at[t, wide(s)], pg_sem, (t, s), (0, 1))

    def pgm_copy(t, s):
        return copy(
            pgm_out.at[t - 1, span(s)], pgm.at[t - 1, wide(s)], pgm_sem, (t - 1, s), (0, 1)
        )

    def cell_back(t, s, carried, first):
        here = span(s)
        if not first:
            keep = keeps[t, here, :1]
        for c in range(2):
            hidden_grad = dot_t(logit_grads[t, wide(s)], dec_all[z_low * 4 + y_at * 2 + c])
            if carried is not None:
                hidden_grad = hidden_grad + carried[:, c * units : (c + 1) * units]
            in_gate = gates[t, c, here, :units]
            forget = gates[t, c, here, units : 2 * units]
            candidate = gates[t, c, here, 2 * units : 3 * units]
            out_gate = gates[t, c, here, 3 * units :]
            squash = jnp.tanh(cells[t, c, here])
            cell_grad = hidden_grad * out_gate * (1.0 - squash * squash)
            if carried is not None:
                cell_grad = cell_grad + carry_c[c, here]
            grads = [
                cell_grad * candidate * in_gate * (1.0 - in_gate),
                None,
                cell_grad * in_gate * (1.0 - candidate * candidate),
                hidden_grad * squash * out_gate * (1.0 - out_gate),
            ]
            if first:
                grads[1] = jnp.zeros_like(cell_grad)
            else:
                grads[1] = cell_grad * (keep * cells[t - 1, c, here]) * forget * (1.0 - forget)
                carry_c[c, here] = keep * forget * cell_grad
            for k in range(4):
                pg_now[c, here, k * units : (k + 1) * units] = grads[k].astype(bf16)
                if not first:
                    pgm_now[c, here, k * units : (k + 1) * units] = (keep * grads[k]).astype(bf16)

    def share(t, s, first):
        here = span(s)
        pgs[t, wide(s)] = pg_now[core, here]
        pg_out[t, here] = pg_now[1 - core, here]
        if not first:
            pgm[t - 1, wide(s)] = pgm_now[core, here]
            pgm_out[t - 1, here] = pgm_now[1 - core, here]
            pgm_copy(t, s).start()
        pg_copy(t, s).start()

    def chip_copy(t, s, j):
        return copy(
            chip_out.at[t - 1, s, j], chip_in.at[t - 1, s, j], chip_sem, (t - 1, s, j), CHIPS[j]
        )

    def spread(t, s):
        here = span(s)
        for j in (2, 0, 1, 3):
            flips = CHIPS[j] if j < 3 else (0, 0)
            first = turn(z_low, flips[0] // 2) * 4 + turn(y_at, flips[1] // 2) * 2
            for k in range(2):
                part_sum = None
                for c in range(2):
                    for gate in range(4):
                        grad = pgm_now[c, here, gate * units : (gate + 1) * units]
                        more = dot(grad, weights[c, first + k, gate])
                        part_sum = more if part_sum is None else part_sum + more
                lanes = slice(k * units, (k + 1) * units)
                if j < 3:
                    chip_out[t - 1, s, j, :, lanes] = part_sum.astype(bf16)
                else:
                    own_sum[s, :, lanes] = part_sum
            if j < 3:
                chip_copy(t, s, j).start()

    def carried_in(t, s):
        total = own_sum[s]
        for j in range(3):
            chip_copy(t + 1, s, j).wait_recv()
            total = total + chip_in[t, s, j].astype(f32)
        return total

    last = steps - 1

    for p in range(PIECES + 1):
        for at in range(8):
            weight_core(block_of(at), at, p).wait_send()
        for k in range(4):
            weight_x(k, p).wait_send()

    def turn_over(at, _):
        for c in range(2):
            for gate in range(4):
                weights[c, at, gate] = weights[c, at, gate].T
        return 0

    lax.fori_loop(0, 8, turn_over, 0)
    for s in range(SPLIT):
        for j in range(3):
            hidden_in(last, s, j).wait_recv()
        hidden_core(last, s).start()
        decode(last, s)
        cell_back(last, s, None, False)
        spread(last, s)
        share(last, s, False)

    def other_rows(s):
        return pl.ds(pl.multiple_of((1 - core) * half + s * part, part), part)

    def dsum_x():
        return copy(dec_x_out, dec_x_in, dsum_sem, (0,), (1, 0))

    def dsum_z(k):
        return copy(dec_z_out, dec_z_in, dsum_sem, (k,), (4, 0))

    def small_copy():
        return copy(small_pair.at[core], small_pair.at[core], small_sem, (0,), (0, 1))

    def decoder_grad():
        for t in range(steps):
            for s in range(SPLIT):
                hidden_core_in(t, s).wait_recv()
                spot = logit_grads.at[t, other_rows(s)]
                copy(spot, spot, lg_sem, (t, s), (0, 1)).wait_recv()
        small_pair[core] = small_acc[...]
        small_copy().start()
        dec_part[...] = t_dot(
            hid[own].reshape(steps * rows, units),
            logit_grads[...].reshape(steps * rows, vocab_pad),
        ).reshape(2, 2, dec_rows, vocab_pad)
        for k in range(2):
            dec_x_out[k] = dec_part[k, 1 - x_at].astype(bf16)
        dsum_x().start()

    def decoder_grad_z():
        dsum_x().wait_recv()
        dec_z_out[...] = (
            dec_part[1 - z_high, x_at] + dec_x_in[1 - z_high].astype(f32)
        ).astype(bf16)
        dsum_z(1).start()

    def backward(i, _):
        t = last - i
        for s in range(SPLIT):
            cell_back(t, s, carried_in(t, s), False)
            spread(t, s)
            share(t, s, False)

        @pl.when(i == 2)
        def _():
            decoder_grad()

        @pl.when(i == 3)
        def _():
            decoder_grad_z()

        return 0

    lax.fori_loop(1, last, backward, 0)

    far = (2, 3, 1, 0)

    piece_rows = LANES // SUB

    def x_copy(k, side, sub):
        here = pl.ds(sub * piece_rows, piece_rows)
        return copy(
            x_out.at[k, side, here], x_in.at[k, side, here], gx_sem, (k, side, sub), (1, 0)
        )

    def z_copy(k, side, sub):
        here = pl.ds(sub * piece_rows, piece_rows)
        return copy(
            z_out.at[k, side, here], z_in.at[k, side, here], gz_sem, (k, side, sub), (far[k] * 2, 0)
        )

    used = (steps - 1) * rows

    def from_core(t, _):
        for s in range(SPLIT):
            spot = pgs.at[t, other_rows(s)]
            copy(spot, spot, pg_sem, (t, s), (0, 1)).wait_recv()
            spot = pgm.at[t - 1, other_rows(s)]
            copy(spot, spot, pgm_sem, (t - 1, s), (0, 1)).wait_recv()
        return 0

    lax.fori_loop(1, steps, from_core, 0)

    def weight_grad(k, side):
        at = side * 4 + turn(z_at, far[k])
        both[...] = t_dot(
            hid[at, 0 : steps - 1].reshape(used, units), pgm[...].reshape(used, cols)
        ).reshape(2, LANES, cols)
        x_out[k, side] = both[1 - x_at].astype(bf16)
        acc[k, side] = both[x_at]

    order = [(k, side, sub) for k in range(4) for side in range(2) for sub in range(SUB)]

    def send_eighth(*which):
        for at in which:
            for k in range(SUB // 2):
                x_copy(*order[at * (SUB // 2) + k]).start()

    def pass_z(at):
        for k in range(SUB // 2):
            pass_piece(at * (SUB // 2) + k)

    def pass_piece(at):
        k, side, sub = order[at]
        here = pl.ds(sub * piece_rows, piece_rows)
        x_copy(k, side, sub).wait_recv()
        total = acc[k, side, here] + x_in[k, side, here].astype(f32)
        if k == 3:
            acc[k, side, here] = total
            return
        z_out[k, side, here] = total.astype(bf16)
        if at in range(SUB, 4 * SUB):
            z_copy(*order[at - SUB]).wait_send()
        z_copy(k, side, sub).start()

    weight_grad(0, 0)
    send_eighth(0, 1)
    weight_grad(0, 1)
    send_eighth(2, 3)
    pass_z(0)

    for s in range(SPLIT):
        cell_back(0, s, carried_in(0, s), True)
        share(0, s, True)
    for s in range(SPLIT):
        spot = pgs.at[0, other_rows(s)]
        copy(spot, spot, pg_sem, (0, s), (0, 1)).wait_recv()
    tokens = steps * rows
    giw_rows = giw_acc.shape[0]
    giw_acc[...] = t_dot(
        embedded[...].reshape(tokens, LANES), pgs[...].reshape(tokens, cols)
    )[:giw_rows]
    for k in range(2):
        at = pl.multiple_of((1 - x_at) * (2 * units) + k * units, units)
        giw_out[k] = giw_acc[:, pl.ds(at, units)].astype(bf16)
    giw_x = copy(giw_out, giw_x_in, giw_sem, (0,), (1, 0))
    giw_x.start()
    pass_z(1)
    weight_grad(1, 0)
    weight_grad(2, 0)
    send_eighth(4, 8)

    emb_rows = emb_full.shape[1]
    by_char = jnp.zeros((vocab_rows, 2 * LANES), f32)
    for t in range(steps):
        by_token = dot_t(pgs[t], iw_pads[core])
        high = by_token.astype(bf16)
        low = (by_token - high.astype(f32)).astype(bf16)
        by_char = by_char + dot(onehots[t], jnp.concatenate([high, low], axis=1))
    emb_part[...] = (by_char[:, :LANES] + by_char[:, LANES:]).reshape(8, emb_rows, LANES)
    emb_copies = [
        copy(emb_part.at[slot(flips)], emb_in.at[own], emb_sem, (j,), flips)
        for j, flips in enumerate(GROUP)
    ]
    for each in emb_copies:
        each.start()
    emb_in[own] = emb_part[own]
    pass_z(2)
    weight_grad(1, 1)
    weight_grad(2, 1)
    send_eighth(5, 9)

    giw_x.wait_recv()
    for k in range(2):
        at = pl.multiple_of(x_at * (2 * units) + k * units, units)
        giw_acc[:, pl.ds(at, units)] += giw_x_in[k].astype(f32)
    giw_z_out[...] = giw_acc[
        :, pl.ds(pl.multiple_of(x_at * (2 * units) + (1 - z_high) * units, units), units)
    ].astype(bf16)
    giw_z = copy(giw_z_out, giw_z_in, giw_sem, (1,), (4, 0))
    giw_z.start()
    for j, flips in enumerate(GROUP):
        spot = emb_in.at[slot(flips)]
        copy(spot, spot, emb_sem, (j,), flips).wait_recv()
    total = emb_in[0]
    for at in range(1, 8):
        total = total + emb_in[at]

    def place(flips):
        return turn(z_high, flips // 4) * 2 + turn(x_at, flips % 2)

    emb_sums[place(0), :emb_rows] = total
    spot = small_pair.at[1 - core]
    copy(spot, spot, small_sem, (0,), (0, 1)).wait_recv()
    smalls = small_pair[0] + small_pair[1]
    for k in range(vocab_pad // LANES):
        emb_sums[place(0), emb_rows + k : emb_rows + k + 1] = smalls[
            :, k * LANES : (k + 1) * LANES
        ]
    spot = emb_sums.at[place(0)]
    emb2 = [copy(spot, spot, emb2_sem, (j,), (flips, 0)) for j, flips in enumerate(OTHERS)]
    for each in emb2:
        each.start()
    pass_z(3)
    weight_grad(3, 0)
    weight_grad(3, 1)
    pass_z(4)
    pass_z(8)
    send_eighth(6, 10)

    giw_z.wait_recv()
    gate_at = x_at * 2 + z_high
    giw_full[z_low, gate_at] = (
        giw_acc[:, pl.ds(pl.multiple_of(gate_at * units, units), units)] + giw_z_in[...].astype(f32)
    ).astype(bf16)
    spot = giw_full.at[z_low, gate_at]
    giw_back_z = copy(spot, spot, giw_sem, (2,), (4, 0))
    giw_back_z.start()
    pass_z(5)
    pass_z(9)
    send_eighth(7, 11, 12, 13)
    for j, flips in enumerate(OTHERS):
        spot = emb_sums.at[place(flips)]
        copy(spot, spot, emb2_sem, (j,), (flips, 0)).wait_recv()
    sums = (emb_sums[0] + emb_sums[1]) + (emb_sums[2] + emb_sums[3])
    emb_full[own] = sums[:emb_rows]
    spot = emb_full.at[own]
    emb3 = [copy(spot, spot, emb3_sem, (j,), flips) for j, flips in enumerate(GROUP)]
    for each in emb3:
        each.start()
    for k in range(vocab_pad // LANES):
        lanes = slice(k * LANES, min(vocab, (k + 1) * LANES))
        decb_final[:, lanes] = sums[emb_rows + k : emb_rows + k + 1, : lanes.stop - lanes.start]
    k = vocab_pad // LANES - 1
    loss_final[...] = sums[emb_rows + k : emb_rows + k + 1, LANES - 1 :]
    spot = giw_full.at[z_low, x_at * 2 + 1 - z_high]
    copy(spot, spot, giw_sem, (2,), (4, 0)).wait_recv()
    spot = giw_full.at[z_low, pl.ds(x_at * 2, 2)]
    giw_back_x = copy(spot, spot, giw_sem, (3,), (1, 0))
    giw_back_x.start()
    send_eighth(14, 15)
    pass_z(6)
    pass_z(10)
    dsum_z(1).wait_recv()
    total = dec_part[z_high, x_at] + dec_x_in[z_high].astype(f32) + dec_z_in[...].astype(f32)
    dec_final[...] = total[:, :vocab]
    spot = giw_full.at[z_low, pl.ds((1 - x_at) * 2, 2)]
    copy(spot, spot, giw_sem, (3,), (1, 0)).wait_recv()
    spot = giw_full.at[z_low]
    giw_side = copy(spot, spot, giw_sem, (4,), (2, 0))
    giw_side.start()
    pass_z(7)
    pass_z(11)
    ids_copy.wait_send()
    dec_z.wait_send()
    for each in dec_x + dec_sends + dec_relays + iw_copies + [small_copy(), dsum_x(), dsum_z(1)]:
        each.wait_send()
    for p in range(PIECES + 1):
        for k in range(3):
            weight_z(k, p).wait_send()

    def sent(t, _):
        for s in range(SPLIT):
            for j in range(3):
                hidden_copy(t, s, j).wait_send()
            hidden_core(t, s).wait_send()
            lg_copy(t, s).wait_send()
            pg_copy(t, s).wait_send()
        return 0

    lax.fori_loop(0, steps, sent, 0)

    def sent_back(t, _):
        for s in range(SPLIT):
            pgm_copy(t, s).wait_send()
            for j in range(3):
                chip_copy(t, s, j).wait_send()
        return 0

    lax.fori_loop(1, steps, sent_back, 0)
    for j, flips in enumerate(GROUP):
        spot = emb_full.at[slot(flips)]
        copy(spot, spot, emb3_sem, (j,), flips).wait_recv()
    emb_final[...] = emb_full[...].reshape(vocab_rows, LANES)[:vocab, :width]
    stores = [
        pltpu.make_async_copy(src, dst, out_sem.at[2 * SUB + k])
        for k, (src, dst) in enumerate(
            (
                (iw_final, out_iw),
                (gb_final, out_gb),
                (loss_final, out_loss),
                (decb_final, out_decb),
                (dec_final, out_dec),
                (emb_final, out_emb),
            )
        )
    ]
    for each in stores[2:]:
        each.start()
    spot = giw_full.at[1 - z_low]
    copy(spot, spot, giw_sem, (4,), (2, 0)).wait_recv()
    for side in range(2):
        for gate in range(4):
            value = giw_full[side, gate].astype(f32)
            for run in range(runs):
                to = slice((run * 2 + side) * LANES, (run * 2 + side + 1) * LANES)
                lanes = slice(run * LANES, (run + 1) * LANES)
                iw_final[:, gate, to] = value[:width, lanes]
                gb_final[gate : gate + 1, to] = value[width : width + 1, lanes]
    for each in stores[:2]:
        each.start()
    for at in range(12, 16):
        pass_z(at)

    def scatter(here, side, gate, value):
        for run in range(runs):
            at = pl.multiple_of((run * 2 + side) * LANES, LANES)
            rec_final[here, gate, pl.ds(at, LANES)] = value[:, run * LANES : (run + 1) * LANES]

    rec_stores = []
    for side in range(2):
        for sub in range(SUB):
            z_copy(0, side, sub).wait_recv()
            z_copy(1, side, sub).wait_recv()
            z_copy(2, side, sub).wait_recv()
            here = pl.ds(side * LANES + sub * piece_rows, piece_rows)
            mine = pl.ds(sub * piece_rows, piece_rows)
            for gate in range(4):
                lanes = slice(gate * units, (gate + 1) * units)
                scatter(
                    here,
                    z_low,
                    gate,
                    acc[3, side, mine, lanes] + z_in[0, side, mine, lanes].astype(f32),
                )
                scatter(
                    here,
                    1 - z_low,
                    gate,
                    z_in[1, side, mine, lanes].astype(f32) + z_in[2, side, mine, lanes].astype(f32),
                )
            rec_stores.append(
                pltpu.make_async_copy(
                    rec_final.at[here], out_rec.at[here], out_sem.at[side * SUB + sub]
                )
            )
            rec_stores[-1].start()

    for each in rec_stores + stores:
        each.wait()
    for each in [giw_x, giw_z, giw_back_z, giw_back_x, giw_side]:
        each.wait_send()
    for each in emb_copies + emb2 + emb3:
        each.wait_send()
    for at, spot in enumerate(order):
        x_copy(*spot).wait_send()
        if spot[0] < 3 and at not in range(3 * SUB):
            z_copy(*spot).wait_send()


def hand_over(*refs):
    for src, dst in zip(refs[:7], refs[7:]):
        dst[...] = src[...].reshape(dst.shape)


def grouped(
    char_ids,
    next_chars,
    resets,
    embedding,
    input_weight,
    recurrent_weight,
    gate_bias,
    decoder_weight,
    decoder_bias,
):
    data_count = lax.axis_size("dp")
    row_count, steps = char_ids.shape
    vocab, width = embedding.shape
    local_units = input_weight.shape[2]
    block = recurrent_weight.shape[0]
    units = local_units // 2
    cols = 4 * units
    rows = 2 * row_count
    dec_rows = decoder_weight.shape[2]
    vocab_pad = pl.cdiv(vocab, LANES) * LANES
    tokens_all = row_count * steps * data_count
    half = rows // 2
    part = half // SPLIT
    emb_rows = pl.cdiv(vocab, 64) * 8
    giw_rows = pl.cdiv(width + 1, 16) * 16

    vocab_rows = 8 * emb_rows
    by_gate = recurrent_weight.transpose(1, 0, 2)
    in_by_gate = input_weight.transpose(1, 0, 2)
    dec = decoder_weight.reshape(dec_rows, vocab)

    vmem = pl.BlockSpec(memory_space=pltpu.VMEM)
    anywhere = pl.BlockSpec(memory_space=pl.ANY)
    dims = (steps, rows, units, vocab, vocab_pad, tokens_all, block)

    def sems(*shape):
        return pltpu.SemaphoreType.DMA((2,) + shape)

    loss, emb_grad, in_grad, rec_grad, bias_grad, dec_grad, dec_bias_grad = pl.pallas_call(
        functools.partial(layer_kernel, dims),
        out_shape=[
            jax.ShapeDtypeStruct((1, 1), f32),
            jax.ShapeDtypeStruct((vocab, width), f32),
            jax.ShapeDtypeStruct((width, 4, local_units), f32),
            jax.ShapeDtypeStruct((block, 4, local_units), f32),
            jax.ShapeDtypeStruct((4, local_units), f32),
            jax.ShapeDtypeStruct((dec_rows, vocab), f32),
            jax.ShapeDtypeStruct((1, vocab), f32),
        ],
        in_specs=[vmem] * 4 + [anywhere] * 2 + [vmem] * 3,
        out_specs=[anywhere] * 7,
        scratch_shapes=[
            pltpu.VMEM((block, 4, local_units), bf16),
            pltpu.VMEM((width, 4, local_units), bf16),
            pltpu.VMEM((block, 4, local_units), f32),
            pltpu.VMEM((width, 4, local_units), f32),
            pltpu.VMEM((4, local_units), f32),
            pltpu.VMEM((1, 1), f32),
            pltpu.VMEM((1, vocab), f32),
            pltpu.VMEM((dec_rows, vocab), f32),
            pltpu.VMEM((vocab, width), f32),
            pltpu.VMEM((2, LANES, row_count), jnp.int32),
            pltpu.VMEM((row_count, LANES), jnp.int32),
            pltpu.VMEM((2, 4, block, units), bf16),
            pltpu.VMEM((2, 8, 4, units, units), bf16),
            pltpu.VMEM((vocab_rows, LANES), bf16),
            pltpu.VMEM((2, LANES, cols), bf16),
            pltpu.VMEM((2, 1, cols), f32),
            pltpu.VMEM((dec_rows, vocab_pad), bf16),
            pltpu.VMEM((1, vocab_pad), f32),
            pltpu.VMEM((8, units, vocab_pad), bf16),
            pltpu.VMEM((8, steps, rows, units), bf16),
            pltpu.VMEM((steps, 2, half, cols), f32),
            pltpu.VMEM((steps, 2, half, units), f32),
            pltpu.VMEM((steps, vocab_rows, rows), bf16),
            pltpu.VMEM((steps, rows, LANES), bf16),
            pltpu.VMEM((steps, half, LANES), f32),
            pltpu.VMEM((steps, half, LANES), jnp.int32),
            pltpu.VMEM((steps, rows, vocab_pad), bf16),
            pltpu.VMEM((steps, rows, cols), bf16),
            pltpu.VMEM((steps - 1, rows, cols), bf16),
            pltpu.VMEM((2, half, units), f32),
            pltpu.VMEM((2, half, cols), bf16),
            pltpu.VMEM((steps, half, cols), bf16),
            pltpu.VMEM((steps - 1, half, cols), bf16),
            pltpu.VMEM((2, half, cols), bf16),
            pltpu.VMEM((SPLIT, part, 2 * units), f32),
            pltpu.VMEM((steps - 1, SPLIT, 3, part, 2 * units), bf16),
            pltpu.VMEM((steps - 1, SPLIT, 3, part, 2 * units), bf16),
            pltpu.VMEM((1, vocab_pad), f32),
            pltpu.VMEM((2, 1, vocab_pad), f32),
            pltpu.VMEM((2, LANES, cols), f32),
            pltpu.VMEM((4, 2, LANES, cols), f32),
            pltpu.VMEM((4, 2, LANES, cols), bf16),
            pltpu.VMEM((4, 2, LANES, cols), bf16),
            pltpu.VMEM((3, 2, LANES, cols), bf16),
            pltpu.VMEM((3, 2, LANES, cols), bf16),
            pltpu.VMEM((giw_rows, cols), f32),
            pltpu.VMEM((2, giw_rows, units), bf16),
            pltpu.VMEM((2, giw_rows, units), bf16),
            pltpu.VMEM((giw_rows, units), bf16),
            pltpu.VMEM((giw_rows, units), bf16),
            pltpu.VMEM((2, 4, giw_rows, units), bf16),
            pltpu.VMEM((8, emb_rows, LANES), f32),
            pltpu.VMEM((8, emb_rows, LANES), f32),
            pltpu.VMEM((4, emb_rows + 8, LANES), f32),
            pltpu.VMEM((8, emb_rows, LANES), f32),
            pltpu.VMEM((2, 2, dec_rows, vocab_pad), f32),
            pltpu.VMEM((2, dec_rows, vocab_pad), bf16),
            pltpu.VMEM((2, dec_rows, vocab_pad), bf16),
            pltpu.VMEM((dec_rows, vocab_pad), bf16),
            pltpu.VMEM((dec_rows, vocab_pad), bf16),
            pltpu.SemaphoreType.DMA((PIECES + 2,)),
            pltpu.SemaphoreType.DMA((2 * SUB + 6,)),
            sems(1),
            sems(3, PIECES + 1),
            sems(4, PIECES + 1),
            sems(8, PIECES + 1),
            sems(2),
            sems(3),
            sems(7),
            sems(steps, SPLIT, 3),
            sems(steps, SPLIT),
            sems(steps, SPLIT),
            sems(steps, SPLIT),
            sems(steps - 1, SPLIT),
            sems(1),
            sems(steps - 1, SPLIT, 3),
            sems(4, 2, SUB),
            sems(3, 2, SUB),
            sems(5),
            sems(7),
            sems(3),
            sems(7),
            sems(2),
        ],
        compiler_params=pltpu.CompilerParams(
            collective_id=0, has_side_effects=True, vmem_limit_bytes=62 << 20
        ),
    )(
        char_ids.T,
        next_chars.T,
        resets.T,
        embedding,
        input_weight,
        recurrent_weight,
        gate_bias,
        dec,
        decoder_bias,
    )
    results = [loss, emb_grad, in_grad, rec_grad, bias_grad, dec_grad, dec_bias_grad]
    parts = 2
    blocks = [
        pl.BlockSpec((each.shape[0] // parts,) + each.shape[1:], lambda i: (i, 0, 0))
        if each.ndim == 3
        else pl.BlockSpec(each.shape, lambda i: (0, 0))
        for each in results
    ]
    loss, emb_grad, in_grad, rec_grad, bias_grad, dec_grad, dec_bias_grad = pl.pallas_call(
        hand_over,
        out_shape=[jax.ShapeDtypeStruct(each.shape, f32) for each in results[:-1]]
        + [jax.ShapeDtypeStruct((vocab,), f32)],
        grid=(parts,),
        in_specs=blocks,
        out_specs=blocks[:-1] + [pl.BlockSpec((vocab,), lambda i: (0,))],
    )(*results)
    return (
        loss.reshape(()),
        emb_grad,
        in_grad,
        rec_grad,
        bias_grad,
        dec_grad.reshape(decoder_weight.shape),
        dec_bias_grad,
    )


def on_device(
    char_ids,
    next_chars,
    resets,
    embedding,
    input_weight,
    recurrent_weight,
    gate_bias,
    decoder_weight,
    decoder_bias,
):
    highest = lax.Precision.HIGHEST
    data_count = lax.axis_size("dp")
    row_count, step_count = char_ids.shape
    vocab_size, width_in = embedding.shape
    local_units = input_weight.shape[2]
    gate_cols = 4 * local_units
    tokens_here = row_count * step_count
    tokens_all = tokens_here * data_count
    gathered_rec, gathered_dec = (
        lax.all_gather(recurrent_weight, "dp", axis=0, tiled=True),
        lax.all_gather(decoder_weight, "dp", axis=1, tiled=True),
    )
    hidden_total = gathered_rec.shape[0]
    rec_matrix = gathered_rec.reshape(hidden_total, gate_cols)
    dec_matrix = gathered_dec.reshape(local_units, vocab_size)
    time_ids = char_ids.T
    keep_mask = (1 - resets.T).astype(f32)
    proj_table = jnp.dot(
        embedding, input_weight.reshape(width_in, gate_cols), preferred_element_type=f32
    )
    projected = jnp.take(proj_table, time_ids, axis=0) + gate_bias.reshape(gate_cols)

    def forward_step(state_pair, inputs):
        hidden_loc, cell_state = state_pair
        proj_now, keep_now = inputs
        hidden_full = lax.all_gather(hidden_loc, "mp", axis=1, tiled=True)
        previous = hidden_full * keep_now[:, None].astype(bf16)
        preact = proj_now + jnp.dot(previous, rec_matrix, preferred_element_type=f32)
        gate_vals = preact.reshape(row_count, 4, local_units)
        in_gate = jax.nn.sigmoid(gate_vals[:, 0])
        forget_gate = jax.nn.sigmoid(gate_vals[:, 1])
        cell_gate = jnp.tanh(gate_vals[:, 2])
        out_gate = jax.nn.sigmoid(gate_vals[:, 3])
        new_cell = forget_gate * cell_state * keep_now[:, None] + in_gate * cell_gate
        new_hidden = (out_gate * jnp.tanh(new_cell)).astype(bf16)
        return ((new_hidden, new_cell), (previous, preact, new_cell, new_hidden))

    first_state = (
        jnp.zeros((row_count, local_units), bf16),
        jnp.zeros((row_count, local_units), f32),
    )
    _, (prevs, preacts, cells, hiddens) = lax.scan(
        forward_step, first_state, (projected, keep_mask)
    )
    flat_hidden = hiddens.reshape(tokens_here, local_units)
    partial_value = jnp.dot(flat_hidden, dec_matrix, preferred_element_type=f32)
    flat_targets = next_chars.T.reshape(tokens_here)
    logit_rows = lax.psum(partial_value, "mp")
    shifted_in = logit_rows + decoder_bias
    row_max = jnp.max(shifted_in, axis=1)
    exp_total = jnp.sum(jnp.exp(shifted_in - row_max[:, None]), axis=1)
    log_total = row_max + jnp.log(exp_total)
    softmax_out = jnp.exp(shifted_in - log_total[:, None])
    onehot = (flat_targets[:, None] == jnp.arange(vocab_size, dtype=jnp.int32)[None, :]).astype(f32)
    picked = jnp.sum(shifted_in * onehot, axis=1)
    grad_rows = ((softmax_out - onehot) / tokens_all).astype(bf16)
    local_loss = jnp.sum(log_total - picked) / tokens_all
    loss_part = jnp.where(lax.axis_index("mp") == 0, local_loss, jnp.zeros((), f32))
    out_grads = jnp.dot(grad_rows, dec_matrix.T, preferred_element_type=f32).reshape(
        step_count, row_count, local_units
    )
    dec_bias_part = jnp.sum(grad_rows.astype(f32), axis=0)
    columns = flat_hidden
    dec_grad = lax.psum_scatter(
        lax.dot_general(columns, grad_rows, (((0,), (0,)), ((), ())), preferred_element_type=f32),
        "dp",
        scatter_dimension=0,
        tiled=True,
    ).reshape(decoder_weight.shape)
    prev_cells = (
        jnp.concatenate([jnp.zeros((1, row_count, local_units), f32), cells[:-1]], axis=0)
        * keep_mask[:, :, None]
    )

    def backward_step(state_pair, inputs):
        carry_hidden, carry_cell = state_pair
        preact, cell_state, prev_cell, hidden_out, keep_now = inputs
        gate_vals = preact.reshape(row_count, 4, local_units)
        in_gate = jax.nn.sigmoid(gate_vals[:, 0])
        forget_gate = jax.nn.sigmoid(gate_vals[:, 1])
        cell_gate = jnp.tanh(gate_vals[:, 2])
        out_gate = jax.nn.sigmoid(gate_vals[:, 3])
        hidden_grad = hidden_out + carry_hidden
        squash = jnp.tanh(cell_state)
        cell_grad = hidden_grad * out_gate * (1.0 - squash * squash) + carry_cell
        grad_in = cell_grad * cell_gate * in_gate * (1.0 - in_gate)
        grad_forget = cell_grad * prev_cell * forget_gate * (1.0 - forget_gate)
        grad_cand = cell_grad * in_gate * (1.0 - cell_gate * cell_gate)
        grad_out = hidden_grad * squash * out_gate * (1.0 - out_gate)
        preact_grad = (
            jnp.stack([grad_in, grad_forget, grad_cand, grad_out], axis=1)
            .reshape(row_count, gate_cols)
            .astype(bf16)
        )
        back_term = lax.dot_general(
            preact_grad, rec_matrix, (((1,), (1,)), ((), ())), preferred_element_type=f32
        )
        next_hidden = (
            lax.psum_scatter(back_term, "mp", scatter_dimension=1, tiled=True) * keep_now[:, None]
        )
        next_cell = cell_grad * forget_gate * keep_now[:, None]
        return ((next_hidden, next_cell), preact_grad)

    zero_rows = jnp.zeros((row_count, local_units), f32)
    _, preact_grads = lax.scan(
        backward_step,
        (zero_rows, zero_rows),
        (preacts, cells, prev_cells, out_grads, keep_mask),
        reverse=True,
    )
    flat_prev = prevs.reshape(tokens_here, hidden_total)
    flat_pgrad = preact_grads.reshape(tokens_here, gate_cols)
    columns = flat_prev
    rec_grad = lax.psum_scatter(
        lax.dot_general(columns, flat_pgrad, (((0,), (0,)), ((), ())), preferred_element_type=f32),
        "dp",
        scatter_dimension=0,
        tiled=True,
    ).reshape(recurrent_weight.shape)
    onehot_ids = (
        time_ids.reshape(tokens_here)[:, None] == jnp.arange(vocab_size, dtype=jnp.int32)[None, :]
    ).astype(bf16)
    table_part = lax.dot_general(
        onehot_ids, flat_pgrad, (((0,), (0,)), ((), ())), preferred_element_type=f32
    )
    table_sum, dec_bias_grad, loss_data = lax.psum((table_part, dec_bias_part, loss_part), "dp")
    in_grad = jnp.dot(embedding.astype(f32).T, table_sum, precision=highest).reshape(
        width_in, 4, local_units
    )
    bias_grad = jnp.sum(table_sum, axis=0).reshape(4, local_units)
    emb_part = lax.dot_general(
        table_sum,
        input_weight.reshape(width_in, gate_cols).astype(f32),
        (((1,), (1,)), ((), ())),
        precision=highest,
    )
    emb_grad, loss = lax.psum((emb_part, loss_data), "mp")
    return (loss, emb_grad, in_grad, rec_grad, bias_grad, dec_grad, dec_bias_grad)


def solution(mesh):
    in_specs = (
        P("dp", None),
        P("dp", None),
        P("dp", None),
        P(),
        P(None, None, "mp"),
        P("dp", None, "mp"),
        P(None, "mp"),
        P("mp", "dp", None, None),
        P(),
    )
    out_specs = (
        P(),
        P(),
        P(None, None, "mp"),
        P("dp", None, "mp"),
        P(None, "mp"),
        P("mp", "dp", None, None),
        P(),
    )
    fits = (mesh.shape["dp"], mesh.shape["mp"]) == (8, 4)
    return jax.shard_map(
        grouped if fits else on_device,
        mesh=mesh,
        in_specs=in_specs,
        out_specs=out_specs,
        check_vma=False,
    )
```

```python
import functools

import jax
import jax.numpy as jnp
from jax import lax
from jax.experimental import pallas as pl
from jax.experimental.pallas import tpu as pltpu
from jax.sharding import PartitionSpec as P

f32 = jnp.float32
bf16 = jnp.bfloat16
MESH = pl.DeviceIdType.MESH
LANES = 128
CHIPS = ((2, 0), (0, 2), (2, 2))
PEERS = ((0, 1), (2, 0), (0, 2), (2, 2), (2, 1), (0, 3), (2, 3), (1, 0), (4, 0), (5, 0), (6, 0))
GROUP = ((0, 1), (2, 0), (0, 2), (2, 2), (2, 1), (0, 3), (2, 3))
OTHERS = (1, 4, 5)
COLUMN = (4, 6, 2)
SPLIT = 2
PIECES = 8
LAG = 2
EARLY = 3
SUB = 4


def turn(value, flips):
    for bit in (1, 2, 4):
        if flips & bit:
            value = value + bit - 2 * bit * lax.rem(lax.div(value, bit), 2)
    return value


def dot(a, b):
    return jnp.dot(a, b, preferred_element_type=f32)


def dot_t(a, b):
    return lax.dot_general(a, b, (((1,), (1,)), ((), ())), preferred_element_type=f32)


def t_dot(a, b):
    return lax.dot_general(a, b, (((0,), (0,)), ((), ())), preferred_element_type=f32)


def layer_kernel(
    dims,
    chars_ref,
    nexts_ref,
    resets_ref,
    emb_ref,
    iw_ref,
    rec_ref,
    gb_ref,
    dec_ref,
    decb_ref,
    out_loss,
    out_emb,
    out_iw,
    out_rec,
    out_gb,
    out_dec,
    out_decb,
    rec_in,
    iw_in,
    rec_final,
    iw_final,
    gb_final,
    loss_final,
    decb_final,
    dec_final,
    emb_final,
    ids_rows,
    ids_cols,
    rec_halves,
    weights,
    emb_pad,
    iw_pads,
    gb_pads,
    dec_pad,
    decb_pad,
    dec_all,
    hid,
    gates,
    cells,
    squashes,
    from_logits,
    onehots,
    embedded,
    keeps,
    targets,
    logit_grads,
    pgs,
    pgm,
    carry_c,
    pg_now,
    pg_out,
    pgm_out,
    pgm_now,
    own_sum,
    chip_out,
    chip_in,
    small_acc,
    small_pair,
    both,
    x_out,
    x_in,
    z_out,
    z_in,
    giw_acc,
    giw_out,
    giw_x_in,
    giw_z_out,
    giw_z_in,
    giw_full,
    emb_part,
    emb_in,
    emb_sums,
    emb_full,
    dec_part,
    dec_x_out,
    dec_x_in,
    dec_z_out,
    dec_z_in,
    in_sem,
    out_sem,
    ids_sem,
    wz_sem,
    wx_sem,
    wc_sem,
    iw_sem,
    decg_sem,
    decr_sem,
    hid_sem,
    hidc_sem,
    lg_sem,
    pg_sem,
    pgm_sem,
    small_sem,
    chip_sem,
    gx_sem,
    gz_sem,
    giw_sem,
    emb_sem,
    emb2_sem,
    emb3_sem,
    dsum_sem,
):
    steps, rows, units, vocab, vocab_pad, tokens_all, block = dims
    cols = 4 * units
    half = rows // 2
    part = half // SPLIT
    d, m = lax.axis_index("dp"), lax.axis_index("mp")
    x_at, z_low, z_high = lax.rem(d, 2), lax.rem(lax.div(d, 2), 2), lax.div(d, 4)
    z_at = lax.div(d, 2)
    core, y_at = lax.rem(m, 2), lax.div(m, 2)

    def device(flips):
        return (turn(d, flips[0]), turn(m, flips[1]))

    def slot(flips):
        return turn(z_low, flips[0] // 2) * 4 + turn(m, flips[1])

    def chip(flips):
        return pl.ds(turn(z_low, flips[0] // 2) * 4 + turn(y_at, flips[1] // 2) * 2, 2)

    own = slot((0, 0))

    def copy(src, dst, sems, at, flips):
        return pltpu.make_async_remote_copy(
            src_ref=src,
            dst_ref=dst,
            send_sem=sems.at[(0,) + at],
            recv_sem=sems.at[(1,) + at],
            device_id=device(flips),
            device_id_type=MESH,
        )

    sizes = [block // PIECES] * (PIECES - 1) + [block // PIECES // 2] * 2
    pieces = [(sum(sizes[:p]), size) for p, size in enumerate(sizes)]
    rec_loads = [
        pltpu.make_async_copy(
            rec_ref.at[pl.ds(first, size)], rec_in.at[pl.ds(first, size)], in_sem.at[p]
        )
        for p, (first, size) in enumerate(pieces)
    ]
    iw_load = pltpu.make_async_copy(iw_ref, iw_in, in_sem.at[PIECES + 1])
    for each in rec_loads + [iw_load]:
        each.start()

    barrier = pltpu.get_barrier_semaphore()
    for flips in PEERS:
        pl.semaphore_signal(barrier, inc=1, device_id=device(flips), device_id_type=MESH)
    pl.semaphore_wait(barrier, len(PEERS))


    def weight_rows(index, p):
        first, size = pieces[p]
        side, inside = first // LANES, first % LANES
        return weights.at[
            core,
            side * 4 + lax.div(index, 2),
            :,
            pl.ds(pl.multiple_of(lax.rem(index, 2) * LANES + inside, size), size),
        ]

    def weight_core(index, at, p):
        spot = weight_rows(index, p)
        return copy(spot, spot, wc_sem, (at, p), (0, 1))

    def block_of(at):
        return turn(d, (0, 4, 6, 2)[at % 4] + at // 4)

    def weight_z(k, p):
        flips = COLUMN[k]
        half = turn(z_low, (flips & 2) // 2)
        return copy(
            rec_halves.at[half, :, pl.ds(*pieces[p])], weight_rows(d, p), wz_sem, (k, p), (flips, 0)
        )

    def weight_z_in(k, p):
        spot = weight_rows(turn(d, COLUMN[k]), p)
        return copy(spot, spot, wz_sem, (k, p), (COLUMN[k], 0))

    def weight_x(k, p):
        if k == 3:
            return copy(
                rec_halves.at[z_low, :, pl.ds(*pieces[p])],
                weight_rows(d, p),
                wx_sem,
                (k, p),
                (1, 0),
            )
        spot = weight_rows(turn(d, COLUMN[k]), p)
        return copy(spot, spot, wx_sem, (k, p), (1, 0))

    def weight_x_in(k, p):
        flips = 0 if k == 3 else COLUMN[k]
        spot = weight_rows(turn(d, flips + 1), p)
        return copy(spot, spot, wx_sem, (k, p), (1, 0))

    runs = units // LANES
    width = iw_ref.shape[0]
    dec_rows = dec_ref.shape[0]
    vocab_rows = emb_pad.shape[0]

    def dec_spot(flips):
        at = turn(z_high, flips // 4) * LANES + turn(x_at, flips % 2) * dec_rows
        return dec_all.at[own, pl.ds(pl.multiple_of(at, dec_rows), dec_rows)]

    ids_rows[z_low, 0:steps] = chars_ref[...]
    ids_rows[z_low, 8 : 8 + steps] = nexts_ref[...]
    ids_rows[z_low, 16 : 16 + steps] = resets_ref[...]
    ids_copy = copy(ids_rows.at[z_low], ids_rows.at[z_low], ids_sem, (0,), (2, 0))
    ids_copy.start()

    def weight_start(p):
        for k in range(3):
            weight_z(k, p).start()
        weight_x(3, p).start()

    for p, (first, size) in enumerate(pieces):
        here = slice(first, first + size)
        rec_loads[p].wait()
        for gate in range(4):
            for run in range(runs):
                for side in range(2):
                    at = (run * 2 + side) * LANES
                    to = run * LANES
                    rec_halves[side, gate, here, to : to + LANES] = rec_in[here, gate, at : at + LANES]
        if p < EARLY:
            weight_start(p)
        if p == 0:
            dec_pad[...] = jnp.zeros_like(dec_pad)
            dec_pad[:, :vocab] = dec_ref[...]
            dec_z = copy(dec_pad, dec_spot(0), decg_sem, (0,), (4, 0))
            dec_z.start()
            dec_x = [copy(dec_pad, dec_spot(0), decg_sem, (1,), (1, 0))]
            dec_x[0].start()

    def weight_round(p):
        for k in range(3):
            weight_z_in(k, p).wait_recv()
            weight_x(k, p).start()
            weight_core(block_of(1 + k), 1 + k, p).start()
        if p >= LAG:
            weight_over_x(p - LAG)

    def weights_from_core(which):
        for p in which:
            for at in range(8):
                index = block_of(at)
                first, size = pieces[p]
                inside = first % LANES
                spot = weights.at[
                    1 - core,
                    first // LANES * 4 + lax.div(index, 2),
                    :,
                    pl.ds(pl.multiple_of(lax.rem(index, 2) * LANES + inside, size), size),
                ]
                copy(spot, spot, wc_sem, (at, p), (0, 1)).wait_recv()

    def weight_over_x(p):
        for k in (3, 0, 1, 2):
            weight_x_in(k, p).wait_recv()
            at = 4 if k == 3 else 5 + k
            weight_core(block_of(at), at, p).start()

    for p in range(PIECES + 1):
        weight_rows(d, p)[...] = rec_halves[z_low, :, pl.ds(*pieces[p])]
        weight_core(block_of(0), 0, p).start()
    dec_spot(0)[...] = dec_pad[...]
    emb_pad[...] = jnp.zeros_like(emb_pad)
    emb_pad[:vocab, :width] = emb_ref[...]
    ones_at = lax.broadcasted_iota(jnp.int32, emb_pad.shape, 1) == width
    emb_pad[...] = jnp.where(ones_at, 1.0, emb_pad[...].astype(f32)).astype(bf16)
    iw_pads[core] = jnp.zeros(iw_pads.shape[1:], bf16)
    iw_load.wait()

    def half_lanes(run):
        return pl.ds(pl.multiple_of((run * 2 + z_low) * LANES, LANES), LANES)

    for gate in range(4):
        for run in range(runs):
            to = gate * units + run * LANES
            iw_pads[core, :width, to : to + LANES] = iw_in[:, gate, half_lanes(run)]
            gb_pads[core, :, to : to + LANES] = gb_ref[gate : gate + 1, half_lanes(run)]
    iw_copies = [
        copy(ref.at[core], ref.at[core], iw_sem, (k,), (0, 1))
        for k, ref in enumerate((iw_pads, gb_pads))
    ]
    for each in iw_copies:
        each.start()
    decb_pad[...] = jnp.full(decb_pad.shape, -1e30, f32)
    decb_pad[0, :vocab] = decb_ref[...]
    ids_copy.wait_recv()
    ids_cols[...] = ids_rows[core].T
    vocab_iota = lax.broadcasted_iota(jnp.int32, (vocab_rows, rows), 0)

    def read_ids(t):
        now = jnp.concatenate([ids_rows[0, t : t + 1], ids_rows[1, t : t + 1]], axis=1)
        onehots[t] = (vocab_iota == now).astype(f32).astype(bf16)
        targets[t] = jnp.broadcast_to(ids_cols[:, 8 + t : 9 + t], (half, LANES))
        keeps[t] = jnp.broadcast_to((1 - ids_cols[:, 16 + t : 17 + t]).astype(f32), (half, LANES))

    def project(t):
        read_ids(t)
        chosen = t_dot(onehots[t], emb_pad[...]).astype(bf16)
        embedded[t] = chosen
        mine = embedded[t, pl.ds(pl.multiple_of(core * half, half), half)]
        for c in range(2):
            gates[t, c] = dot(mine, iw_pads[c]) + gb_pads[c]

    for k, ref in enumerate((iw_pads, gb_pads)):
        copy(ref.at[1 - core], ref.at[1 - core], iw_sem, (k,), (0, 1)).wait_recv()
    project(0)

    def span(s):
        return pl.ds(s * part, part)

    def wide(s):
        return pl.ds(pl.multiple_of(core * half + s * part, part), part)

    def hidden_copy(t, s, j):
        spot = hid.at[chip((0, 0)), t, wide(s)]
        return copy(spot, spot, hid_sem, (t, s, j), CHIPS[j])

    def hidden_in(t, s, j):
        spot = hid.at[chip(CHIPS[j]), t, wide(s)]
        return copy(spot, spot, hid_sem, (t, s, j), CHIPS[j])

    def hidden_core(t, s):
        spot = hid.at[:, t, wide(s)]
        return copy(spot, spot, hidc_sem, (t, s), (0, 1))

    def hidden_core_in(t, s):
        rows_there = pl.ds(pl.multiple_of((1 - core) * half + s * part, part), part)
        spot = hid.at[:, t, rows_there]
        return copy(spot, spot, hidc_sem, (t, s), (0, 1))

    def cell_step(t, s, added):
        here = span(s)
        if added is not None:
            keep = keeps[t, here, :1]
        for c in range(2):
            preact = [gates[t, c, here, k * units : (k + 1) * units] for k in range(4)]
            if added is not None:
                preact = [preact[k] + keep * added[c][k] for k in range(4)]
            in_gate = jax.nn.sigmoid(preact[0])
            forget = jax.nn.sigmoid(preact[1])
            candidate = jnp.tanh(preact[2])
            out_gate = jax.nn.sigmoid(preact[3])
            cell = in_gate * candidate
            if added is not None:
                cell = forget * keep * cells[t - 1, c, here] + cell
            cells[t, c, here] = cell
            squash = jnp.tanh(cell)
            hid[z_low * 4 + y_at * 2 + c, t, wide(s)] = (out_gate * squash).astype(bf16)
            squashes[t, c, here] = squash
            gates[t, c, here, :units] = in_gate
            gates[t, c, here, units : 2 * units] = forget
            gates[t, c, here, 2 * units : 3 * units] = candidate
            gates[t, c, here, 3 * units :] = out_gate
        for j in (2, 0, 1):
            hidden_copy(t, s, j).start()

    def add_slot(total, t, here, at):
        some = hid[at, t, here]
        for c in range(2):
            for gate in range(4):
                more = dot(some, weights[c, at, gate])
                total[c][gate] = more if total[c][gate] is None else total[c][gate] + more

    for s in range(SPLIT):
        cell_step(0, s, None)

    for p in range(EARLY, PIECES + 1):
        weight_start(p)
    weight_round(0)
    project(1)
    project(2)
    weight_round(1)
    spot = dec_spot(4)
    copy(spot, spot, decg_sem, (0,), (4, 0)).wait_recv()
    dec_x.append(copy(spot, spot, decg_sem, (2,), (1, 0)))
    dec_x[1].start()
    project(3)
    weight_round(2)
    project(4)
    project(5)
    weight_round(3)
    for j, flips in enumerate((1, 5)):
        spot = dec_spot(flips)
        copy(spot, spot, decg_sem, (1 + j,), (1, 0)).wait_recv()
    dec_own = dec_all.at[own]
    dec_sends = [
        copy(dec_own, dec_own, decr_sem, (j,), flips) for j, flips in enumerate(CHIPS + ((0, 1),))
    ]
    for each in dec_sends:
        each.start()
    weight_round(4)
    weight_round(5)
    weights_from_core(range(PIECES // 2))
    for s in range(SPLIT):
        for j in range(3):
            hidden_in(0, s, j).wait_recv()
    mine = pl.ds(pl.multiple_of(core * half, half), half)
    total = [[None] * 4, [None] * 4]
    for at in range(4):
        add_slot(total, 0, mine, at)
    for c in range(2):
        for gate in range(4):
            lanes = slice(gate * units, (gate + 1) * units)
            gates[1, c, :, lanes] += keeps[1, :, :1] * total[c][gate]
    for p in range(6, PIECES + 1):
        weight_round(p)
    for p in range(PIECES + 1 - LAG, PIECES + 1):
        weight_over_x(p)
    weights_from_core(range(PIECES // 2, PIECES + 1))

    def dec_relay(j):
        spot = dec_all.at[slot(CHIPS[j])]
        return copy(spot, spot, decr_sem, (4 + j,), (0, 1))

    def pass_decoder():
        for j in range(3):
            spot = dec_all.at[slot(CHIPS[j])]
            copy(spot, spot, decr_sem, (j,), CHIPS[j]).wait_recv()
            dec_relay(j).start()

    def weight_sent():
        for p in range(PIECES + 1):
            for at in range(8):
                weight_core(block_of(at), at, p).wait_send()
            for k in range(4):
                weight_x(k, p).wait_send()

    def add_chip(total, t, s, flips):
        first = turn(z_low, flips[0] // 2) * 4 + turn(y_at, flips[1] // 2) * 2
        for k in range(2):
            add_slot(total, t, wide(s), first + k)

    def gather_hidden(t, s):
        total = [[None] * 4, [None] * 4]
        add_chip(total, t, s, (0, 0))
        for j in range(3):
            hidden_in(t, s, j).wait_recv()
            add_chip(total, t, s, CHIPS[j])
        hidden_core(t, s).start()
        return total

    vocab_part = lax.broadcasted_iota(jnp.int32, (part, vocab_pad), 1)
    last_lane = lax.broadcasted_iota(jnp.int32, (1, vocab_pad), 1) == vocab_pad - 1
    small_acc[...] = jnp.zeros_like(small_acc)

    def lg_copy(t, s):
        spot = logit_grads.at[t, wide(s)]
        return copy(spot, spot, lg_sem, (t, s), (0, 1))

    def decode(t, s):
        here = span(s)
        logits = decb_pad[...]
        for at in range(8):
            logits = logits + dot(hid[at, t, wide(s)], dec_all[at])
        top = jnp.max(logits, axis=1, keepdims=True)
        exps = jnp.exp(logits - top)
        total = jnp.sum(exps, axis=1, keepdims=True)
        hot = targets[t, here, :1] == vocab_part
        picked = jnp.sum(jnp.where(hot, logits, 0.0), axis=1, keepdims=True)
        lost = top + jnp.log(total) - picked
        grad = ((exps / total - jnp.where(hot, 1.0, 0.0)) / tokens_all).astype(bf16)
        logit_grads[t, wide(s)] = grad
        lg_copy(t, s).start()
        for c in range(2):
            from_logits[t, c, here] = dot_t(grad, dec_all[z_low * 4 + y_at * 2 + c])
        small_acc[...] += jnp.sum(grad.astype(f32), axis=0, keepdims=True) + jnp.where(
            last_lane, jnp.sum(lost, axis=0, keepdims=True) / tokens_all, 0.0
        )

    def forward(t, _):
        for s in range(SPLIT):
            cell_step(t, s, gather_hidden(t - 1, s))
            decode(t - 1, s)
        return 0

    @pl.when(core == 1)
    def _():
        pass_decoder()

    total = [[None] * 4, [None] * 4]
    for at in range(4, 8):
        add_slot(total, 0, mine, at)
    for s in range(SPLIT):
        here = slice(s * part, (s + 1) * part)
        cell_step(1, s, [[more[here] for more in total[c]] for c in range(2)])
        hidden_core(0, s).start()

    @pl.when(core == 0)
    def _():
        pass_decoder()

    spot = dec_all.at[slot((0, 1))]
    copy(spot, spot, decr_sem, (3,), (0, 1)).wait_recv()
    for j in range(3):
        spot = dec_all.at[slot((CHIPS[j][0], CHIPS[j][1] + 1))]
        copy(spot, spot, decr_sem, (4 + j,), (0, 1)).wait_recv()
    for s in range(SPLIT):
        decode(0, s)
    lax.fori_loop(2, steps, forward, 0)

    def pg_copy(t, s):
        return copy(pg_out.at[t, span(s)], pgs.at[t, wide(s)], pg_sem, (t, s), (0, 1))

    def pgm_copy(t, s):
        return copy(
            pgm_out.at[t - 1, span(s)], pgm.at[t - 1, wide(s)], pgm_sem, (t - 1, s), (0, 1)
        )

    def cell_back(t, s, carried, first):
        here = span(s)
        if not first:
            keep = keeps[t, here, :1]
        for c in range(2):
            hidden_grad = from_logits[t, c, here]
            if carried is not None:
                hidden_grad = hidden_grad + carried[:, c * units : (c + 1) * units]
            in_gate = gates[t, c, here, :units]
            forget = gates[t, c, here, units : 2 * units]
            candidate = gates[t, c, here, 2 * units : 3 * units]
            out_gate = gates[t, c, here, 3 * units :]
            squash = squashes[t, c, here]
            cell_grad = hidden_grad * out_gate * (1.0 - squash * squash)
            if carried is not None:
                cell_grad = cell_grad + carry_c[c, here]
            grads = [
                cell_grad * candidate * in_gate * (1.0 - in_gate),
                None,
                cell_grad * in_gate * (1.0 - candidate * candidate),
                hidden_grad * squash * out_gate * (1.0 - out_gate),
            ]
            if first:
                grads[1] = jnp.zeros_like(cell_grad)
            else:
                grads[1] = cell_grad * (keep * cells[t - 1, c, here]) * forget * (1.0 - forget)
                carry_c[c, here] = keep * forget * cell_grad
            for k in range(4):
                pg_now[c, here, k * units : (k + 1) * units] = grads[k].astype(bf16)
                if not first:
                    pgm_now[c, here, k * units : (k + 1) * units] = (keep * grads[k]).astype(bf16)

    def share(t, s, first):
        here = span(s)
        pgs[t, wide(s)] = pg_now[core, here]
        pg_out[t, here] = pg_now[1 - core, here]
        if not first:
            pgm[t - 1, wide(s)] = pgm_now[core, here]
            pgm_out[t - 1, here] = pgm_now[1 - core, here]
            pgm_copy(t, s).start()
        pg_copy(t, s).start()

    def chip_copy(t, s, j):
        return copy(
            chip_out.at[t - 1, s, j], chip_in.at[t - 1, s, j], chip_sem, (t - 1, s, j), CHIPS[j]
        )

    def spread(t, s):
        here = span(s)
        for j in (2, 0, 1, 3):
            flips = CHIPS[j] if j < 3 else (0, 0)
            first = turn(z_low, flips[0] // 2) * 4 + turn(y_at, flips[1] // 2) * 2
            for k in range(2):
                part_sum = None
                for c in range(2):
                    for gate in range(4):
                        grad = pgm_now[c, here, gate * units : (gate + 1) * units]
                        more = dot(grad, weights[c, first + k, gate])
                        part_sum = more if part_sum is None else part_sum + more
                lanes = slice(k * units, (k + 1) * units)
                if j < 3:
                    chip_out[t - 1, s, j, :, lanes] = part_sum.astype(bf16)
                else:
                    own_sum[s, :, lanes] = part_sum
            if j < 3:
                chip_copy(t, s, j).start()

    def carried_in(t, s):
        total = own_sum[s]
        for j in range(3):
            chip_copy(t + 1, s, j).wait_recv()
            total = total + chip_in[t, s, j].astype(f32)
        return total

    last = steps - 1

    weight_sent()

    def turn_over(at, _):
        for c in range(2):
            for gate in range(4):
                weights[c, at, gate] = weights[c, at, gate].T
        return 0

    lax.fori_loop(0, 8, turn_over, 0)
    for s in range(SPLIT):
        for j in range(3):
            hidden_in(last, s, j).wait_recv()
        hidden_core(last, s).start()
        decode(last, s)
        cell_back(last, s, None, False)
        spread(last, s)
        share(last, s, False)

    def other_rows(s):
        return pl.ds(pl.multiple_of((1 - core) * half + s * part, part), part)

    def dsum_x():
        return copy(dec_x_out, dec_x_in, dsum_sem, (0,), (1, 0))

    def dsum_z(k):
        return copy(dec_z_out, dec_z_in, dsum_sem, (k,), (4, 0))

    def small_copy():
        return copy(small_pair.at[core], small_pair.at[core], small_sem, (0,), (0, 1))

    def decoder_grad():
        for t in range(steps):
            for s in range(SPLIT):
                hidden_core_in(t, s).wait_recv()
                spot = logit_grads.at[t, other_rows(s)]
                copy(spot, spot, lg_sem, (t, s), (0, 1)).wait_recv()
        small_pair[core] = small_acc[...]
        small_copy().start()
        dec_part[...] = t_dot(
            hid[own].reshape(steps * rows, units),
            logit_grads[...].reshape(steps * rows, vocab_pad),
        ).reshape(2, 2, dec_rows, vocab_pad)
        for k in range(2):
            dec_x_out[k] = dec_part[k, 1 - x_at].astype(bf16)
        dsum_x().start()

    def decoder_grad_z():
        dsum_x().wait_recv()
        dec_z_out[...] = (
            dec_part[1 - z_high, x_at] + dec_x_in[1 - z_high].astype(f32)
        ).astype(bf16)
        dsum_z(1).start()

    def backward(i, _):
        t = last - i
        for s in range(SPLIT):
            cell_back(t, s, carried_in(t, s), False)
            spread(t, s)
            share(t, s, False)

        @pl.when(i == 2)
        def _():
            decoder_grad()

        @pl.when(i == 3)
        def _():
            decoder_grad_z()

        return 0

    lax.fori_loop(1, last - 1, backward, 0)
    for s in range(SPLIT):
        cell_back(1, s, carried_in(1, s), False)
        share(1, s, False)

    acc = gates.at[pl.ds(steps - 4, 4)]

    far = (2, 3, 1, 0)

    piece_rows = LANES // SUB

    def x_copy(k, side, sub):
        here = pl.ds(sub * piece_rows, piece_rows)
        return copy(
            x_out.at[k, side, here], x_in.at[k, side, here], gx_sem, (k, side, sub), (1, 0)
        )

    def z_copy(k, side, sub):
        here = pl.ds(sub * piece_rows, piece_rows)
        return copy(
            z_out.at[k, side, here], z_in.at[k, side, here], gz_sem, (k, side, sub), (far[k] * 2, 0)
        )

    used = (steps - 1) * rows

    def from_core(t, _):
        for s in range(SPLIT):
            spot = pgs.at[t, other_rows(s)]
            copy(spot, spot, pg_sem, (t, s), (0, 1)).wait_recv()
            spot = pgm.at[t - 1, other_rows(s)]
            copy(spot, spot, pgm_sem, (t - 1, s), (0, 1)).wait_recv()
        return 0

    lax.fori_loop(1, steps, from_core, 0)

    def weight_grad(k, side):
        at = side * 4 + turn(z_at, far[k])
        both[...] = t_dot(
            hid[at, 0 : steps - 1].reshape(used, units), pgm[...].reshape(used, cols)
        ).reshape(2, LANES, cols)
        x_out[k, side] = both[1 - x_at].astype(bf16)
        acc[k, side] = both[x_at]

    def weight_grad_first(side):
        at = side * 4 + turn(z_at, far[0])
        for k in (1, 0):
            lanes = pl.ds(pl.multiple_of((x_at if k == 0 else 1 - x_at) * LANES, LANES), LANES)
            some = t_dot(
                hid[at, 0 : steps - 1, :, lanes].reshape(used, LANES),
                pgm[...].reshape(used, cols),
            )
            if k:
                x_out[0, side] = some.astype(bf16)
                send_eighth(2 * side, 2 * side + 1)
            else:
                acc[0, side] = some

    order = [(k, side, sub) for k in range(4) for side in range(2) for sub in range(SUB)]

    def send_eighth(*which):
        for at in which:
            for k in range(SUB // 2):
                x_copy(*order[at * (SUB // 2) + k]).start()

    def pass_z(at):
        for k in range(SUB // 2):
            pass_piece(at * (SUB // 2) + k)

    def pass_piece(at):
        k, side, sub = order[at]
        here = pl.ds(sub * piece_rows, piece_rows)
        x_copy(k, side, sub).wait_recv()
        total = acc[k, side, here] + x_in[k, side, here].astype(f32)
        if k == 3:
            acc[k, side, here] = total
            return
        z_out[k, side, here] = total.astype(bf16)
        if at in range(3, 4 * SUB):
            z_copy(*order[at - 3]).wait_send()
        z_copy(k, side, sub).start()

    rec_stores = []

    def scatter(here, side, gate, value):
        for run in range(runs):
            at = pl.multiple_of((run * 2 + side) * LANES, LANES)
            rec_final[here, gate, pl.ds(at, LANES)] = value[:, run * LANES : (run + 1) * LANES]

    def finish(at):
        pass_z(12 + at)
        for which in range(at * (SUB // 2), (at + 1) * (SUB // 2)):
            side, sub = divmod(which, SUB)
            for k in range(3):
                z_copy(k, side, sub).wait_recv()
            here = pl.ds(side * LANES + sub * piece_rows, piece_rows)
            mine = pl.ds(sub * piece_rows, piece_rows)
            for gate in range(4):
                lanes = slice(gate * units, (gate + 1) * units)
                value = acc[3, side, mine, lanes] + z_in[0, side, mine, lanes].astype(f32)
                scatter(here, z_low, gate, value)
                value = z_in[1, side, mine, lanes].astype(f32) + z_in[2, side, mine, lanes].astype(
                    f32
                )
                scatter(here, 1 - z_low, gate, value)
            rec_stores.append(
                pltpu.make_async_copy(rec_final.at[here], out_rec.at[here], out_sem.at[which])
            )
            rec_stores[-1].start()

    weight_grad_first(0)
    weight_grad(0, 1)
    send_eighth(2, 3)
    for s in range(SPLIT):
        spread(1, s)
    pass_piece(0)
    pass_piece(1)
    weight_grad(1, 0)
    pass_piece(2)
    weight_grad(2, 0)
    pass_piece(3)

    for s in range(SPLIT):
        cell_back(0, s, carried_in(0, s), True)
        share(0, s, True)
    for s in range(SPLIT):
        spot = pgs.at[0, other_rows(s)]
        copy(spot, spot, pg_sem, (0, s), (0, 1)).wait_recv()
    tokens = steps * rows
    giw_rows = giw_acc.shape[0]
    giw_acc[...] = t_dot(
        embedded[...].reshape(tokens, LANES), pgs[...].reshape(tokens, cols)
    )[:giw_rows]
    for k in range(2):
        at = pl.multiple_of((1 - x_at) * (2 * units) + k * units, units)
        giw_out[k] = giw_acc[:, pl.ds(at, units)].astype(bf16)
    giw_x = copy(giw_out, giw_x_in, giw_sem, (0,), (1, 0))
    giw_x.start()
    send_eighth(4, 8)
    pass_piece(4)

    emb_rows = emb_full.shape[1]
    by_char = jnp.zeros((vocab_rows, 2 * LANES), f32)
    for t in range(steps):
        by_token = dot_t(pgs[t], iw_pads[core])
        high = by_token.astype(bf16)
        low = (by_token - high.astype(f32)).astype(bf16)
        by_char = by_char + dot(onehots[t], jnp.concatenate([high, low], axis=1))
    emb_part[...] = (by_char[:, :LANES] + by_char[:, LANES:]).reshape(8, emb_rows, LANES)
    emb_copies = [
        copy(emb_part.at[slot(flips)], emb_in.at[own], emb_sem, (j,), flips)
        for j, flips in enumerate(GROUP)
    ]
    for each in emb_copies:
        each.start()
    emb_in[own] = emb_part[own]
    pass_piece(5)
    weight_grad(1, 1)

    giw_x.wait_recv()
    for k in range(2):
        at = pl.multiple_of(x_at * (2 * units) + k * units, units)
        giw_acc[:, pl.ds(at, units)] += giw_x_in[k].astype(f32)
    giw_z_out[...] = giw_acc[
        :, pl.ds(pl.multiple_of(x_at * (2 * units) + (1 - z_high) * units, units), units)
    ].astype(bf16)
    giw_z = copy(giw_z_out, giw_z_in, giw_sem, (1,), (4, 0))
    giw_z.start()
    send_eighth(5, 9)
    pass_piece(6)
    for j, flips in enumerate(GROUP):
        spot = emb_in.at[slot(flips)]
        copy(spot, spot, emb_sem, (j,), flips).wait_recv()
    total = emb_in[0]
    for at in range(1, 8):
        total = total + emb_in[at]

    def place(flips):
        return turn(z_high, flips // 4) * 2 + turn(x_at, flips % 2)

    emb_sums[place(0), :emb_rows] = total
    spot = small_pair.at[1 - core]
    copy(spot, spot, small_sem, (0,), (0, 1)).wait_recv()
    smalls = small_pair[0] + small_pair[1]
    for k in range(vocab_pad // LANES):
        emb_sums[place(0), emb_rows + k : emb_rows + k + 1] = smalls[
            :, k * LANES : (k + 1) * LANES
        ]
    spot = emb_sums.at[place(0)]
    emb2 = [copy(spot, spot, emb2_sem, (j,), (flips, 0)) for j, flips in enumerate(OTHERS)]
    for each in emb2:
        each.start()
    weight_grad(2, 1)
    pass_piece(7)
    send_eighth(6, 10)
    weight_grad(3, 0)
    weight_grad(3, 1)

    giw_z.wait_recv()
    gate_at = x_at * 2 + z_high
    giw_full[z_low, gate_at] = (
        giw_acc[:, pl.ds(pl.multiple_of(gate_at * units, units), units)] + giw_z_in[...].astype(f32)
    ).astype(bf16)
    spot = giw_full.at[z_low, gate_at]
    giw_back_z = copy(spot, spot, giw_sem, (2,), (4, 0))
    giw_back_z.start()

    giw_turn = (gate_at, x_at * 2 + 1 - z_high, (1 - x_at) * 2, (1 - x_at) * 2 + 1)

    def giw_side(k, half_at):
        spot = giw_full.at[half_at, giw_turn[k]]
        return copy(spot, spot, giw_sem, (4 + k,), (2, 0))

    giw_side(0, z_low).start()
    pass_piece(8)
    send_eighth(7, 11)
    pass_piece(9)
    pass_z(8)
    for j, flips in enumerate(OTHERS):
        spot = emb_sums.at[place(flips)]
        copy(spot, spot, emb2_sem, (j,), (flips, 0)).wait_recv()
    sums = (emb_sums[0] + emb_sums[1]) + (emb_sums[2] + emb_sums[3])
    emb_full[own] = sums[:emb_rows]
    spot = emb_full.at[own]
    emb3 = [copy(spot, spot, emb3_sem, (j,), flips) for j, flips in enumerate(GROUP)]
    for each in emb3:
        each.start()
    for k in range(vocab_pad // LANES):
        lanes = slice(k * LANES, min(vocab, (k + 1) * LANES))
        decb_final[:, lanes] = sums[emb_rows + k : emb_rows + k + 1, : lanes.stop - lanes.start]
    k = vocab_pad // LANES - 1
    loss_final[...] = sums[emb_rows + k : emb_rows + k + 1, LANES - 1 :]
    spot = giw_full.at[z_low, x_at * 2 + 1 - z_high]
    copy(spot, spot, giw_sem, (2,), (4, 0)).wait_recv()
    giw_side(1, z_low).start()
    spot = giw_full.at[z_low, pl.ds(x_at * 2, 2)]
    giw_back_x = copy(spot, spot, giw_sem, (3,), (1, 0))
    giw_back_x.start()
    send_eighth(12, 13, 14, 15)
    pass_piece(10)
    pass_z(9)
    pass_piece(11)
    spot = giw_full.at[z_low, pl.ds((1 - x_at) * 2, 2)]
    copy(spot, spot, giw_sem, (3,), (1, 0)).wait_recv()
    giw_side(2, z_low).start()
    pass_piece(12)
    pass_z(10)
    dsum_z(1).wait_recv()
    total = dec_part[z_high, x_at] + dec_x_in[z_high].astype(f32) + dec_z_in[...].astype(f32)
    dec_final[...] = total[:, :vocab]
    pass_piece(13)
    pass_z(11)
    for j, flips in enumerate(GROUP):
        spot = emb_full.at[slot(flips)]
        copy(spot, spot, emb3_sem, (j,), flips).wait_recv()
    emb_final[...] = emb_full[...].reshape(vocab_rows, LANES)[:vocab, :width]
    stores = [
        pltpu.make_async_copy(src, dst, out_sem.at[2 * SUB + k])
        for k, (src, dst) in enumerate(
            (
                (iw_final, out_iw),
                (gb_final, out_gb),
                (loss_final, out_loss),
                (decb_final, out_decb),
                (dec_final, out_dec),
                (emb_final, out_emb),
            )
        )
    ]
    for each in stores[2:]:
        each.start()
    finish(0)
    giw_side(3, z_low).start()
    pass_piece(14)
    ids_copy.wait_send()
    dec_z.wait_send()
    for each in dec_x + dec_sends + [dec_relay(j) for j in range(3)] + iw_copies + [small_copy(), dsum_x(), dsum_z(1)]:
        each.wait_send()
    for p in range(PIECES + 1):
        for k in range(3):
            weight_z(k, p).wait_send()

    def sent(t, _):
        for s in range(SPLIT):
            for j in range(3):
                hidden_copy(t, s, j).wait_send()
            hidden_core(t, s).wait_send()
            lg_copy(t, s).wait_send()
            pg_copy(t, s).wait_send()
        return 0

    lax.fori_loop(0, steps, sent, 0)

    def sent_back(t, _):
        for s in range(SPLIT):
            pgm_copy(t, s).wait_send()
            for j in range(3):
                chip_copy(t, s, j).wait_send()
        return 0

    lax.fori_loop(1, steps, sent_back, 0)
    finish(1)
    pass_piece(15)
    finish(2)
    finish(3)
    for k in range(4):
        giw_side(k, 1 - z_low).wait_recv()
    for side in range(2):
        for gate in range(4):
            value = giw_full[side, gate].astype(f32)
            for run in range(runs):
                to = slice((run * 2 + side) * LANES, (run * 2 + side + 1) * LANES)
                lanes = slice(run * LANES, (run + 1) * LANES)
                iw_final[:, gate, to] = value[:width, lanes]
                gb_final[gate : gate + 1, to] = value[width : width + 1, lanes]
    for each in stores[:2]:
        each.start()

    for each in rec_stores + stores:
        each.wait()
    for each in [giw_x, giw_z, giw_back_z, giw_back_x]:
        each.wait_send()
    for k in range(4):
        giw_side(k, z_low).wait_send()
    for each in emb_copies + emb2 + emb3:
        each.wait_send()
    for at, spot in enumerate(order):
        x_copy(*spot).wait_send()
        if spot[0] < 3 and at not in range(4 * SUB - 3):
            z_copy(*spot).wait_send()


def hand_over(*refs):
    for src, dst in zip(refs[:7], refs[7:]):
        dst[...] = src[...].reshape(dst.shape)


def grouped(
    char_ids,
    next_chars,
    resets,
    embedding,
    input_weight,
    recurrent_weight,
    gate_bias,
    decoder_weight,
    decoder_bias,
):
    data_count = lax.axis_size("dp")
    row_count, steps = char_ids.shape
    vocab, width = embedding.shape
    local_units = input_weight.shape[2]
    block = recurrent_weight.shape[0]
    units = local_units // 2
    cols = 4 * units
    rows = 2 * row_count
    dec_rows = decoder_weight.shape[2]
    vocab_pad = pl.cdiv(vocab, LANES) * LANES
    tokens_all = row_count * steps * data_count
    half = rows // 2
    part = half // SPLIT
    emb_rows = pl.cdiv(vocab, 64) * 8
    giw_rows = pl.cdiv(width + 1, 16) * 16

    vocab_rows = 8 * emb_rows
    by_gate = recurrent_weight.transpose(1, 0, 2)
    in_by_gate = input_weight.transpose(1, 0, 2)
    dec = decoder_weight.reshape(dec_rows, vocab)

    vmem = pl.BlockSpec(memory_space=pltpu.VMEM)
    anywhere = pl.BlockSpec(memory_space=pl.ANY)
    dims = (steps, rows, units, vocab, vocab_pad, tokens_all, block)

    def sems(*shape):
        return pltpu.SemaphoreType.DMA((2,) + shape)

    loss, emb_grad, in_grad, rec_grad, bias_grad, dec_grad, dec_bias_grad = pl.pallas_call(
        functools.partial(layer_kernel, dims),
        out_shape=[
            jax.ShapeDtypeStruct((1, 1), f32),
            jax.ShapeDtypeStruct((vocab, width), f32),
            jax.ShapeDtypeStruct((width, 4, local_units), f32),
            jax.ShapeDtypeStruct((block, 4, local_units), f32),
            jax.ShapeDtypeStruct((4, local_units), f32),
            jax.ShapeDtypeStruct((dec_rows, vocab), f32),
            jax.ShapeDtypeStruct((1, vocab), f32),
        ],
        in_specs=[vmem] * 4 + [anywhere] * 2 + [vmem] * 3,
        out_specs=[anywhere] * 7,
        scratch_shapes=[
            pltpu.VMEM((block, 4, local_units), bf16),
            pltpu.VMEM((width, 4, local_units), bf16),
            pltpu.VMEM((block, 4, local_units), f32),
            pltpu.VMEM((width, 4, local_units), f32),
            pltpu.VMEM((4, local_units), f32),
            pltpu.VMEM((1, 1), f32),
            pltpu.VMEM((1, vocab), f32),
            pltpu.VMEM((dec_rows, vocab), f32),
            pltpu.VMEM((vocab, width), f32),
            pltpu.VMEM((2, LANES, row_count), jnp.int32),
            pltpu.VMEM((row_count, LANES), jnp.int32),
            pltpu.VMEM((2, 4, block, units), bf16),
            pltpu.VMEM((2, 8, 4, units, units), bf16),
            pltpu.VMEM((vocab_rows, LANES), bf16),
            pltpu.VMEM((2, LANES, cols), bf16),
            pltpu.VMEM((2, 1, cols), f32),
            pltpu.VMEM((dec_rows, vocab_pad), bf16),
            pltpu.VMEM((1, vocab_pad), f32),
            pltpu.VMEM((8, units, vocab_pad), bf16),
            pltpu.VMEM((8, steps, rows, units), bf16),
            pltpu.VMEM((steps, 2, half, cols), f32),
            pltpu.VMEM((steps, 2, half, units), f32),
            pltpu.VMEM((steps, 2, half, units), f32),
            pltpu.VMEM((steps, 2, half, units), f32),
            pltpu.VMEM((steps, vocab_rows, rows), bf16),
            pltpu.VMEM((steps, rows, LANES), bf16),
            pltpu.VMEM((steps, half, LANES), f32),
            pltpu.VMEM((steps, half, LANES), jnp.int32),
            pltpu.VMEM((steps, rows, vocab_pad), bf16),
            pltpu.VMEM((steps, rows, cols), bf16),
            pltpu.VMEM((steps - 1, rows, cols), bf16),
            pltpu.VMEM((2, half, units), f32),
            pltpu.VMEM((2, half, cols), bf16),
            pltpu.VMEM((steps, half, cols), bf16),
            pltpu.VMEM((steps - 1, half, cols), bf16),
            pltpu.VMEM((2, half, cols), bf16),
            pltpu.VMEM((SPLIT, part, 2 * units), f32),
            pltpu.VMEM((steps - 1, SPLIT, 3, part, 2 * units), bf16),
            pltpu.VMEM((steps - 1, SPLIT, 3, part, 2 * units), bf16),
            pltpu.VMEM((1, vocab_pad), f32),
            pltpu.VMEM((2, 1, vocab_pad), f32),
            pltpu.VMEM((2, LANES, cols), f32),
            pltpu.VMEM((4, 2, LANES, cols), bf16),
            pltpu.VMEM((4, 2, LANES, cols), bf16),
            pltpu.VMEM((3, 2, LANES, cols), bf16),
            pltpu.VMEM((3, 2, LANES, cols), bf16),
            pltpu.VMEM((giw_rows, cols), f32),
            pltpu.VMEM((2, giw_rows, units), bf16),
            pltpu.VMEM((2, giw_rows, units), bf16),
            pltpu.VMEM((giw_rows, units), bf16),
            pltpu.VMEM((giw_rows, units), bf16),
            pltpu.VMEM((2, 4, giw_rows, units), bf16),
            pltpu.VMEM((8, emb_rows, LANES), f32),
            pltpu.VMEM((8, emb_rows, LANES), f32),
            pltpu.VMEM((4, emb_rows + 8, LANES), f32),
            pltpu.VMEM((8, emb_rows, LANES), f32),
            pltpu.VMEM((2, 2, dec_rows, vocab_pad), f32),
            pltpu.VMEM((2, dec_rows, vocab_pad), bf16),
            pltpu.VMEM((2, dec_rows, vocab_pad), bf16),
            pltpu.VMEM((dec_rows, vocab_pad), bf16),
            pltpu.VMEM((dec_rows, vocab_pad), bf16),
            pltpu.SemaphoreType.DMA((PIECES + 2,)),
            pltpu.SemaphoreType.DMA((2 * SUB + 6,)),
            sems(1),
            sems(3, PIECES + 1),
            sems(4, PIECES + 1),
            sems(8, PIECES + 1),
            sems(2),
            sems(3),
            sems(7),
            sems(steps, SPLIT, 3),
            sems(steps, SPLIT),
            sems(steps, SPLIT),
            sems(steps, SPLIT),
            sems(steps - 1, SPLIT),
            sems(1),
            sems(steps - 1, SPLIT, 3),
            sems(4, 2, SUB),
            sems(3, 2, SUB),
            sems(8),
            sems(7),
            sems(3),
            sems(7),
            sems(2),
        ],
        compiler_params=pltpu.CompilerParams(
            collective_id=0, has_side_effects=True, vmem_limit_bytes=62 << 20
        ),
    )(
        char_ids.T,
        next_chars.T,
        resets.T,
        embedding,
        input_weight,
        recurrent_weight,
        gate_bias,
        dec,
        decoder_bias,
    )
    results = [loss, emb_grad, in_grad, rec_grad, bias_grad, dec_grad, dec_bias_grad]
    parts = 2
    blocks = [
        pl.BlockSpec((each.shape[0] // parts,) + each.shape[1:], lambda i: (i, 0, 0))
        if each.ndim == 3
        else pl.BlockSpec(each.shape, lambda i: (0, 0))
        for each in results
    ]
    loss, emb_grad, in_grad, rec_grad, bias_grad, dec_grad, dec_bias_grad = pl.pallas_call(
        hand_over,
        out_shape=[jax.ShapeDtypeStruct(each.shape, f32) for each in results[:-1]]
        + [jax.ShapeDtypeStruct((vocab,), f32)],
        grid=(parts,),
        in_specs=blocks,
        out_specs=blocks[:-1] + [pl.BlockSpec((vocab,), lambda i: (0,))],
    )(*results)
    return (
        loss.reshape(()),
        emb_grad,
        in_grad,
        rec_grad,
        bias_grad,
        dec_grad.reshape(decoder_weight.shape),
        dec_bias_grad,
    )


def on_device(
    char_ids,
    next_chars,
    resets,
    embedding,
    input_weight,
    recurrent_weight,
    gate_bias,
    decoder_weight,
    decoder_bias,
):
    highest = lax.Precision.HIGHEST
    data_count = lax.axis_size("dp")
    row_count, step_count = char_ids.shape
    vocab_size, width_in = embedding.shape
    local_units = input_weight.shape[2]
    gate_cols = 4 * local_units
    tokens_here = row_count * step_count
    tokens_all = tokens_here * data_count
    gathered_rec, gathered_dec = (
        lax.all_gather(recurrent_weight, "dp", axis=0, tiled=True),
        lax.all_gather(decoder_weight, "dp", axis=1, tiled=True),
    )
    hidden_total = gathered_rec.shape[0]
    rec_matrix = gathered_rec.reshape(hidden_total, gate_cols)
    dec_matrix = gathered_dec.reshape(local_units, vocab_size)
    time_ids = char_ids.T
    keep_mask = (1 - resets.T).astype(f32)
    proj_table = jnp.dot(
        embedding, input_weight.reshape(width_in, gate_cols), preferred_element_type=f32
    )
    projected = jnp.take(proj_table, time_ids, axis=0) + gate_bias.reshape(gate_cols)

    def forward_step(state_pair, inputs):
        hidden_loc, cell_state = state_pair
        proj_now, keep_now = inputs
        hidden_full = lax.all_gather(hidden_loc, "mp", axis=1, tiled=True)
        previous = hidden_full * keep_now[:, None].astype(bf16)
        preact = proj_now + jnp.dot(previous, rec_matrix, preferred_element_type=f32)
        gate_vals = preact.reshape(row_count, 4, local_units)
        in_gate = jax.nn.sigmoid(gate_vals[:, 0])
        forget_gate = jax.nn.sigmoid(gate_vals[:, 1])
        cell_gate = jnp.tanh(gate_vals[:, 2])
        out_gate = jax.nn.sigmoid(gate_vals[:, 3])
        new_cell = forget_gate * cell_state * keep_now[:, None] + in_gate * cell_gate
        new_hidden = (out_gate * jnp.tanh(new_cell)).astype(bf16)
        return ((new_hidden, new_cell), (previous, preact, new_cell, new_hidden))

    first_state = (
        jnp.zeros((row_count, local_units), bf16),
        jnp.zeros((row_count, local_units), f32),
    )
    _, (prevs, preacts, cells, hiddens) = lax.scan(
        forward_step, first_state, (projected, keep_mask)
    )
    flat_hidden = hiddens.reshape(tokens_here, local_units)
    partial_value = jnp.dot(flat_hidden, dec_matrix, preferred_element_type=f32)
    flat_targets = next_chars.T.reshape(tokens_here)
    logit_rows = lax.psum(partial_value, "mp")
    shifted_in = logit_rows + decoder_bias
    row_max = jnp.max(shifted_in, axis=1)
    exp_total = jnp.sum(jnp.exp(shifted_in - row_max[:, None]), axis=1)
    log_total = row_max + jnp.log(exp_total)
    softmax_out = jnp.exp(shifted_in - log_total[:, None])
    onehot = (flat_targets[:, None] == jnp.arange(vocab_size, dtype=jnp.int32)[None, :]).astype(f32)
    picked = jnp.sum(shifted_in * onehot, axis=1)
    grad_rows = ((softmax_out - onehot) / tokens_all).astype(bf16)
    local_loss = jnp.sum(log_total - picked) / tokens_all
    loss_part = jnp.where(lax.axis_index("mp") == 0, local_loss, jnp.zeros((), f32))
    out_grads = jnp.dot(grad_rows, dec_matrix.T, preferred_element_type=f32).reshape(
        step_count, row_count, local_units
    )
    dec_bias_part = jnp.sum(grad_rows.astype(f32), axis=0)
    columns = flat_hidden
    dec_grad = lax.psum_scatter(
        lax.dot_general(columns, grad_rows, (((0,), (0,)), ((), ())), preferred_element_type=f32),
        "dp",
        scatter_dimension=0,
        tiled=True,
    ).reshape(decoder_weight.shape)
    prev_cells = (
        jnp.concatenate([jnp.zeros((1, row_count, local_units), f32), cells[:-1]], axis=0)
        * keep_mask[:, :, None]
    )

    def backward_step(state_pair, inputs):
        carry_hidden, carry_cell = state_pair
        preact, cell_state, prev_cell, hidden_out, keep_now = inputs
        gate_vals = preact.reshape(row_count, 4, local_units)
        in_gate = jax.nn.sigmoid(gate_vals[:, 0])
        forget_gate = jax.nn.sigmoid(gate_vals[:, 1])
        cell_gate = jnp.tanh(gate_vals[:, 2])
        out_gate = jax.nn.sigmoid(gate_vals[:, 3])
        hidden_grad = hidden_out + carry_hidden
        squash = jnp.tanh(cell_state)
        cell_grad = hidden_grad * out_gate * (1.0 - squash * squash) + carry_cell
        grad_in = cell_grad * cell_gate * in_gate * (1.0 - in_gate)
        grad_forget = cell_grad * prev_cell * forget_gate * (1.0 - forget_gate)
        grad_cand = cell_grad * in_gate * (1.0 - cell_gate * cell_gate)
        grad_out = hidden_grad * squash * out_gate * (1.0 - out_gate)
        preact_grad = (
            jnp.stack([grad_in, grad_forget, grad_cand, grad_out], axis=1)
            .reshape(row_count, gate_cols)
            .astype(bf16)
        )
        back_term = lax.dot_general(
            preact_grad, rec_matrix, (((1,), (1,)), ((), ())), preferred_element_type=f32
        )
        next_hidden = (
            lax.psum_scatter(back_term, "mp", scatter_dimension=1, tiled=True) * keep_now[:, None]
        )
        next_cell = cell_grad * forget_gate * keep_now[:, None]
        return ((next_hidden, next_cell), preact_grad)

    zero_rows = jnp.zeros((row_count, local_units), f32)
    _, preact_grads = lax.scan(
        backward_step,
        (zero_rows, zero_rows),
        (preacts, cells, prev_cells, out_grads, keep_mask),
        reverse=True,
    )
    flat_prev = prevs.reshape(tokens_here, hidden_total)
    flat_pgrad = preact_grads.reshape(tokens_here, gate_cols)
    columns = flat_prev
    rec_grad = lax.psum_scatter(
        lax.dot_general(columns, flat_pgrad, (((0,), (0,)), ((), ())), preferred_element_type=f32),
        "dp",
        scatter_dimension=0,
        tiled=True,
    ).reshape(recurrent_weight.shape)
    onehot_ids = (
        time_ids.reshape(tokens_here)[:, None] == jnp.arange(vocab_size, dtype=jnp.int32)[None, :]
    ).astype(bf16)
    table_part = lax.dot_general(
        onehot_ids, flat_pgrad, (((0,), (0,)), ((), ())), preferred_element_type=f32
    )
    table_sum, dec_bias_grad, loss_data = lax.psum((table_part, dec_bias_part, loss_part), "dp")
    in_grad = jnp.dot(embedding.astype(f32).T, table_sum, precision=highest).reshape(
        width_in, 4, local_units
    )
    bias_grad = jnp.sum(table_sum, axis=0).reshape(4, local_units)
    emb_part = lax.dot_general(
        table_sum,
        input_weight.reshape(width_in, gate_cols).astype(f32),
        (((1,), (1,)), ((), ())),
        precision=highest,
    )
    emb_grad, loss = lax.psum((emb_part, loss_data), "mp")
    return (loss, emb_grad, in_grad, rec_grad, bias_grad, dec_grad, dec_bias_grad)


def solution(mesh):
    in_specs = (
        P("dp", None),
        P("dp", None),
        P("dp", None),
        P(),
        P(None, None, "mp"),
        P("dp", None, "mp"),
        P(None, "mp"),
        P("mp", "dp", None, None),
        P(),
    )
    out_specs = (
        P(),
        P(),
        P(None, None, "mp"),
        P("dp", None, "mp"),
        P(None, "mp"),
        P("mp", "dp", None, None),
        P(),
    )
    fits = (mesh.shape["dp"], mesh.shape["mp"]) == (8, 4)
    return jax.shard_map(
        grouped if fits else on_device,
        mesh=mesh,
        in_specs=in_specs,
        out_specs=out_specs,
        check_vma=False,
    )
```

```python
import functools

import jax
import jax.numpy as jnp
from jax import lax
from jax.experimental import pallas as pl
from jax.experimental.pallas import tpu as pltpu
from jax.sharding import PartitionSpec as P

f32 = jnp.float32
bf16 = jnp.bfloat16
MESH = pl.DeviceIdType.MESH
LANES = 128
CHIPS = ((2, 0), (0, 2), (2, 2))
PEERS = ((0, 1), (2, 0), (0, 2), (2, 2), (2, 1), (0, 3), (2, 3), (1, 0), (4, 0), (5, 0), (6, 0))
GROUP = ((0, 1), (2, 0), (0, 2), (2, 2), (2, 1), (0, 3), (2, 3))
OTHERS = (1, 4, 5)
COLUMN = (4, 6, 2)
SPLIT = 2
PIECES = 8
LAG = 2
EARLY = 3
SUB = 4


def turn(value, flips):
    for bit in (1, 2, 4):
        if flips & bit:
            value = value + bit - 2 * bit * lax.rem(lax.div(value, bit), 2)
    return value


def dot(a, b):
    return jnp.dot(a, b, preferred_element_type=f32)


def dot_t(a, b):
    return lax.dot_general(a, b, (((1,), (1,)), ((), ())), preferred_element_type=f32)


def t_dot(a, b):
    return lax.dot_general(a, b, (((0,), (0,)), ((), ())), preferred_element_type=f32)


def layer_kernel(
    dims,
    chars_ref,
    nexts_ref,
    resets_ref,
    emb_ref,
    iw_ref,
    rec_ref,
    gb_ref,
    dec_ref,
    decb_ref,
    out_loss,
    out_emb,
    out_iw,
    out_rec,
    out_gb,
    out_dec,
    out_decb,
    rec_in,
    iw_in,
    ids_rows,
    ids_cols,
    rec_halves,
    weights,
    emb_pad,
    iw_pads,
    gb_pads,
    dec_pad,
    decb_pad,
    dec_all,
    hid,
    gates,
    cells,
    squashes,
    from_logits,
    onehots,
    embedded,
    keeps,
    targets,
    logit_grads,
    pgs,
    pgm,
    carry_c,
    pg_now,
    pg_out,
    pgm_out,
    pgm_now,
    own_sum,
    chip_out,
    chip_in,
    small_acc,
    small_pair,
    both,
    x_out,
    x_in,
    z_out,
    z_in,
    giw_acc,
    giw_out,
    giw_x_in,
    giw_z_out,
    giw_z_in,
    giw_full,
    emb_part,
    emb_in,
    emb_sums,
    emb_full,
    dec_part,
    dec_x_out,
    dec_x_in,
    dec_z_out,
    dec_z_in,
    in_sem,
    ids_sem,
    wz_sem,
    wx_sem,
    wc_sem,
    iw_sem,
    decg_sem,
    decr_sem,
    hid_sem,
    hidc_sem,
    lg_sem,
    pg_sem,
    pgm_sem,
    small_sem,
    chip_sem,
    gx_sem,
    gz_sem,
    giw_sem,
    emb_sem,
    emb2_sem,
    emb3_sem,
    dsum_sem,
):
    steps, rows, units, vocab, vocab_pad, tokens_all, block = dims
    cols = 4 * units
    half = rows // 2
    part = half // SPLIT
    d, m = lax.axis_index("dp"), lax.axis_index("mp")
    x_at, z_low, z_high = lax.rem(d, 2), lax.rem(lax.div(d, 2), 2), lax.div(d, 4)
    z_at = lax.div(d, 2)
    core, y_at = lax.rem(m, 2), lax.div(m, 2)

    def device(flips):
        return (turn(d, flips[0]), turn(m, flips[1]))

    def slot(flips):
        return turn(z_low, flips[0] // 2) * 4 + turn(m, flips[1])

    def chip(flips):
        return pl.ds(turn(z_low, flips[0] // 2) * 4 + turn(y_at, flips[1] // 2) * 2, 2)

    own = slot((0, 0))

    def copy(src, dst, sems, at, flips):
        return pltpu.make_async_remote_copy(
            src_ref=src,
            dst_ref=dst,
            send_sem=sems.at[(0,) + at],
            recv_sem=sems.at[(1,) + at],
            device_id=device(flips),
            device_id_type=MESH,
        )

    sizes = [block // PIECES] * (PIECES - 1) + [block // PIECES // 2] * 2
    pieces = [(sum(sizes[:p]), size) for p, size in enumerate(sizes)]
    rec_loads = [
        pltpu.make_async_copy(
            rec_ref.at[pl.ds(first, size)], rec_in.at[pl.ds(first, size)], in_sem.at[p]
        )
        for p, (first, size) in enumerate(pieces)
    ]
    iw_load = pltpu.make_async_copy(iw_ref, iw_in, in_sem.at[PIECES + 1])
    for each in rec_loads + [iw_load]:
        each.start()

    barrier = pltpu.get_barrier_semaphore()
    for flips in PEERS:
        pl.semaphore_signal(barrier, inc=1, device_id=device(flips), device_id_type=MESH)
    pl.semaphore_wait(barrier, len(PEERS))


    def weight_rows(index, p):
        first, size = pieces[p]
        side, inside = first // LANES, first % LANES
        return weights.at[
            core,
            side * 4 + lax.div(index, 2),
            :,
            pl.ds(pl.multiple_of(lax.rem(index, 2) * LANES + inside, size), size),
        ]

    def weight_core(index, at, p):
        spot = weight_rows(index, p)
        return copy(spot, spot, wc_sem, (at, p), (0, 1))

    def block_of(at):
        return turn(d, (0, 4, 6, 2)[at % 4] + at // 4)

    def weight_z(k, p):
        flips = COLUMN[k]
        half = turn(z_low, (flips & 2) // 2)
        return copy(
            rec_halves.at[half, :, pl.ds(*pieces[p])], weight_rows(d, p), wz_sem, (k, p), (flips, 0)
        )

    def weight_z_in(k, p):
        spot = weight_rows(turn(d, COLUMN[k]), p)
        return copy(spot, spot, wz_sem, (k, p), (COLUMN[k], 0))

    def weight_x(k, p):
        if k == 3:
            return copy(
                rec_halves.at[z_low, :, pl.ds(*pieces[p])],
                weight_rows(d, p),
                wx_sem,
                (k, p),
                (1, 0),
            )
        spot = weight_rows(turn(d, COLUMN[k]), p)
        return copy(spot, spot, wx_sem, (k, p), (1, 0))

    def weight_x_in(k, p):
        flips = 0 if k == 3 else COLUMN[k]
        spot = weight_rows(turn(d, flips + 1), p)
        return copy(spot, spot, wx_sem, (k, p), (1, 0))

    runs = units // LANES
    width = iw_ref.shape[0]
    dec_rows = dec_ref.shape[0]
    vocab_rows = emb_pad.shape[0]

    def dec_spot(flips):
        at = turn(z_high, flips // 4) * LANES + turn(x_at, flips % 2) * dec_rows
        return dec_all.at[own, pl.ds(pl.multiple_of(at, dec_rows), dec_rows)]

    ids_rows[z_low, 0:steps] = chars_ref[...]
    ids_rows[z_low, 8 : 8 + steps] = nexts_ref[...]
    ids_rows[z_low, 16 : 16 + steps] = resets_ref[...]
    ids_copy = copy(ids_rows.at[z_low], ids_rows.at[z_low], ids_sem, (0,), (2, 0))
    ids_copy.start()

    def weight_start(p):
        for k in range(3):
            weight_z(k, p).start()
        weight_x(3, p).start()

    for p, (first, size) in enumerate(pieces):
        here = slice(first, first + size)
        rec_loads[p].wait()
        for gate in range(4):
            for run in range(runs):
                for side in range(2):
                    at = (run * 2 + side) * LANES
                    to = run * LANES
                    rec_halves[side, gate, here, to : to + LANES] = rec_in[here, gate, at : at + LANES]
        if p < EARLY:
            weight_start(p)
        if p == 0:
            dec_pad[...] = jnp.zeros_like(dec_pad)
            dec_pad[:, :vocab] = dec_ref[...]
            dec_z = copy(dec_pad, dec_spot(0), decg_sem, (0,), (4, 0))
            dec_z.start()
            dec_x = [copy(dec_pad, dec_spot(0), decg_sem, (1,), (1, 0))]
            dec_x[0].start()

    def weight_round(p):
        for k in range(3):
            weight_z_in(k, p).wait_recv()
            weight_x(k, p).start()
            weight_core(block_of(1 + k), 1 + k, p).start()
        if p >= LAG:
            weight_over_x(p - LAG)

    def weights_from_core(which):
        for p in which:
            for at in range(8):
                index = block_of(at)
                first, size = pieces[p]
                inside = first % LANES
                spot = weights.at[
                    1 - core,
                    first // LANES * 4 + lax.div(index, 2),
                    :,
                    pl.ds(pl.multiple_of(lax.rem(index, 2) * LANES + inside, size), size),
                ]
                copy(spot, spot, wc_sem, (at, p), (0, 1)).wait_recv()

    def weight_over_x(p):
        for k in (3, 0, 1, 2):
            weight_x_in(k, p).wait_recv()
            at = 4 if k == 3 else 5 + k
            weight_core(block_of(at), at, p).start()

    for p in range(PIECES + 1):
        weight_rows(d, p)[...] = rec_halves[z_low, :, pl.ds(*pieces[p])]
        weight_core(block_of(0), 0, p).start()
    dec_spot(0)[...] = dec_pad[...]
    emb_pad[...] = jnp.zeros_like(emb_pad)
    emb_pad[:vocab, :width] = emb_ref[...]
    ones_at = lax.broadcasted_iota(jnp.int32, emb_pad.shape, 1) == width
    emb_pad[...] = jnp.where(ones_at, 1.0, emb_pad[...].astype(f32)).astype(bf16)
    iw_pads[core] = jnp.zeros(iw_pads.shape[1:], bf16)
    iw_load.wait()

    def half_lanes(run):
        return pl.ds(pl.multiple_of((run * 2 + z_low) * LANES, LANES), LANES)

    for gate in range(4):
        for run in range(runs):
            to = gate * units + run * LANES
            iw_pads[core, :width, to : to + LANES] = iw_in[:, gate, half_lanes(run)]
            gb_pads[core, :, to : to + LANES] = gb_ref[gate : gate + 1, half_lanes(run)]
    iw_copies = [
        copy(ref.at[core], ref.at[core], iw_sem, (k,), (0, 1))
        for k, ref in enumerate((iw_pads, gb_pads))
    ]
    for each in iw_copies:
        each.start()
    decb_pad[...] = jnp.full(decb_pad.shape, -1e30, f32)
    decb_pad[0, :vocab] = decb_ref[...]
    ids_copy.wait_recv()
    ids_cols[...] = ids_rows[core].T
    vocab_iota = lax.broadcasted_iota(jnp.int32, (vocab_rows, rows), 0)

    def read_ids(t):
        now = jnp.concatenate([ids_rows[0, t : t + 1], ids_rows[1, t : t + 1]], axis=1)
        onehots[t] = (vocab_iota == now).astype(f32).astype(bf16)
        targets[t] = jnp.broadcast_to(ids_cols[:, 8 + t : 9 + t], (half, LANES))
        keeps[t] = jnp.broadcast_to((1 - ids_cols[:, 16 + t : 17 + t]).astype(f32), (half, LANES))

    def project(t):
        read_ids(t)
        chosen = t_dot(onehots[t], emb_pad[...]).astype(bf16)
        embedded[t] = chosen
        mine = embedded[t, pl.ds(pl.multiple_of(core * half, half), half)]
        for c in range(2):
            gates[t, c] = dot(mine, iw_pads[c]) + gb_pads[c]

    for k, ref in enumerate((iw_pads, gb_pads)):
        copy(ref.at[1 - core], ref.at[1 - core], iw_sem, (k,), (0, 1)).wait_recv()
    project(0)

    def span(s):
        return pl.ds(s * part, part)

    def wide(s):
        return pl.ds(pl.multiple_of(core * half + s * part, part), part)

    def hidden_copy(t, s, j):
        spot = hid.at[chip((0, 0)), t, wide(s)]
        return copy(spot, spot, hid_sem, (t, s, j), CHIPS[j])

    def hidden_in(t, s, j):
        spot = hid.at[chip(CHIPS[j]), t, wide(s)]
        return copy(spot, spot, hid_sem, (t, s, j), CHIPS[j])

    def hidden_core(t, s):
        spot = hid.at[:, t, wide(s)]
        return copy(spot, spot, hidc_sem, (t, s), (0, 1))

    def hidden_core_in(t, s):
        rows_there = pl.ds(pl.multiple_of((1 - core) * half + s * part, part), part)
        spot = hid.at[:, t, rows_there]
        return copy(spot, spot, hidc_sem, (t, s), (0, 1))

    def cell_step(t, s, added):
        here = span(s)
        if added is not None:
            keep = keeps[t, here, :1]
        for c in range(2):
            preact = [gates[t, c, here, k * units : (k + 1) * units] for k in range(4)]
            if added is not None:
                preact = [preact[k] + keep * added[c][k] for k in range(4)]
            in_gate = jax.nn.sigmoid(preact[0])
            forget = jax.nn.sigmoid(preact[1])
            candidate = jnp.tanh(preact[2])
            out_gate = jax.nn.sigmoid(preact[3])
            cell = in_gate * candidate
            if added is not None:
                cell = forget * keep * cells[t - 1, c, here] + cell
            cells[t, c, here] = cell
            squash = jnp.tanh(cell)
            hid[z_low * 4 + y_at * 2 + c, t, wide(s)] = (out_gate * squash).astype(bf16)
            squashes[t, c, here] = squash
            gates[t, c, here, :units] = in_gate
            gates[t, c, here, units : 2 * units] = forget
            gates[t, c, here, 2 * units : 3 * units] = candidate
            gates[t, c, here, 3 * units :] = out_gate
        for j in (2, 0, 1):
            hidden_copy(t, s, j).start()

    def add_slot(total, t, here, at):
        some = hid[at, t, here]
        for c in range(2):
            for gate in range(4):
                more = dot(some, weights[c, at, gate])
                total[c][gate] = more if total[c][gate] is None else total[c][gate] + more

    for s in range(SPLIT):
        cell_step(0, s, None)

    for p in range(EARLY, PIECES + 1):
        weight_start(p)
    weight_round(0)
    project(1)
    project(2)
    weight_round(1)
    spot = dec_spot(4)
    copy(spot, spot, decg_sem, (0,), (4, 0)).wait_recv()
    dec_x.append(copy(spot, spot, decg_sem, (2,), (1, 0)))
    dec_x[1].start()
    project(3)
    weight_round(2)
    project(4)
    project(5)
    weight_round(3)
    for j, flips in enumerate((1, 5)):
        spot = dec_spot(flips)
        copy(spot, spot, decg_sem, (1 + j,), (1, 0)).wait_recv()
    dec_own = dec_all.at[own]
    dec_sends = [
        copy(dec_own, dec_own, decr_sem, (j,), flips) for j, flips in enumerate(CHIPS + ((0, 1),))
    ]
    for each in dec_sends:
        each.start()
    weight_round(4)
    weight_round(5)
    weights_from_core(range(PIECES // 2))
    for s in range(SPLIT):
        for j in range(3):
            hidden_in(0, s, j).wait_recv()
    mine = pl.ds(pl.multiple_of(core * half, half), half)
    total = [[None] * 4, [None] * 4]
    for at in range(4):
        add_slot(total, 0, mine, at)
    for c in range(2):
        for gate in range(4):
            lanes = slice(gate * units, (gate + 1) * units)
            gates[1, c, :, lanes] += keeps[1, :, :1] * total[c][gate]
    for p in range(6, PIECES + 1):
        weight_round(p)
    for p in range(PIECES + 1 - LAG, PIECES + 1):
        weight_over_x(p)
    weights_from_core(range(PIECES // 2, PIECES + 1))

    def dec_relay(j):
        spot = dec_all.at[slot(CHIPS[j])]
        return copy(spot, spot, decr_sem, (4 + j,), (0, 1))

    def pass_decoder():
        for j in range(3):
            spot = dec_all.at[slot(CHIPS[j])]
            copy(spot, spot, decr_sem, (j,), CHIPS[j]).wait_recv()
            dec_relay(j).start()

    def weight_sent():
        for p in range(PIECES + 1):
            for at in range(8):
                weight_core(block_of(at), at, p).wait_send()
            for k in range(4):
                weight_x(k, p).wait_send()

    def add_chip(total, t, s, flips):
        first = turn(z_low, flips[0] // 2) * 4 + turn(y_at, flips[1] // 2) * 2
        for k in range(2):
            add_slot(total, t, wide(s), first + k)

    def gather_hidden(t, s):
        total = [[None] * 4, [None] * 4]
        add_chip(total, t, s, (0, 0))
        for j in range(3):
            hidden_in(t, s, j).wait_recv()
            add_chip(total, t, s, CHIPS[j])
        hidden_core(t, s).start()
        return total

    vocab_part = lax.broadcasted_iota(jnp.int32, (part, vocab_pad), 1)
    last_lane = lax.broadcasted_iota(jnp.int32, (1, vocab_pad), 1) == vocab_pad - 1
    small_acc[...] = jnp.zeros_like(small_acc)

    def lg_copy(t, s):
        spot = logit_grads.at[t, wide(s)]
        return copy(spot, spot, lg_sem, (t, s), (0, 1))

    def decode(t, s):
        here = span(s)
        logits = decb_pad[...]
        for at in range(8):
            logits = logits + dot(hid[at, t, wide(s)], dec_all[at])
        top = jnp.max(logits, axis=1, keepdims=True)
        exps = jnp.exp(logits - top)
        total = jnp.sum(exps, axis=1, keepdims=True)
        hot = targets[t, here, :1] == vocab_part
        picked = jnp.sum(jnp.where(hot, logits, 0.0), axis=1, keepdims=True)
        lost = top + jnp.log(total) - picked
        grad = ((exps / total - jnp.where(hot, 1.0, 0.0)) / tokens_all).astype(bf16)
        logit_grads[t, wide(s)] = grad
        lg_copy(t, s).start()
        for c in range(2):
            from_logits[t, c, here] = dot_t(grad, dec_all[z_low * 4 + y_at * 2 + c])
        small_acc[...] += jnp.sum(grad.astype(f32), axis=0, keepdims=True) + jnp.where(
            last_lane, jnp.sum(lost, axis=0, keepdims=True) / tokens_all, 0.0
        )

    def forward(t, _):
        for s in range(SPLIT):
            cell_step(t, s, gather_hidden(t - 1, s))
            decode(t - 1, s)
        return 0

    @pl.when(core == 1)
    def _():
        pass_decoder()

    total = [[None] * 4, [None] * 4]
    for at in range(4, 8):
        add_slot(total, 0, mine, at)
    for s in range(SPLIT):
        here = slice(s * part, (s + 1) * part)
        cell_step(1, s, [[more[here] for more in total[c]] for c in range(2)])
        hidden_core(0, s).start()

    @pl.when(core == 0)
    def _():
        pass_decoder()

    spot = dec_all.at[slot((0, 1))]
    copy(spot, spot, decr_sem, (3,), (0, 1)).wait_recv()
    for j in range(3):
        spot = dec_all.at[slot((CHIPS[j][0], CHIPS[j][1] + 1))]
        copy(spot, spot, decr_sem, (4 + j,), (0, 1)).wait_recv()
    for s in range(SPLIT):
        decode(0, s)
    lax.fori_loop(2, steps, forward, 0)

    def pg_copy(t, s):
        return copy(pg_out.at[t, span(s)], pgs.at[t, wide(s)], pg_sem, (t, s), (0, 1))

    def pgm_copy(t, s):
        return copy(
            pgm_out.at[t - 1, span(s)], pgm.at[t - 1, wide(s)], pgm_sem, (t - 1, s), (0, 1)
        )

    def cell_back(t, s, carried, first):
        here = span(s)
        if not first:
            keep = keeps[t, here, :1]
        for c in range(2):
            hidden_grad = from_logits[t, c, here]
            if carried is not None:
                hidden_grad = hidden_grad + carried[:, c * units : (c + 1) * units]
            in_gate = gates[t, c, here, :units]
            forget = gates[t, c, here, units : 2 * units]
            candidate = gates[t, c, here, 2 * units : 3 * units]
            out_gate = gates[t, c, here, 3 * units :]
            squash = squashes[t, c, here]
            cell_grad = hidden_grad * out_gate * (1.0 - squash * squash)
            if carried is not None:
                cell_grad = cell_grad + carry_c[c, here]
            grads = [
                cell_grad * candidate * in_gate * (1.0 - in_gate),
                None,
                cell_grad * in_gate * (1.0 - candidate * candidate),
                hidden_grad * squash * out_gate * (1.0 - out_gate),
            ]
            if first:
                grads[1] = jnp.zeros_like(cell_grad)
            else:
                grads[1] = cell_grad * (keep * cells[t - 1, c, here]) * forget * (1.0 - forget)
                carry_c[c, here] = keep * forget * cell_grad
            for k in range(4):
                pg_now[c, here, k * units : (k + 1) * units] = grads[k].astype(bf16)
                if not first:
                    pgm_now[c, here, k * units : (k + 1) * units] = (keep * grads[k]).astype(bf16)

    def share(t, s, first):
        here = span(s)
        pgs[t, wide(s)] = pg_now[core, here]
        pg_out[t, here] = pg_now[1 - core, here]
        if not first:
            pgm[t - 1, wide(s)] = pgm_now[core, here]
            pgm_out[t - 1, here] = pgm_now[1 - core, here]
            pgm_copy(t, s).start()
        pg_copy(t, s).start()

    def chip_copy(t, s, j):
        return copy(
            chip_out.at[t - 1, s, j], chip_in.at[t - 1, s, j], chip_sem, (t - 1, s, j), CHIPS[j]
        )

    def spread(t, s):
        here = span(s)
        for j in (2, 0, 1, 3):
            flips = CHIPS[j] if j < 3 else (0, 0)
            first = turn(z_low, flips[0] // 2) * 4 + turn(y_at, flips[1] // 2) * 2
            for k in range(2):
                part_sum = None
                for c in range(2):
                    for gate in range(4):
                        grad = pgm_now[c, here, gate * units : (gate + 1) * units]
                        more = dot(grad, weights[c, first + k, gate])
                        part_sum = more if part_sum is None else part_sum + more
                lanes = slice(k * units, (k + 1) * units)
                if j < 3:
                    chip_out[t - 1, s, j, :, lanes] = part_sum.astype(bf16)
                else:
                    own_sum[s, :, lanes] = part_sum
            if j < 3:
                chip_copy(t, s, j).start()

    def carried_in(t, s):
        total = own_sum[s]
        for j in range(3):
            chip_copy(t + 1, s, j).wait_recv()
            total = total + chip_in[t, s, j].astype(f32)
        return total

    last = steps - 1

    weight_sent()

    def turn_over(at, _):
        for c in range(2):
            for gate in range(4):
                weights[c, at, gate] = weights[c, at, gate].T
        return 0

    lax.fori_loop(0, 8, turn_over, 0)
    for s in range(SPLIT):
        for j in range(3):
            hidden_in(last, s, j).wait_recv()
        hidden_core(last, s).start()
        decode(last, s)
        cell_back(last, s, None, False)
        spread(last, s)
        share(last, s, False)

    def other_rows(s):
        return pl.ds(pl.multiple_of((1 - core) * half + s * part, part), part)

    def dsum_x():
        return copy(dec_x_out, dec_x_in, dsum_sem, (0,), (1, 0))

    def dsum_z(k):
        return copy(dec_z_out, dec_z_in, dsum_sem, (k,), (4, 0))

    def small_copy():
        return copy(small_pair.at[core], small_pair.at[core], small_sem, (0,), (0, 1))

    def decoder_grad():
        for t in range(steps):
            for s in range(SPLIT):
                hidden_core_in(t, s).wait_recv()
                spot = logit_grads.at[t, other_rows(s)]
                copy(spot, spot, lg_sem, (t, s), (0, 1)).wait_recv()
        small_pair[core] = small_acc[...]
        small_copy().start()
        dec_part[...] = t_dot(
            hid[own].reshape(steps * rows, units),
            logit_grads[...].reshape(steps * rows, vocab_pad),
        ).reshape(2, 2, dec_rows, vocab_pad)
        for k in range(2):
            dec_x_out[k] = dec_part[k, 1 - x_at].astype(bf16)
        dsum_x().start()

    def decoder_grad_z():
        dsum_x().wait_recv()
        dec_z_out[...] = (
            dec_part[1 - z_high, x_at] + dec_x_in[1 - z_high].astype(f32)
        ).astype(bf16)
        dsum_z(1).start()

    def backward(i, _):
        t = last - i
        for s in range(SPLIT):
            cell_back(t, s, carried_in(t, s), False)
            spread(t, s)
            share(t, s, False)

        @pl.when(i == 2)
        def _():
            decoder_grad()

        @pl.when(i == 3)
        def _():
            decoder_grad_z()

        return 0

    lax.fori_loop(1, last - 1, backward, 0)
    for s in range(SPLIT):
        cell_back(1, s, carried_in(1, s), False)
        share(1, s, False)

    acc = gates.at[pl.ds(steps - 4, 4)]

    far = (2, 3, 1, 0)

    piece_rows = LANES // SUB

    def x_copy(k, side, sub):
        here = pl.ds(sub * piece_rows, piece_rows)
        return copy(
            x_out.at[k, side, here], x_in.at[k, side, here], gx_sem, (k, side, sub), (1, 0)
        )

    def z_copy(k, side, sub):
        here = pl.ds(sub * piece_rows, piece_rows)
        return copy(
            z_out.at[k, side, here], z_in.at[k, side, here], gz_sem, (k, side, sub), (far[k] * 2, 0)
        )

    used = (steps - 1) * rows

    def from_core(t, _):
        for s in range(SPLIT):
            spot = pgs.at[t, other_rows(s)]
            copy(spot, spot, pg_sem, (t, s), (0, 1)).wait_recv()
            spot = pgm.at[t - 1, other_rows(s)]
            copy(spot, spot, pgm_sem, (t - 1, s), (0, 1)).wait_recv()
        return 0

    lax.fori_loop(1, steps, from_core, 0)

    def weight_grad(k, side):
        at = side * 4 + turn(z_at, far[k])
        both[...] = t_dot(
            hid[at, 0 : steps - 1].reshape(used, units), pgm[...].reshape(used, cols)
        ).reshape(2, LANES, cols)
        x_out[k, side] = both[1 - x_at].astype(bf16)
        acc[k, side] = both[x_at]

    def weight_grad_first(side):
        at = side * 4 + turn(z_at, far[0])
        for k in (1, 0):
            lanes = pl.ds(pl.multiple_of((x_at if k == 0 else 1 - x_at) * LANES, LANES), LANES)
            some = t_dot(
                hid[at, 0 : steps - 1, :, lanes].reshape(used, LANES),
                pgm[...].reshape(used, cols),
            )
            if k:
                x_out[0, side] = some.astype(bf16)
                send_eighth(2 * side, 2 * side + 1)
            else:
                acc[0, side] = some

    order = [(k, side, sub) for k in range(4) for side in range(2) for sub in range(SUB)]

    def send_eighth(*which):
        for at in which:
            for k in range(SUB // 2):
                x_copy(*order[at * (SUB // 2) + k]).start()

    def pass_z(at):
        for k in range(SUB // 2):
            pass_piece(at * (SUB // 2) + k)

    def pass_piece(at):
        k, side, sub = order[at]
        here = pl.ds(sub * piece_rows, piece_rows)
        x_copy(k, side, sub).wait_recv()
        total = acc[k, side, here] + x_in[k, side, here].astype(f32)
        if k == 3:
            acc[k, side, here] = total
            return
        z_out[k, side, here] = total.astype(bf16)
        if at in range(3, 4 * SUB):
            z_copy(*order[at - 3]).wait_send()
        z_copy(k, side, sub).start()

    def scatter(here, side, gate, value):
        for run in range(runs):
            at = pl.multiple_of((run * 2 + side) * LANES, LANES)
            out_rec[here, gate, pl.ds(at, LANES)] = value[:, run * LANES : (run + 1) * LANES]

    def finish(at):
        pass_z(12 + at)
        for which in range(at * (SUB // 2), (at + 1) * (SUB // 2)):
            side, sub = divmod(which, SUB)
            for k in range(3):
                z_copy(k, side, sub).wait_recv()
            here = pl.ds(side * LANES + sub * piece_rows, piece_rows)
            mine = pl.ds(sub * piece_rows, piece_rows)
            for gate in range(4):
                lanes = slice(gate * units, (gate + 1) * units)
                value = acc[3, side, mine, lanes] + z_in[0, side, mine, lanes].astype(f32)
                scatter(here, z_low, gate, value)
                value = z_in[1, side, mine, lanes].astype(f32) + z_in[2, side, mine, lanes].astype(
                    f32
                )
                scatter(here, 1 - z_low, gate, value)

    weight_grad_first(0)
    weight_grad(0, 1)
    send_eighth(2, 3)
    for s in range(SPLIT):
        spread(1, s)
    pass_piece(0)
    pass_piece(1)
    weight_grad(1, 0)
    pass_piece(2)
    weight_grad(2, 0)
    pass_piece(3)

    for s in range(SPLIT):
        cell_back(0, s, carried_in(0, s), True)
        share(0, s, True)
    for s in range(SPLIT):
        spot = pgs.at[0, other_rows(s)]
        copy(spot, spot, pg_sem, (0, s), (0, 1)).wait_recv()
    tokens = steps * rows
    giw_rows = giw_acc.shape[0]
    giw_acc[...] = t_dot(
        embedded[...].reshape(tokens, LANES), pgs[...].reshape(tokens, cols)
    )[:giw_rows]
    for k in range(2):
        at = pl.multiple_of((1 - x_at) * (2 * units) + k * units, units)
        giw_out[k] = giw_acc[:, pl.ds(at, units)].astype(bf16)
    giw_x = copy(giw_out, giw_x_in, giw_sem, (0,), (1, 0))
    giw_x.start()
    send_eighth(4, 8)
    pass_piece(4)

    emb_rows = emb_full.shape[1]
    by_char = jnp.zeros((vocab_rows, 2 * LANES), f32)
    for t in range(steps):
        by_token = dot_t(pgs[t], iw_pads[core])
        high = by_token.astype(bf16)
        low = (by_token - high.astype(f32)).astype(bf16)
        by_char = by_char + dot(onehots[t], jnp.concatenate([high, low], axis=1))
    emb_part[...] = (by_char[:, :LANES] + by_char[:, LANES:]).reshape(8, emb_rows, LANES)
    emb_copies = [
        copy(emb_part.at[slot(flips)], emb_in.at[own], emb_sem, (j,), flips)
        for j, flips in enumerate(GROUP)
    ]
    for each in emb_copies:
        each.start()
    emb_in[own] = emb_part[own]
    pass_piece(5)
    weight_grad(1, 1)

    giw_x.wait_recv()
    for k in range(2):
        at = pl.multiple_of(x_at * (2 * units) + k * units, units)
        giw_acc[:, pl.ds(at, units)] += giw_x_in[k].astype(f32)
    giw_z_out[...] = giw_acc[
        :, pl.ds(pl.multiple_of(x_at * (2 * units) + (1 - z_high) * units, units), units)
    ].astype(bf16)
    giw_z = copy(giw_z_out, giw_z_in, giw_sem, (1,), (4, 0))
    giw_z.start()
    send_eighth(5, 9)
    pass_piece(6)
    for j, flips in enumerate(GROUP):
        spot = emb_in.at[slot(flips)]
        copy(spot, spot, emb_sem, (j,), flips).wait_recv()
    total = emb_in[0]
    for at in range(1, 8):
        total = total + emb_in[at]

    def place(flips):
        return turn(z_high, flips // 4) * 2 + turn(x_at, flips % 2)

    emb_sums[place(0), :emb_rows] = total
    spot = small_pair.at[1 - core]
    copy(spot, spot, small_sem, (0,), (0, 1)).wait_recv()
    smalls = small_pair[0] + small_pair[1]
    for k in range(vocab_pad // LANES):
        emb_sums[place(0), emb_rows + k : emb_rows + k + 1] = smalls[
            :, k * LANES : (k + 1) * LANES
        ]
    spot = emb_sums.at[place(0)]
    emb2 = [copy(spot, spot, emb2_sem, (j,), (flips, 0)) for j, flips in enumerate(OTHERS)]
    for each in emb2:
        each.start()
    weight_grad(2, 1)
    pass_piece(7)
    send_eighth(6, 10)
    weight_grad(3, 0)
    weight_grad(3, 1)

    giw_z.wait_recv()
    gate_at = x_at * 2 + z_high
    giw_full[z_low, gate_at] = (
        giw_acc[:, pl.ds(pl.multiple_of(gate_at * units, units), units)] + giw_z_in[...].astype(f32)
    ).astype(bf16)
    spot = giw_full.at[z_low, gate_at]
    giw_back_z = copy(spot, spot, giw_sem, (2,), (4, 0))
    giw_back_z.start()

    giw_turn = (gate_at, x_at * 2 + 1 - z_high, (1 - x_at) * 2, (1 - x_at) * 2 + 1)

    def giw_side(k, half_at):
        spot = giw_full.at[half_at, giw_turn[k]]
        return copy(spot, spot, giw_sem, (4 + k,), (2, 0))

    giw_side(0, z_low).start()
    pass_piece(8)
    send_eighth(7, 11)
    pass_piece(9)
    pass_z(8)
    for j, flips in enumerate(OTHERS):
        spot = emb_sums.at[place(flips)]
        copy(spot, spot, emb2_sem, (j,), (flips, 0)).wait_recv()
    sums = (emb_sums[0] + emb_sums[1]) + (emb_sums[2] + emb_sums[3])
    emb_full[own] = sums[:emb_rows]
    spot = emb_full.at[own]
    emb3 = [copy(spot, spot, emb3_sem, (j,), flips) for j, flips in enumerate(GROUP)]
    for each in emb3:
        each.start()
    for k in range(vocab_pad // LANES):
        lanes = slice(k * LANES, min(vocab, (k + 1) * LANES))
        out_decb[:, lanes] = sums[emb_rows + k : emb_rows + k + 1, : lanes.stop - lanes.start]
    k = vocab_pad // LANES - 1
    out_loss[...] = sums[emb_rows + k : emb_rows + k + 1, LANES - 1 :]
    spot = giw_full.at[z_low, x_at * 2 + 1 - z_high]
    copy(spot, spot, giw_sem, (2,), (4, 0)).wait_recv()
    giw_side(1, z_low).start()
    spot = giw_full.at[z_low, pl.ds(x_at * 2, 2)]
    giw_back_x = copy(spot, spot, giw_sem, (3,), (1, 0))
    giw_back_x.start()
    send_eighth(12, 13, 14, 15)
    pass_piece(10)
    pass_z(9)
    pass_piece(11)
    spot = giw_full.at[z_low, pl.ds((1 - x_at) * 2, 2)]
    copy(spot, spot, giw_sem, (3,), (1, 0)).wait_recv()
    giw_side(2, z_low).start()
    pass_piece(12)
    pass_z(10)
    dsum_z(1).wait_recv()
    total = dec_part[z_high, x_at] + dec_x_in[z_high].astype(f32) + dec_z_in[...].astype(f32)
    out_dec[...] = total[:, :vocab]
    pass_piece(13)
    pass_z(11)
    for j, flips in enumerate(GROUP):
        spot = emb_full.at[slot(flips)]
        copy(spot, spot, emb3_sem, (j,), flips).wait_recv()
    out_emb[...] = emb_full[...].reshape(vocab_rows, LANES)[:vocab, :width]
    finish(0)
    giw_side(3, z_low).start()
    pass_piece(14)
    ids_copy.wait_send()
    dec_z.wait_send()
    for each in dec_x + dec_sends + [dec_relay(j) for j in range(3)] + iw_copies + [small_copy(), dsum_x(), dsum_z(1)]:
        each.wait_send()
    for p in range(PIECES + 1):
        for k in range(3):
            weight_z(k, p).wait_send()

    def sent(t, _):
        for s in range(SPLIT):
            for j in range(3):
                hidden_copy(t, s, j).wait_send()
            hidden_core(t, s).wait_send()
            lg_copy(t, s).wait_send()
            pg_copy(t, s).wait_send()
        return 0

    lax.fori_loop(0, steps, sent, 0)

    def sent_back(t, _):
        for s in range(SPLIT):
            pgm_copy(t, s).wait_send()
            for j in range(3):
                chip_copy(t, s, j).wait_send()
        return 0

    lax.fori_loop(1, steps, sent_back, 0)
    finish(1)
    pass_piece(15)
    finish(2)
    finish(3)
    for k in range(4):
        giw_side(k, 1 - z_low).wait_recv()
    for side in range(2):
        for gate in range(4):
            value = giw_full[side, gate].astype(f32)
            for run in range(runs):
                to = slice((run * 2 + side) * LANES, (run * 2 + side + 1) * LANES)
                lanes = slice(run * LANES, (run + 1) * LANES)
                out_iw[:, gate, to] = value[:width, lanes]
                out_gb[gate : gate + 1, to] = value[width : width + 1, lanes]

    for each in [giw_x, giw_z, giw_back_z, giw_back_x]:
        each.wait_send()
    for k in range(4):
        giw_side(k, z_low).wait_send()
    for each in emb_copies + emb2 + emb3:
        each.wait_send()
    for at, spot in enumerate(order):
        x_copy(*spot).wait_send()
        if spot[0] < 3 and at not in range(4 * SUB - 3):
            z_copy(*spot).wait_send()


def hand_over(*refs):
    sources, places, flat, sems = list(refs[:7]), refs[7:14], refs[14], refs[15]
    flat[...] = sources[6][...].reshape(flat.shape)
    sources[6] = flat
    copies = [
        pltpu.make_async_copy(src, dst, sems.at[k])
        for k, (src, dst) in enumerate(zip(sources, places))
    ]
    for each in copies:
        each.start()
    for each in copies:
        each.wait()


def grouped(
    char_ids,
    next_chars,
    resets,
    embedding,
    input_weight,
    recurrent_weight,
    gate_bias,
    decoder_weight,
    decoder_bias,
):
    data_count = lax.axis_size("dp")
    row_count, steps = char_ids.shape
    vocab, width = embedding.shape
    local_units = input_weight.shape[2]
    block = recurrent_weight.shape[0]
    units = local_units // 2
    cols = 4 * units
    rows = 2 * row_count
    dec_rows = decoder_weight.shape[2]
    vocab_pad = pl.cdiv(vocab, LANES) * LANES
    tokens_all = row_count * steps * data_count
    half = rows // 2
    part = half // SPLIT
    emb_rows = pl.cdiv(vocab, 64) * 8
    giw_rows = pl.cdiv(width + 1, 16) * 16

    vocab_rows = 8 * emb_rows
    by_gate = recurrent_weight.transpose(1, 0, 2)
    in_by_gate = input_weight.transpose(1, 0, 2)
    dec = decoder_weight.reshape(dec_rows, vocab)

    vmem = pl.BlockSpec(memory_space=pltpu.VMEM)
    anywhere = pl.BlockSpec(memory_space=pl.ANY)
    dims = (steps, rows, units, vocab, vocab_pad, tokens_all, block)

    def sems(*shape):
        return pltpu.SemaphoreType.DMA((2,) + shape)

    loss, emb_grad, in_grad, rec_grad, bias_grad, dec_grad, dec_bias_grad = pl.pallas_call(
        functools.partial(layer_kernel, dims),
        out_shape=[
            pltpu.VMEM((1, 1), f32),
            pltpu.VMEM((vocab, width), f32),
            pltpu.VMEM((width, 4, local_units), f32),
            pltpu.VMEM((block, 4, local_units), f32),
            pltpu.VMEM((4, local_units), f32),
            pltpu.VMEM((dec_rows, vocab), f32),
            pltpu.VMEM((1, vocab), f32),
        ],
        in_specs=[vmem] * 4 + [anywhere] * 2 + [vmem] * 3,
        out_specs=[vmem] * 7,
        scratch_shapes=[
            pltpu.VMEM((block, 4, local_units), bf16),
            pltpu.VMEM((width, 4, local_units), bf16),
            pltpu.VMEM((2, LANES, row_count), jnp.int32),
            pltpu.VMEM((row_count, LANES), jnp.int32),
            pltpu.VMEM((2, 4, block, units), bf16),
            pltpu.VMEM((2, 8, 4, units, units), bf16),
            pltpu.VMEM((vocab_rows, LANES), bf16),
            pltpu.VMEM((2, LANES, cols), bf16),
            pltpu.VMEM((2, 1, cols), f32),
            pltpu.VMEM((dec_rows, vocab_pad), bf16),
            pltpu.VMEM((1, vocab_pad), f32),
            pltpu.VMEM((8, units, vocab_pad), bf16),
            pltpu.VMEM((8, steps, rows, units), bf16),
            pltpu.VMEM((steps, 2, half, cols), f32),
            pltpu.VMEM((steps, 2, half, units), f32),
            pltpu.VMEM((steps, 2, half, units), f32),
            pltpu.VMEM((steps, 2, half, units), f32),
            pltpu.VMEM((steps, vocab_rows, rows), bf16),
            pltpu.VMEM((steps, rows, LANES), bf16),
            pltpu.VMEM((steps, half, LANES), f32),
            pltpu.VMEM((steps, half, LANES), jnp.int32),
            pltpu.VMEM((steps, rows, vocab_pad), bf16),
            pltpu.VMEM((steps, rows, cols), bf16),
            pltpu.VMEM((steps - 1, rows, cols), bf16),
            pltpu.VMEM((2, half, units), f32),
            pltpu.VMEM((2, half, cols), bf16),
            pltpu.VMEM((steps, half, cols), bf16),
            pltpu.VMEM((steps - 1, half, cols), bf16),
            pltpu.VMEM((2, half, cols), bf16),
            pltpu.VMEM((SPLIT, part, 2 * units), f32),
            pltpu.VMEM((steps - 1, SPLIT, 3, part, 2 * units), bf16),
            pltpu.VMEM((steps - 1, SPLIT, 3, part, 2 * units), bf16),
            pltpu.VMEM((1, vocab_pad), f32),
            pltpu.VMEM((2, 1, vocab_pad), f32),
            pltpu.VMEM((2, LANES, cols), f32),
            pltpu.VMEM((4, 2, LANES, cols), bf16),
            pltpu.VMEM((4, 2, LANES, cols), bf16),
            pltpu.VMEM((3, 2, LANES, cols), bf16),
            pltpu.VMEM((3, 2, LANES, cols), bf16),
            pltpu.VMEM((giw_rows, cols), f32),
            pltpu.VMEM((2, giw_rows, units), bf16),
            pltpu.VMEM((2, giw_rows, units), bf16),
            pltpu.VMEM((giw_rows, units), bf16),
            pltpu.VMEM((giw_rows, units), bf16),
            pltpu.VMEM((2, 4, giw_rows, units), bf16),
            pltpu.VMEM((8, emb_rows, LANES), f32),
            pltpu.VMEM((8, emb_rows, LANES), f32),
            pltpu.VMEM((4, emb_rows + 8, LANES), f32),
            pltpu.VMEM((8, emb_rows, LANES), f32),
            pltpu.VMEM((2, 2, dec_rows, vocab_pad), f32),
            pltpu.VMEM((2, dec_rows, vocab_pad), bf16),
            pltpu.VMEM((2, dec_rows, vocab_pad), bf16),
            pltpu.VMEM((dec_rows, vocab_pad), bf16),
            pltpu.VMEM((dec_rows, vocab_pad), bf16),
            pltpu.SemaphoreType.DMA((PIECES + 2,)),
            sems(1),
            sems(3, PIECES + 1),
            sems(4, PIECES + 1),
            sems(8, PIECES + 1),
            sems(2),
            sems(3),
            sems(7),
            sems(steps, SPLIT, 3),
            sems(steps, SPLIT),
            sems(steps, SPLIT),
            sems(steps, SPLIT),
            sems(steps - 1, SPLIT),
            sems(1),
            sems(steps - 1, SPLIT, 3),
            sems(4, 2, SUB),
            sems(3, 2, SUB),
            sems(8),
            sems(7),
            sems(3),
            sems(7),
            sems(2),
        ],
        compiler_params=pltpu.CompilerParams(
            collective_id=0, has_side_effects=True, vmem_limit_bytes=60 << 20
        ),
    )(
        char_ids.T,
        next_chars.T,
        resets.T,
        embedding,
        input_weight,
        recurrent_weight,
        gate_bias,
        dec,
        decoder_bias,
    )
    results = [loss, emb_grad, in_grad, rec_grad, bias_grad, dec_grad, dec_bias_grad]
    results = [pltpu.with_memory_space_constraint(each, pltpu.VMEM) for each in results]
    loss, emb_grad, in_grad, rec_grad, bias_grad, dec_grad, dec_bias_grad = pl.pallas_call(
        hand_over,
        out_shape=[jax.ShapeDtypeStruct(each.shape, f32) for each in results[:-1]]
        + [jax.ShapeDtypeStruct((vocab,), f32)],
        in_specs=[vmem] * 7,
        out_specs=[anywhere] * 7,
        scratch_shapes=[pltpu.VMEM((vocab,), f32), pltpu.SemaphoreType.DMA((7,))],
        compiler_params=pltpu.CompilerParams(vmem_limit_bytes=2 << 20),
    )(*results)
    return (
        loss.reshape(()),
        emb_grad,
        in_grad,
        rec_grad,
        bias_grad,
        dec_grad.reshape(decoder_weight.shape),
        dec_bias_grad,
    )


def on_device(
    char_ids,
    next_chars,
    resets,
    embedding,
    input_weight,
    recurrent_weight,
    gate_bias,
    decoder_weight,
    decoder_bias,
):
    highest = lax.Precision.HIGHEST
    data_count = lax.axis_size("dp")
    row_count, step_count = char_ids.shape
    vocab_size, width_in = embedding.shape
    local_units = input_weight.shape[2]
    gate_cols = 4 * local_units
    tokens_here = row_count * step_count
    tokens_all = tokens_here * data_count
    gathered_rec, gathered_dec = (
        lax.all_gather(recurrent_weight, "dp", axis=0, tiled=True),
        lax.all_gather(decoder_weight, "dp", axis=1, tiled=True),
    )
    hidden_total = gathered_rec.shape[0]
    rec_matrix = gathered_rec.reshape(hidden_total, gate_cols)
    dec_matrix = gathered_dec.reshape(local_units, vocab_size)
    time_ids = char_ids.T
    keep_mask = (1 - resets.T).astype(f32)
    proj_table = jnp.dot(
        embedding, input_weight.reshape(width_in, gate_cols), preferred_element_type=f32
    )
    projected = jnp.take(proj_table, time_ids, axis=0) + gate_bias.reshape(gate_cols)

    def forward_step(state_pair, inputs):
        hidden_loc, cell_state = state_pair
        proj_now, keep_now = inputs
        hidden_full = lax.all_gather(hidden_loc, "mp", axis=1, tiled=True)
        previous = hidden_full * keep_now[:, None].astype(bf16)
        preact = proj_now + jnp.dot(previous, rec_matrix, preferred_element_type=f32)
        gate_vals = preact.reshape(row_count, 4, local_units)
        in_gate = jax.nn.sigmoid(gate_vals[:, 0])
        forget_gate = jax.nn.sigmoid(gate_vals[:, 1])
        cell_gate = jnp.tanh(gate_vals[:, 2])
        out_gate = jax.nn.sigmoid(gate_vals[:, 3])
        new_cell = forget_gate * cell_state * keep_now[:, None] + in_gate * cell_gate
        new_hidden = (out_gate * jnp.tanh(new_cell)).astype(bf16)
        return ((new_hidden, new_cell), (previous, preact, new_cell, new_hidden))

    first_state = (
        jnp.zeros((row_count, local_units), bf16),
        jnp.zeros((row_count, local_units), f32),
    )
    _, (prevs, preacts, cells, hiddens) = lax.scan(
        forward_step, first_state, (projected, keep_mask)
    )
    flat_hidden = hiddens.reshape(tokens_here, local_units)
    partial_value = jnp.dot(flat_hidden, dec_matrix, preferred_element_type=f32)
    flat_targets = next_chars.T.reshape(tokens_here)
    logit_rows = lax.psum(partial_value, "mp")
    shifted_in = logit_rows + decoder_bias
    row_max = jnp.max(shifted_in, axis=1)
    exp_total = jnp.sum(jnp.exp(shifted_in - row_max[:, None]), axis=1)
    log_total = row_max + jnp.log(exp_total)
    softmax_out = jnp.exp(shifted_in - log_total[:, None])
    onehot = (flat_targets[:, None] == jnp.arange(vocab_size, dtype=jnp.int32)[None, :]).astype(f32)
    picked = jnp.sum(shifted_in * onehot, axis=1)
    grad_rows = ((softmax_out - onehot) / tokens_all).astype(bf16)
    local_loss = jnp.sum(log_total - picked) / tokens_all
    loss_part = jnp.where(lax.axis_index("mp") == 0, local_loss, jnp.zeros((), f32))
    out_grads = jnp.dot(grad_rows, dec_matrix.T, preferred_element_type=f32).reshape(
        step_count, row_count, local_units
    )
    dec_bias_part = jnp.sum(grad_rows.astype(f32), axis=0)
    columns = flat_hidden
    dec_grad = lax.psum_scatter(
        lax.dot_general(columns, grad_rows, (((0,), (0,)), ((), ())), preferred_element_type=f32),
        "dp",
        scatter_dimension=0,
        tiled=True,
    ).reshape(decoder_weight.shape)
    prev_cells = (
        jnp.concatenate([jnp.zeros((1, row_count, local_units), f32), cells[:-1]], axis=0)
        * keep_mask[:, :, None]
    )

    def backward_step(state_pair, inputs):
        carry_hidden, carry_cell = state_pair
        preact, cell_state, prev_cell, hidden_out, keep_now = inputs
        gate_vals = preact.reshape(row_count, 4, local_units)
        in_gate = jax.nn.sigmoid(gate_vals[:, 0])
        forget_gate = jax.nn.sigmoid(gate_vals[:, 1])
        cell_gate = jnp.tanh(gate_vals[:, 2])
        out_gate = jax.nn.sigmoid(gate_vals[:, 3])
        hidden_grad = hidden_out + carry_hidden
        squash = jnp.tanh(cell_state)
        cell_grad = hidden_grad * out_gate * (1.0 - squash * squash) + carry_cell
        grad_in = cell_grad * cell_gate * in_gate * (1.0 - in_gate)
        grad_forget = cell_grad * prev_cell * forget_gate * (1.0 - forget_gate)
        grad_cand = cell_grad * in_gate * (1.0 - cell_gate * cell_gate)
        grad_out = hidden_grad * squash * out_gate * (1.0 - out_gate)
        preact_grad = (
            jnp.stack([grad_in, grad_forget, grad_cand, grad_out], axis=1)
            .reshape(row_count, gate_cols)
            .astype(bf16)
        )
        back_term = lax.dot_general(
            preact_grad, rec_matrix, (((1,), (1,)), ((), ())), preferred_element_type=f32
        )
        next_hidden = (
            lax.psum_scatter(back_term, "mp", scatter_dimension=1, tiled=True) * keep_now[:, None]
        )
        next_cell = cell_grad * forget_gate * keep_now[:, None]
        return ((next_hidden, next_cell), preact_grad)

    zero_rows = jnp.zeros((row_count, local_units), f32)
    _, preact_grads = lax.scan(
        backward_step,
        (zero_rows, zero_rows),
        (preacts, cells, prev_cells, out_grads, keep_mask),
        reverse=True,
    )
    flat_prev = prevs.reshape(tokens_here, hidden_total)
    flat_pgrad = preact_grads.reshape(tokens_here, gate_cols)
    columns = flat_prev
    rec_grad = lax.psum_scatter(
        lax.dot_general(columns, flat_pgrad, (((0,), (0,)), ((), ())), preferred_element_type=f32),
        "dp",
        scatter_dimension=0,
        tiled=True,
    ).reshape(recurrent_weight.shape)
    onehot_ids = (
        time_ids.reshape(tokens_here)[:, None] == jnp.arange(vocab_size, dtype=jnp.int32)[None, :]
    ).astype(bf16)
    table_part = lax.dot_general(
        onehot_ids, flat_pgrad, (((0,), (0,)), ((), ())), preferred_element_type=f32
    )
    table_sum, dec_bias_grad, loss_data = lax.psum((table_part, dec_bias_part, loss_part), "dp")
    in_grad = jnp.dot(embedding.astype(f32).T, table_sum, precision=highest).reshape(
        width_in, 4, local_units
    )
    bias_grad = jnp.sum(table_sum, axis=0).reshape(4, local_units)
    emb_part = lax.dot_general(
        table_sum,
        input_weight.reshape(width_in, gate_cols).astype(f32),
        (((1,), (1,)), ((), ())),
        precision=highest,
    )
    emb_grad, loss = lax.psum((emb_part, loss_data), "mp")
    return (loss, emb_grad, in_grad, rec_grad, bias_grad, dec_grad, dec_bias_grad)


def solution(mesh):
    in_specs = (
        P("dp", None),
        P("dp", None),
        P("dp", None),
        P(),
        P(None, None, "mp"),
        P("dp", None, "mp"),
        P(None, "mp"),
        P("mp", "dp", None, None),
        P(),
    )
    out_specs = (
        P(),
        P(),
        P(None, None, "mp"),
        P("dp", None, "mp"),
        P(None, "mp"),
        P("mp", "dp", None, None),
        P(),
    )
    fits = (mesh.shape["dp"], mesh.shape["mp"]) == (8, 4)
    return jax.shard_map(
        grouped if fits else on_device,
        mesh=mesh,
        in_specs=in_specs,
        out_specs=out_specs,
        check_vma=False,
    )
```

```python
import functools

import jax
import jax.numpy as jnp
from jax import lax
from jax.experimental import pallas as pl
from jax.experimental.pallas import tpu as pltpu
from jax.sharding import PartitionSpec as P

f32 = jnp.float32
bf16 = jnp.bfloat16
MESH = pl.DeviceIdType.MESH
LANES = 128
CHIPS = ((2, 0), (0, 2), (2, 2))
PEERS = ((0, 1), (2, 0), (0, 2), (2, 2), (2, 1), (0, 3), (2, 3), (1, 0), (4, 0), (5, 0), (6, 0))
GROUP = ((0, 1), (2, 0), (0, 2), (2, 2), (2, 1), (0, 3), (2, 3))
OTHERS = (1, 4, 5)
COLUMN = (4, 6, 2)
SPLIT = 2
PIECES = 8
LAG = 2
EARLY = 2
SUB = 4


def turn(value, flips):
    for bit in (1, 2, 4):
        if flips & bit:
            value = value + bit - 2 * bit * lax.rem(lax.div(value, bit), 2)
    return value


def dot(a, b):
    return jnp.dot(a, b, preferred_element_type=f32)


def dot_t(a, b):
    return lax.dot_general(a, b, (((1,), (1,)), ((), ())), preferred_element_type=f32)


def t_dot(a, b):
    return lax.dot_general(a, b, (((0,), (0,)), ((), ())), preferred_element_type=f32)


def layer_kernel(
    dims,
    chars_ref,
    nexts_ref,
    resets_ref,
    emb_ref,
    iw_ref,
    rec_ref,
    gb_ref,
    dec_ref,
    decb_ref,
    out_loss,
    out_emb,
    out_iw,
    out_rec,
    out_gb,
    out_dec,
    out_decb,
    rec_in,
    iw_in,
    ids_rows,
    ids_cols,
    rec_halves,
    weights,
    emb_pad,
    iw_pads,
    gb_pads,
    dec_pad,
    decb_pad,
    dec_all,
    hid,
    gates,
    cells,
    squashes,
    from_logits,
    onehots,
    embedded,
    keeps,
    targets,
    logit_grads,
    pgs,
    pgm,
    carry_c,
    pg_now,
    pg_out,
    pgm_out,
    pgm_now,
    own_sum,
    chip_out,
    chip_in,
    small_acc,
    small_pair,
    both,
    x_out,
    x_in,
    z_out,
    z_in,
    giw_acc,
    giw_out,
    giw_x_in,
    giw_z_out,
    giw_z_in,
    giw_full,
    emb_part,
    emb_in,
    emb_sums,
    emb_pairs,
    emb_full,
    dec_part,
    dec_x_out,
    dec_x_in,
    dec_z_out,
    dec_z_in,
    in_sem,
    ids_sem,
    wz_sem,
    wx_sem,
    wc_sem,
    iw_sem,
    decg_sem,
    decr_sem,
    hid_sem,
    hidc_sem,
    lg_sem,
    pg_sem,
    pgm_sem,
    small_sem,
    chip_sem,
    gx_sem,
    gz_sem,
    giw_sem,
    emb_sem,
    emb2_sem,
    emb3_sem,
    dsum_sem,
):
    steps, rows, units, vocab, vocab_pad, tokens_all, block = dims
    cols = 4 * units
    half = rows // 2
    part = half // SPLIT
    d, m = lax.axis_index("dp"), lax.axis_index("mp")
    x_at, z_low, z_high = lax.rem(d, 2), lax.rem(lax.div(d, 2), 2), lax.div(d, 4)
    z_at = lax.div(d, 2)
    core, y_at = lax.rem(m, 2), lax.div(m, 2)

    def device(flips):
        return (turn(d, flips[0]), turn(m, flips[1]))

    def slot(flips):
        return turn(z_low, flips[0] // 2) * 4 + turn(m, flips[1])

    def chip(flips):
        return pl.ds(turn(z_low, flips[0] // 2) * 4 + turn(y_at, flips[1] // 2) * 2, 2)

    own = slot((0, 0))

    def copy(src, dst, sems, at, flips):
        return pltpu.make_async_remote_copy(
            src_ref=src,
            dst_ref=dst,
            send_sem=sems.at[(0,) + at],
            recv_sem=sems.at[(1,) + at],
            device_id=device(flips),
            device_id_type=MESH,
        )

    sizes = [block // PIECES] * (PIECES - 1) + [block // PIECES // 2] * 2
    pieces = [(sum(sizes[:p]), size) for p, size in enumerate(sizes)]
    rec_loads = [
        pltpu.make_async_copy(
            rec_ref.at[pl.ds(first, size)], rec_in.at[pl.ds(first, size)], in_sem.at[p]
        )
        for p, (first, size) in enumerate(pieces)
    ]
    iw_load = pltpu.make_async_copy(iw_ref, iw_in, in_sem.at[PIECES + 1])
    for each in rec_loads + [iw_load]:
        each.start()

    barrier = pltpu.get_barrier_semaphore()
    for flips in PEERS:
        pl.semaphore_signal(barrier, inc=1, device_id=device(flips), device_id_type=MESH)
    pl.semaphore_wait(barrier, len(PEERS))


    def weight_rows(index, p):
        first, size = pieces[p]
        side, inside = first // LANES, first % LANES
        return weights.at[
            core,
            side * 4 + lax.div(index, 2),
            :,
            pl.ds(pl.multiple_of(lax.rem(index, 2) * LANES + inside, size), size),
        ]

    def weight_core(index, at, p):
        spot = weight_rows(index, p)
        return copy(spot, spot, wc_sem, (at, p), (0, 1))

    def block_of(at):
        return turn(d, (0, 4, 6, 2)[at % 4] + at // 4)

    def weight_z(k, p):
        flips = COLUMN[k]
        half = turn(z_low, (flips & 2) // 2)
        return copy(
            rec_halves.at[half, :, pl.ds(*pieces[p])], weight_rows(d, p), wz_sem, (k, p), (flips, 0)
        )

    def weight_z_in(k, p):
        spot = weight_rows(turn(d, COLUMN[k]), p)
        return copy(spot, spot, wz_sem, (k, p), (COLUMN[k], 0))

    def weight_x(k, p):
        if k == 3:
            return copy(
                rec_halves.at[z_low, :, pl.ds(*pieces[p])],
                weight_rows(d, p),
                wx_sem,
                (k, p),
                (1, 0),
            )
        spot = weight_rows(turn(d, COLUMN[k]), p)
        return copy(spot, spot, wx_sem, (k, p), (1, 0))

    def weight_x_in(k, p):
        flips = 0 if k == 3 else COLUMN[k]
        spot = weight_rows(turn(d, flips + 1), p)
        return copy(spot, spot, wx_sem, (k, p), (1, 0))

    runs = units // LANES
    width = iw_ref.shape[0]
    dec_rows = dec_ref.shape[0]
    vocab_rows = emb_pad.shape[0]

    def dec_spot(flips):
        at = turn(z_high, flips // 4) * LANES + turn(x_at, flips % 2) * dec_rows
        return dec_all.at[own, pl.ds(pl.multiple_of(at, dec_rows), dec_rows)]

    ids_rows[z_low, 0:steps] = chars_ref[...]
    ids_rows[z_low, 8 : 8 + steps] = nexts_ref[...]
    ids_rows[z_low, 16 : 16 + steps] = resets_ref[...]
    ids_copy = copy(ids_rows.at[z_low], ids_rows.at[z_low], ids_sem, (0,), (2, 0))
    ids_copy.start()

    def weight_start(p):
        for k in range(3):
            weight_z(k, p).start()
        weight_x(3, p).start()

    for p, (first, size) in enumerate(pieces):
        here = slice(first, first + size)
        rec_loads[p].wait()
        for gate in range(4):
            for run in range(runs):
                for side in range(2):
                    at = (run * 2 + side) * LANES
                    to = run * LANES
                    rec_halves[side, gate, here, to : to + LANES] = rec_in[here, gate, at : at + LANES]
        if p < EARLY:
            weight_start(p)
        if p == 0:
            dec_pad[...] = jnp.zeros_like(dec_pad)
            dec_pad[:, :vocab] = dec_ref[...]
            dec_z = copy(dec_pad, dec_spot(0), decg_sem, (0,), (4, 0))
            dec_z.start()
            dec_x = [copy(dec_pad, dec_spot(0), decg_sem, (1,), (1, 0))]
            dec_x[0].start()

    def weight_round(p):
        for k in range(3):
            weight_z_in(k, p).wait_recv()
            weight_x(k, p).start()
            weight_core(block_of(1 + k), 1 + k, p).start()
        if p >= LAG:
            weight_over_x(p - LAG)

    def weights_from_core(which):
        for p in which:
            for at in range(8):
                index = block_of(at)
                first, size = pieces[p]
                inside = first % LANES
                spot = weights.at[
                    1 - core,
                    first // LANES * 4 + lax.div(index, 2),
                    :,
                    pl.ds(pl.multiple_of(lax.rem(index, 2) * LANES + inside, size), size),
                ]
                copy(spot, spot, wc_sem, (at, p), (0, 1)).wait_recv()

    def weight_over_x(p):
        for k in (3, 0, 1, 2):
            weight_x_in(k, p).wait_recv()
            at = 4 if k == 3 else 5 + k
            weight_core(block_of(at), at, p).start()

    for p in range(PIECES + 1):
        weight_rows(d, p)[...] = rec_halves[z_low, :, pl.ds(*pieces[p])]
        weight_core(block_of(0), 0, p).start()
    dec_spot(0)[...] = dec_pad[...]
    emb_pad[...] = jnp.zeros_like(emb_pad)
    emb_pad[:vocab, :width] = emb_ref[...]
    ones_at = lax.broadcasted_iota(jnp.int32, emb_pad.shape, 1) == width
    emb_pad[...] = jnp.where(ones_at, 1.0, emb_pad[...].astype(f32)).astype(bf16)
    iw_pads[core] = jnp.zeros(iw_pads.shape[1:], bf16)
    iw_load.wait()

    def half_lanes(run):
        return pl.ds(pl.multiple_of((run * 2 + z_low) * LANES, LANES), LANES)

    for gate in range(4):
        for run in range(runs):
            to = gate * units + run * LANES
            iw_pads[core, :width, to : to + LANES] = iw_in[:, gate, half_lanes(run)]
            gb_pads[core, :, to : to + LANES] = gb_ref[gate : gate + 1, half_lanes(run)]
    iw_copies = [
        copy(ref.at[core], ref.at[core], iw_sem, (k,), (0, 1))
        for k, ref in enumerate((iw_pads, gb_pads))
    ]
    for each in iw_copies:
        each.start()
    decb_pad[...] = jnp.full(decb_pad.shape, -1e30, f32)
    decb_pad[0, :vocab] = decb_ref[...]
    ids_copy.wait_recv()
    ids_cols[...] = ids_rows[core].T
    vocab_iota = lax.broadcasted_iota(jnp.int32, (vocab_rows, rows), 0)

    def read_ids(t):
        now = jnp.concatenate([ids_rows[0, t : t + 1], ids_rows[1, t : t + 1]], axis=1)
        onehots[t] = (vocab_iota == now).astype(f32).astype(bf16)
        targets[t] = jnp.broadcast_to(ids_cols[:, 8 + t : 9 + t], (half, LANES))
        keeps[t] = jnp.broadcast_to((1 - ids_cols[:, 16 + t : 17 + t]).astype(f32), (half, LANES))

    def project(t):
        read_ids(t)
        chosen = t_dot(onehots[t], emb_pad[...]).astype(bf16)
        embedded[t] = chosen
        mine = embedded[t, pl.ds(pl.multiple_of(core * half, half), half)]
        for c in range(2):
            gates[t, c] = dot(mine, iw_pads[c]) + gb_pads[c]

    for k, ref in enumerate((iw_pads, gb_pads)):
        copy(ref.at[1 - core], ref.at[1 - core], iw_sem, (k,), (0, 1)).wait_recv()
    project(0)

    def span(s):
        return pl.ds(s * part, part)

    def wide(s):
        return pl.ds(pl.multiple_of(core * half + s * part, part), part)

    def hidden_copy(t, s, j):
        spot = hid.at[chip((0, 0)), t, wide(s)]
        return copy(spot, spot, hid_sem, (t, s, j), CHIPS[j])

    def hidden_in(t, s, j):
        spot = hid.at[chip(CHIPS[j]), t, wide(s)]
        return copy(spot, spot, hid_sem, (t, s, j), CHIPS[j])

    def hidden_core(t, s):
        spot = hid.at[:, t, wide(s)]
        return copy(spot, spot, hidc_sem, (t, s), (0, 1))

    def hidden_core_in(t, s):
        rows_there = pl.ds(pl.multiple_of((1 - core) * half + s * part, part), part)
        spot = hid.at[:, t, rows_there]
        return copy(spot, spot, hidc_sem, (t, s), (0, 1))

    def cell_step(t, s, added):
        here = span(s)
        if added is not None:
            keep = keeps[t, here, :1]
        for c in range(2):
            preact = [gates[t, c, here, k * units : (k + 1) * units] for k in range(4)]
            if added is not None:
                preact = [preact[k] + keep * added[c][k] for k in range(4)]
            in_gate = jax.nn.sigmoid(preact[0])
            forget = jax.nn.sigmoid(preact[1])
            candidate = jnp.tanh(preact[2])
            out_gate = jax.nn.sigmoid(preact[3])
            cell = in_gate * candidate
            if added is not None:
                cell = forget * keep * cells[t - 1, c, here] + cell
            cells[t, c, here] = cell
            squash = jnp.tanh(cell)
            hid[z_low * 4 + y_at * 2 + c, t, wide(s)] = (out_gate * squash).astype(bf16)
            squashes[t, c, here] = squash
            gates[t, c, here, :units] = in_gate
            gates[t, c, here, units : 2 * units] = forget
            gates[t, c, here, 2 * units : 3 * units] = candidate
            gates[t, c, here, 3 * units :] = out_gate
        for j in (2, 0, 1):
            hidden_copy(t, s, j).start()

    def add_slot(total, t, here, at):
        some = hid[at, t, here]
        for c in range(2):
            for gate in range(4):
                more = dot(some, weights[c, at, gate])
                total[c][gate] = more if total[c][gate] is None else total[c][gate] + more

    for s in range(SPLIT):
        cell_step(0, s, None)

    for p in range(EARLY, PIECES + 1):
        weight_start(p)
    weight_round(0)
    project(1)
    project(2)
    weight_round(1)
    spot = dec_spot(4)
    copy(spot, spot, decg_sem, (0,), (4, 0)).wait_recv()
    dec_x.append(copy(spot, spot, decg_sem, (2,), (1, 0)))
    dec_x[1].start()
    project(3)
    weight_round(2)
    project(4)
    project(5)
    weight_round(3)
    for j, flips in enumerate((1, 5)):
        spot = dec_spot(flips)
        copy(spot, spot, decg_sem, (1 + j,), (1, 0)).wait_recv()
    dec_own = dec_all.at[own]
    dec_sends = [
        copy(dec_own, dec_own, decr_sem, (j,), flips) for j, flips in enumerate(CHIPS + ((0, 1),))
    ]
    for each in dec_sends:
        each.start()
    weight_round(4)
    weight_round(5)
    weights_from_core(range(PIECES // 2))
    for s in range(SPLIT):
        for j in range(3):
            hidden_in(0, s, j).wait_recv()
    mine = pl.ds(pl.multiple_of(core * half, half), half)
    total = [[None] * 4, [None] * 4]
    for at in range(4):
        add_slot(total, 0, mine, at)
    for c in range(2):
        for gate in range(4):
            lanes = slice(gate * units, (gate + 1) * units)
            gates[1, c, :, lanes] += keeps[1, :, :1] * total[c][gate]
    for p in range(6, PIECES + 1):
        weight_round(p)
    for p in range(PIECES + 1 - LAG, PIECES + 1):
        weight_over_x(p)
    weights_from_core(range(PIECES // 2, PIECES + 1))

    def dec_relay(j):
        spot = dec_all.at[slot(CHIPS[j])]
        return copy(spot, spot, decr_sem, (4 + j,), (0, 1))

    def pass_decoder():
        for j in range(3):
            spot = dec_all.at[slot(CHIPS[j])]
            copy(spot, spot, decr_sem, (j,), CHIPS[j]).wait_recv()
            dec_relay(j).start()

    def weight_sent():
        for p in range(PIECES + 1):
            for at in range(8):
                weight_core(block_of(at), at, p).wait_send()
            for k in range(4):
                weight_x(k, p).wait_send()

    def add_chip(total, t, s, flips):
        first = turn(z_low, flips[0] // 2) * 4 + turn(y_at, flips[1] // 2) * 2
        for k in range(2):
            add_slot(total, t, wide(s), first + k)

    def gather_hidden(t, s):
        total = [[None] * 4, [None] * 4]
        add_chip(total, t, s, (0, 0))
        for j in range(3):
            hidden_in(t, s, j).wait_recv()
            add_chip(total, t, s, CHIPS[j])
        hidden_core(t, s).start()
        return total

    vocab_part = lax.broadcasted_iota(jnp.int32, (part, vocab_pad), 1)
    last_lane = lax.broadcasted_iota(jnp.int32, (1, vocab_pad), 1) == vocab_pad - 1
    small_acc[...] = jnp.zeros_like(small_acc)

    def lg_copy(t, s):
        spot = logit_grads.at[t, wide(s)]
        return copy(spot, spot, lg_sem, (t, s), (0, 1))

    def decode(t, s):
        here = span(s)
        logits = decb_pad[...]
        for at in range(8):
            logits = logits + dot(hid[at, t, wide(s)], dec_all[at])
        top = jnp.max(logits, axis=1, keepdims=True)
        exps = jnp.exp(logits - top)
        total = jnp.sum(exps, axis=1, keepdims=True)
        hot = targets[t, here, :1] == vocab_part
        picked = jnp.sum(jnp.where(hot, logits, 0.0), axis=1, keepdims=True)
        lost = top + jnp.log(total) - picked
        grad = ((exps / total - jnp.where(hot, 1.0, 0.0)) / tokens_all).astype(bf16)
        logit_grads[t, wide(s)] = grad
        lg_copy(t, s).start()
        for c in range(2):
            from_logits[t, c, here] = dot_t(grad, dec_all[z_low * 4 + y_at * 2 + c])
        small_acc[...] += jnp.sum(grad.astype(f32), axis=0, keepdims=True) + jnp.where(
            last_lane, jnp.sum(lost, axis=0, keepdims=True) / tokens_all, 0.0
        )

    def forward(t, _):
        for s in range(SPLIT):
            cell_step(t, s, gather_hidden(t - 1, s))
            decode(t - 1, s)
        return 0

    @pl.when(core == 1)
    def _():
        pass_decoder()

    total = [[None] * 4, [None] * 4]
    for at in range(4, 8):
        add_slot(total, 0, mine, at)
    for s in range(SPLIT):
        here = slice(s * part, (s + 1) * part)
        cell_step(1, s, [[more[here] for more in total[c]] for c in range(2)])
        hidden_core(0, s).start()

    @pl.when(core == 0)
    def _():
        pass_decoder()

    spot = dec_all.at[slot((0, 1))]
    copy(spot, spot, decr_sem, (3,), (0, 1)).wait_recv()
    for j in range(3):
        spot = dec_all.at[slot((CHIPS[j][0], CHIPS[j][1] + 1))]
        copy(spot, spot, decr_sem, (4 + j,), (0, 1)).wait_recv()
    for s in range(SPLIT):
        decode(0, s)
    lax.fori_loop(2, steps, forward, 0)

    def pg_copy(t, s):
        return copy(pg_out.at[t, span(s)], pgs.at[t, wide(s)], pg_sem, (t, s), (0, 1))

    def pgm_copy(t, s):
        return copy(
            pgm_out.at[t - 1, span(s)], pgm.at[t - 1, wide(s)], pgm_sem, (t - 1, s), (0, 1)
        )

    def cell_back(t, s, carried, first):
        here = span(s)
        if not first:
            keep = keeps[t, here, :1]
        for c in range(2):
            hidden_grad = from_logits[t, c, here]
            if carried is not None:
                hidden_grad = hidden_grad + carried[:, c * units : (c + 1) * units]
            in_gate = gates[t, c, here, :units]
            forget = gates[t, c, here, units : 2 * units]
            candidate = gates[t, c, here, 2 * units : 3 * units]
            out_gate = gates[t, c, here, 3 * units :]
            squash = squashes[t, c, here]
            cell_grad = hidden_grad * out_gate * (1.0 - squash * squash)
            if carried is not None:
                cell_grad = cell_grad + carry_c[c, here]
            grads = [
                cell_grad * candidate * in_gate * (1.0 - in_gate),
                None,
                cell_grad * in_gate * (1.0 - candidate * candidate),
                hidden_grad * squash * out_gate * (1.0 - out_gate),
            ]
            if first:
                grads[1] = jnp.zeros_like(cell_grad)
            else:
                grads[1] = cell_grad * (keep * cells[t - 1, c, here]) * forget * (1.0 - forget)
                carry_c[c, here] = keep * forget * cell_grad
            for k in range(4):
                pg_now[c, here, k * units : (k + 1) * units] = grads[k].astype(bf16)
                if not first:
                    pgm_now[c, here, k * units : (k + 1) * units] = (keep * grads[k]).astype(bf16)

    def share(t, s, first):
        here = span(s)
        pgs[t, wide(s)] = pg_now[core, here]
        pg_out[t, here] = pg_now[1 - core, here]
        if not first:
            pgm[t - 1, wide(s)] = pgm_now[core, here]
            pgm_out[t - 1, here] = pgm_now[1 - core, here]
            pgm_copy(t, s).start()
        pg_copy(t, s).start()

    def chip_copy(t, s, j):
        return copy(
            chip_out.at[t - 1, s, j], chip_in.at[t - 1, s, j], chip_sem, (t - 1, s, j), CHIPS[j]
        )

    def spread(t, s):
        here = span(s)
        for j in (2, 0, 1, 3):
            flips = CHIPS[j] if j < 3 else (0, 0)
            first = turn(z_low, flips[0] // 2) * 4 + turn(y_at, flips[1] // 2) * 2
            for k in range(2):
                part_sum = None
                for c in range(2):
                    for gate in range(4):
                        grad = pgm_now[c, here, gate * units : (gate + 1) * units]
                        more = dot(grad, weights[c, first + k, gate])
                        part_sum = more if part_sum is None else part_sum + more
                lanes = slice(k * units, (k + 1) * units)
                if j < 3:
                    chip_out[t - 1, s, j, :, lanes] = part_sum.astype(bf16)
                else:
                    own_sum[s, :, lanes] = part_sum
            if j < 3:
                chip_copy(t, s, j).start()

    def carried_in(t, s):
        total = own_sum[s]
        for j in range(3):
            chip_copy(t + 1, s, j).wait_recv()
            total = total + chip_in[t, s, j].astype(f32)
        return total

    last = steps - 1

    weight_sent()

    def turn_over(at, _):
        for c in range(2):
            for gate in range(4):
                weights[c, at, gate] = weights[c, at, gate].T
        return 0

    lax.fori_loop(0, 8, turn_over, 0)
    for s in range(SPLIT):
        for j in range(3):
            hidden_in(last, s, j).wait_recv()
        hidden_core(last, s).start()
        decode(last, s)
        cell_back(last, s, None, False)
        spread(last, s)
        share(last, s, False)

    def other_rows(s):
        return pl.ds(pl.multiple_of((1 - core) * half + s * part, part), part)

    def dsum_x():
        return copy(dec_x_out, dec_x_in, dsum_sem, (0,), (1, 0))

    def dsum_z(k):
        return copy(dec_z_out, dec_z_in, dsum_sem, (k,), (4, 0))

    def small_copy():
        return copy(small_pair.at[core], small_pair.at[core], small_sem, (0,), (0, 1))

    def decoder_grad():
        for t in range(steps):
            for s in range(SPLIT):
                hidden_core_in(t, s).wait_recv()
                spot = logit_grads.at[t, other_rows(s)]
                copy(spot, spot, lg_sem, (t, s), (0, 1)).wait_recv()
        small_pair[core] = small_acc[...]
        small_copy().start()
        dec_part[...] = t_dot(
            hid[own].reshape(steps * rows, units),
            logit_grads[...].reshape(steps * rows, vocab_pad),
        ).reshape(2, 2, dec_rows, vocab_pad)
        for k in range(2):
            dec_x_out[k] = dec_part[k, 1 - x_at].astype(bf16)
        dsum_x().start()

    def decoder_grad_z():
        dsum_x().wait_recv()
        dec_z_out[...] = (
            dec_part[1 - z_high, x_at] + dec_x_in[1 - z_high].astype(f32)
        ).astype(bf16)
        dsum_z(1).start()

    def backward(i, _):
        t = last - i
        for s in range(SPLIT):
            cell_back(t, s, carried_in(t, s), False)
            spread(t, s)
            share(t, s, False)

        @pl.when(i == 2)
        def _():
            decoder_grad()

        @pl.when(i == 3)
        def _():
            decoder_grad_z()

        return 0

    lax.fori_loop(1, last - 1, backward, 0)
    for s in range(SPLIT):
        cell_back(1, s, carried_in(1, s), False)
        share(1, s, False)

    acc = gates.at[pl.ds(steps - 4, 4)]

    far = (2, 3, 1, 0)

    piece_rows = LANES // SUB

    def x_copy(k, side, sub):
        here = pl.ds(sub * piece_rows, piece_rows)
        return copy(
            x_out.at[k, side, here], x_in.at[k, side, here], gx_sem, (k, side, sub), (1, 0)
        )

    def z_copy(k, side, sub):
        here = pl.ds(sub * piece_rows, piece_rows)
        return copy(
            z_out.at[k, side, here], z_in.at[k, side, here], gz_sem, (k, side, sub), (far[k] * 2, 0)
        )

    used = (steps - 1) * rows

    def from_core(t, _):
        for s in range(SPLIT):
            spot = pgs.at[t, other_rows(s)]
            copy(spot, spot, pg_sem, (t, s), (0, 1)).wait_recv()
            spot = pgm.at[t - 1, other_rows(s)]
            copy(spot, spot, pgm_sem, (t - 1, s), (0, 1)).wait_recv()
        return 0

    lax.fori_loop(1, steps, from_core, 0)

    def weight_grad(k, side):
        at = side * 4 + turn(z_at, far[k])
        both[...] = t_dot(
            hid[at, 0 : steps - 1].reshape(used, units), pgm[...].reshape(used, cols)
        ).reshape(2, LANES, cols)
        x_out[k, side] = both[1 - x_at].astype(bf16)
        acc[k, side] = both[x_at]

    def weight_grad_first(side):
        at = side * 4 + turn(z_at, far[0])
        for k in (1, 0):
            lanes = pl.ds(pl.multiple_of((x_at if k == 0 else 1 - x_at) * LANES, LANES), LANES)
            some = t_dot(
                hid[at, 0 : steps - 1, :, lanes].reshape(used, LANES),
                pgm[...].reshape(used, cols),
            )
            if k:
                x_out[0, side] = some.astype(bf16)
                send_eighth(2 * side, 2 * side + 1)
            else:
                acc[0, side] = some

    order = [(k, side, sub) for k in range(4) for side in range(2) for sub in range(SUB)]

    def send_eighth(*which):
        for at in which:
            for k in range(SUB // 2):
                x_copy(*order[at * (SUB // 2) + k]).start()

    def pass_z(at):
        for k in range(SUB // 2):
            pass_piece(at * (SUB // 2) + k)

    def pass_piece(at):
        k, side, sub = order[at]
        here = pl.ds(sub * piece_rows, piece_rows)
        x_copy(k, side, sub).wait_recv()
        total = acc[k, side, here] + x_in[k, side, here].astype(f32)
        if k == 3:
            acc[k, side, here] = total
            return
        z_out[k, side, here] = total.astype(bf16)
        if at in range(3, 4 * SUB):
            z_copy(*order[at - 3]).wait_send()
        z_copy(k, side, sub).start()

    def scatter(here, side, gate, value):
        for run in range(runs):
            at = pl.multiple_of((run * 2 + side) * LANES, LANES)
            out_rec[here, gate, pl.ds(at, LANES)] = value[:, run * LANES : (run + 1) * LANES]

    def finish(at):
        pass_z(12 + at)
        for which in range(at * (SUB // 2), (at + 1) * (SUB // 2)):
            side, sub = divmod(which, SUB)
            for k in range(3):
                z_copy(k, side, sub).wait_recv()
            here = pl.ds(side * LANES + sub * piece_rows, piece_rows)
            mine = pl.ds(sub * piece_rows, piece_rows)
            for gate in range(4):
                lanes = slice(gate * units, (gate + 1) * units)
                value = acc[3, side, mine, lanes] + z_in[0, side, mine, lanes].astype(f32)
                scatter(here, z_low, gate, value)
                value = z_in[1, side, mine, lanes].astype(f32) + z_in[2, side, mine, lanes].astype(
                    f32
                )
                scatter(here, 1 - z_low, gate, value)

    weight_grad_first(0)
    weight_grad(0, 1)
    send_eighth(2, 3)
    for s in range(SPLIT):
        spread(1, s)
    pass_piece(0)
    pass_piece(1)
    weight_grad(1, 0)
    pass_piece(2)
    weight_grad(2, 0)
    pass_piece(3)

    for s in range(SPLIT):
        cell_back(0, s, carried_in(0, s), True)
        share(0, s, True)
    for s in range(SPLIT):
        spot = pgs.at[0, other_rows(s)]
        copy(spot, spot, pg_sem, (0, s), (0, 1)).wait_recv()
    tokens = steps * rows
    giw_rows = giw_acc.shape[0]
    giw_acc[...] = t_dot(
        embedded[...].reshape(tokens, LANES), pgs[...].reshape(tokens, cols)
    )[:giw_rows]
    for k in range(2):
        at = pl.multiple_of((1 - x_at) * (2 * units) + k * units, units)
        giw_out[k] = giw_acc[:, pl.ds(at, units)].astype(bf16)
    giw_x = copy(giw_out, giw_x_in, giw_sem, (0,), (1, 0))
    giw_x.start()
    send_eighth(4, 8)
    pass_piece(4)

    emb_rows = emb_full.shape[1]
    by_char = jnp.zeros((vocab_rows, 2 * LANES), f32)
    for t in range(steps):
        by_token = dot_t(pgs[t], iw_pads[core])
        high = by_token.astype(bf16)
        low = (by_token - high.astype(f32)).astype(bf16)
        by_char = by_char + dot(onehots[t], jnp.concatenate([high, low], axis=1))
    emb_part[...] = (by_char[:, :LANES] + by_char[:, LANES:]).reshape(8, emb_rows, LANES)
    emb_copies = [
        copy(emb_part.at[slot(flips)], emb_in.at[own], emb_sem, (j,), flips)
        for j, flips in enumerate(GROUP)
    ]
    for each in emb_copies:
        each.start()
    emb_in[own] = emb_part[own]
    pass_piece(5)
    weight_grad(1, 1)

    giw_x.wait_recv()
    for k in range(2):
        at = pl.multiple_of(x_at * (2 * units) + k * units, units)
        giw_acc[:, pl.ds(at, units)] += giw_x_in[k].astype(f32)
    giw_z_out[...] = giw_acc[
        :, pl.ds(pl.multiple_of(x_at * (2 * units) + (1 - z_high) * units, units), units)
    ].astype(bf16)
    giw_z = copy(giw_z_out, giw_z_in, giw_sem, (1,), (4, 0))
    giw_z.start()
    send_eighth(5, 9)
    pass_piece(6)
    for j, flips in enumerate(GROUP):
        spot = emb_in.at[slot(flips)]
        copy(spot, spot, emb_sem, (j,), flips).wait_recv()
    total = emb_in[0]
    for at in range(1, 8):
        total = total + emb_in[at]

    def place(flips):
        return turn(z_high, flips // 4) * 2 + turn(x_at, flips % 2)

    emb_sums[place(0), :emb_rows] = total
    spot = small_pair.at[1 - core]
    copy(spot, spot, small_sem, (0,), (0, 1)).wait_recv()
    smalls = small_pair[0] + small_pair[1]
    for k in range(vocab_pad // LANES):
        emb_sums[place(0), emb_rows + k : emb_rows + k + 1] = smalls[
            :, k * LANES : (k + 1) * LANES
        ]
    spot = emb_sums.at[place(0)]
    emb2 = [copy(spot, spot, emb2_sem, (0,), (1, 0))]
    emb2[0].start()
    weight_grad(2, 1)
    pass_piece(7)
    send_eighth(6, 10)
    weight_grad(3, 0)
    weight_grad(3, 1)

    spot = emb_sums.at[place(1)]
    copy(spot, spot, emb2_sem, (0,), (1, 0)).wait_recv()
    emb_pairs[z_high] = emb_sums[z_high * 2] + emb_sums[z_high * 2 + 1]
    spot = emb_pairs.at[z_high]
    emb2.append(copy(spot, spot, emb2_sem, (1,), (4, 0)))
    emb2[1].start()

    giw_z.wait_recv()
    gate_at = x_at * 2 + z_high
    giw_full[z_low, gate_at] = (
        giw_acc[:, pl.ds(pl.multiple_of(gate_at * units, units), units)] + giw_z_in[...].astype(f32)
    ).astype(bf16)
    spot = giw_full.at[z_low, gate_at]
    giw_back_z = copy(spot, spot, giw_sem, (2,), (4, 0))
    giw_back_z.start()

    giw_turn = (gate_at, x_at * 2 + 1 - z_high, (1 - x_at) * 2, (1 - x_at) * 2 + 1)

    def giw_side(k, half_at):
        spot = giw_full.at[half_at, giw_turn[k]]
        return copy(spot, spot, giw_sem, (4 + k,), (2, 0))

    giw_side(0, z_low).start()
    pass_piece(8)
    send_eighth(7, 11)
    pass_piece(9)
    pass_z(8)
    spot = emb_pairs.at[1 - z_high]
    copy(spot, spot, emb2_sem, (1,), (4, 0)).wait_recv()
    sums = emb_pairs[0] + emb_pairs[1]
    emb_full[own] = sums[:emb_rows]
    spot = emb_full.at[own]
    emb3 = [copy(spot, spot, emb3_sem, (j,), flips) for j, flips in enumerate(GROUP)]
    for each in emb3:
        each.start()
    for k in range(vocab_pad // LANES):
        lanes = slice(k * LANES, min(vocab, (k + 1) * LANES))
        out_decb[:, lanes] = sums[emb_rows + k : emb_rows + k + 1, : lanes.stop - lanes.start]
    k = vocab_pad // LANES - 1
    out_loss[...] = sums[emb_rows + k : emb_rows + k + 1, LANES - 1 :]
    spot = giw_full.at[z_low, x_at * 2 + 1 - z_high]
    copy(spot, spot, giw_sem, (2,), (4, 0)).wait_recv()
    giw_side(1, z_low).start()
    spot = giw_full.at[z_low, pl.ds(x_at * 2, 2)]
    giw_back_x = copy(spot, spot, giw_sem, (3,), (1, 0))
    giw_back_x.start()
    send_eighth(12, 13, 14, 15)
    pass_piece(10)
    pass_z(9)
    pass_piece(11)
    spot = giw_full.at[z_low, pl.ds((1 - x_at) * 2, 2)]
    copy(spot, spot, giw_sem, (3,), (1, 0)).wait_recv()
    giw_side(2, z_low).start()
    pass_piece(12)
    pass_z(10)
    dsum_z(1).wait_recv()
    total = dec_part[z_high, x_at] + dec_x_in[z_high].astype(f32) + dec_z_in[...].astype(f32)
    out_dec[...] = total[:, :vocab]
    pass_piece(13)
    pass_z(11)
    for j, flips in enumerate(GROUP):
        spot = emb_full.at[slot(flips)]
        copy(spot, spot, emb3_sem, (j,), flips).wait_recv()
    out_emb[...] = emb_full[...].reshape(vocab_rows, LANES)[:vocab, :width]
    finish(0)
    giw_side(3, z_low).start()
    pass_piece(14)
    ids_copy.wait_send()
    dec_z.wait_send()
    for each in dec_x + dec_sends + [dec_relay(j) for j in range(3)] + iw_copies + [small_copy(), dsum_x(), dsum_z(1)]:
        each.wait_send()
    for p in range(PIECES + 1):
        for k in range(3):
            weight_z(k, p).wait_send()

    def sent(t, _):
        for s in range(SPLIT):
            for j in range(3):
                hidden_copy(t, s, j).wait_send()
            hidden_core(t, s).wait_send()
            lg_copy(t, s).wait_send()
            pg_copy(t, s).wait_send()
        return 0

    lax.fori_loop(0, steps, sent, 0)

    def sent_back(t, _):
        for s in range(SPLIT):
            pgm_copy(t, s).wait_send()
            for j in range(3):
                chip_copy(t, s, j).wait_send()
        return 0

    lax.fori_loop(1, steps, sent_back, 0)
    finish(1)
    pass_piece(15)
    finish(2)
    finish(3)
    for k in range(4):
        giw_side(k, 1 - z_low).wait_recv()
    for side in range(2):
        for gate in range(4):
            value = giw_full[side, gate].astype(f32)
            for run in range(runs):
                to = slice((run * 2 + side) * LANES, (run * 2 + side + 1) * LANES)
                lanes = slice(run * LANES, (run + 1) * LANES)
                out_iw[:, gate, to] = value[:width, lanes]
                out_gb[gate : gate + 1, to] = value[width : width + 1, lanes]

    for each in [giw_x, giw_z, giw_back_z, giw_back_x]:
        each.wait_send()
    for k in range(4):
        giw_side(k, z_low).wait_send()
    for each in emb_copies + emb2 + emb3:
        each.wait_send()
    for at, spot in enumerate(order):
        x_copy(*spot).wait_send()
        if spot[0] < 3 and at not in range(4 * SUB - 3):
            z_copy(*spot).wait_send()


def hand_over(*refs):
    sources, places, flat, sems = list(refs[:7]), refs[7:14], refs[14], refs[15]
    flat[...] = sources[6][...].reshape(flat.shape)
    sources[6] = flat
    copies = [
        pltpu.make_async_copy(src, dst, sems.at[k])
        for k, (src, dst) in enumerate(zip(sources, places))
    ]
    for each in copies:
        each.start()
    for each in copies:
        each.wait()


def grouped(
    char_ids,
    next_chars,
    resets,
    embedding,
    input_weight,
    recurrent_weight,
    gate_bias,
    decoder_weight,
    decoder_bias,
):
    data_count = lax.axis_size("dp")
    row_count, steps = char_ids.shape
    vocab, width = embedding.shape
    local_units = input_weight.shape[2]
    block = recurrent_weight.shape[0]
    units = local_units // 2
    cols = 4 * units
    rows = 2 * row_count
    dec_rows = decoder_weight.shape[2]
    vocab_pad = pl.cdiv(vocab, LANES) * LANES
    tokens_all = row_count * steps * data_count
    half = rows // 2
    part = half // SPLIT
    emb_rows = pl.cdiv(vocab, 64) * 8
    giw_rows = pl.cdiv(width + 1, 16) * 16

    vocab_rows = 8 * emb_rows
    by_gate = recurrent_weight.transpose(1, 0, 2)
    in_by_gate = input_weight.transpose(1, 0, 2)
    dec = decoder_weight.reshape(dec_rows, vocab)

    vmem = pl.BlockSpec(memory_space=pltpu.VMEM)
    anywhere = pl.BlockSpec(memory_space=pl.ANY)
    dims = (steps, rows, units, vocab, vocab_pad, tokens_all, block)

    def sems(*shape):
        return pltpu.SemaphoreType.DMA((2,) + shape)

    loss, emb_grad, in_grad, rec_grad, bias_grad, dec_grad, dec_bias_grad = pl.pallas_call(
        functools.partial(layer_kernel, dims),
        out_shape=[
            pltpu.VMEM((1, 1), f32),
            pltpu.VMEM((vocab, width), f32),
            pltpu.VMEM((width, 4, local_units), f32),
            pltpu.VMEM((block, 4, local_units), f32),
            pltpu.VMEM((4, local_units), f32),
            pltpu.VMEM((dec_rows, vocab), f32),
            pltpu.VMEM((1, vocab), f32),
        ],
        in_specs=[vmem] * 4 + [anywhere] * 2 + [vmem] * 3,
        out_specs=[vmem] * 7,
        scratch_shapes=[
            pltpu.VMEM((block, 4, local_units), bf16),
            pltpu.VMEM((width, 4, local_units), bf16),
            pltpu.VMEM((2, LANES, row_count), jnp.int32),
            pltpu.VMEM((row_count, LANES), jnp.int32),
            pltpu.VMEM((2, 4, block, units), bf16),
            pltpu.VMEM((2, 8, 4, units, units), bf16),
            pltpu.VMEM((vocab_rows, LANES), bf16),
            pltpu.VMEM((2, LANES, cols), bf16),
            pltpu.VMEM((2, 1, cols), f32),
            pltpu.VMEM((dec_rows, vocab_pad), bf16),
            pltpu.VMEM((1, vocab_pad), f32),
            pltpu.VMEM((8, units, vocab_pad), bf16),
            pltpu.VMEM((8, steps, rows, units), bf16),
            pltpu.VMEM((steps, 2, half, cols), f32),
            pltpu.VMEM((steps, 2, half, units), f32),
            pltpu.VMEM((steps, 2, half, units), f32),
            pltpu.VMEM((steps, 2, half, units), f32),
            pltpu.VMEM((steps, vocab_rows, rows), bf16),
            pltpu.VMEM((steps, rows, LANES), bf16),
            pltpu.VMEM((steps, half, LANES), f32),
            pltpu.VMEM((steps, half, LANES), jnp.int32),
            pltpu.VMEM((steps, rows, vocab_pad), bf16),
            pltpu.VMEM((steps, rows, cols), bf16),
            pltpu.VMEM((steps - 1, rows, cols), bf16),
            pltpu.VMEM((2, half, units), f32),
            pltpu.VMEM((2, half, cols), bf16),
            pltpu.VMEM((steps, half, cols), bf16),
            pltpu.VMEM((steps - 1, half, cols), bf16),
            pltpu.VMEM((2, half, cols), bf16),
            pltpu.VMEM((SPLIT, part, 2 * units), f32),
            pltpu.VMEM((steps - 1, SPLIT, 3, part, 2 * units), bf16),
            pltpu.VMEM((steps - 1, SPLIT, 3, part, 2 * units), bf16),
            pltpu.VMEM((1, vocab_pad), f32),
            pltpu.VMEM((2, 1, vocab_pad), f32),
            pltpu.VMEM((2, LANES, cols), f32),
            pltpu.VMEM((4, 2, LANES, cols), bf16),
            pltpu.VMEM((4, 2, LANES, cols), bf16),
            pltpu.VMEM((3, 2, LANES, cols), bf16),
            pltpu.VMEM((3, 2, LANES, cols), bf16),
            pltpu.VMEM((giw_rows, cols), f32),
            pltpu.VMEM((2, giw_rows, units), bf16),
            pltpu.VMEM((2, giw_rows, units), bf16),
            pltpu.VMEM((giw_rows, units), bf16),
            pltpu.VMEM((giw_rows, units), bf16),
            pltpu.VMEM((2, 4, giw_rows, units), bf16),
            pltpu.VMEM((8, emb_rows, LANES), f32),
            pltpu.VMEM((8, emb_rows, LANES), f32),
            pltpu.VMEM((4, emb_rows + 8, LANES), f32),
            pltpu.VMEM((2, emb_rows + 8, LANES), f32),
            pltpu.VMEM((8, emb_rows, LANES), f32),
            pltpu.VMEM((2, 2, dec_rows, vocab_pad), f32),
            pltpu.VMEM((2, dec_rows, vocab_pad), bf16),
            pltpu.VMEM((2, dec_rows, vocab_pad), bf16),
            pltpu.VMEM((dec_rows, vocab_pad), bf16),
            pltpu.VMEM((dec_rows, vocab_pad), bf16),
            pltpu.SemaphoreType.DMA((PIECES + 2,)),
            sems(1),
            sems(3, PIECES + 1),
            sems(4, PIECES + 1),
            sems(8, PIECES + 1),
            sems(2),
            sems(3),
            sems(7),
            sems(steps, SPLIT, 3),
            sems(steps, SPLIT),
            sems(steps, SPLIT),
            sems(steps, SPLIT),
            sems(steps - 1, SPLIT),
            sems(1),
            sems(steps - 1, SPLIT, 3),
            sems(4, 2, SUB),
            sems(3, 2, SUB),
            sems(8),
            sems(7),
            sems(2),
            sems(7),
            sems(2),
        ],
        compiler_params=pltpu.CompilerParams(
            collective_id=0, has_side_effects=True, vmem_limit_bytes=60 << 20
        ),
    )(
        char_ids.T,
        next_chars.T,
        resets.T,
        embedding,
        input_weight,
        recurrent_weight,
        gate_bias,
        dec,
        decoder_bias,
    )
    results = [loss, emb_grad, in_grad, rec_grad, bias_grad, dec_grad, dec_bias_grad]
    results = [pltpu.with_memory_space_constraint(each, pltpu.VMEM) for each in results]
    loss, emb_grad, in_grad, rec_grad, bias_grad, dec_grad, dec_bias_grad = pl.pallas_call(
        hand_over,
        out_shape=[jax.ShapeDtypeStruct(each.shape, f32) for each in results[:-1]]
        + [jax.ShapeDtypeStruct((vocab,), f32)],
        in_specs=[vmem] * 7,
        out_specs=[anywhere] * 7,
        scratch_shapes=[pltpu.VMEM((vocab,), f32), pltpu.SemaphoreType.DMA((7,))],
        compiler_params=pltpu.CompilerParams(vmem_limit_bytes=2 << 20),
    )(*results)
    return (
        loss.reshape(()),
        emb_grad,
        in_grad,
        rec_grad,
        bias_grad,
        dec_grad.reshape(decoder_weight.shape),
        dec_bias_grad,
    )


def on_device(
    char_ids,
    next_chars,
    resets,
    embedding,
    input_weight,
    recurrent_weight,
    gate_bias,
    decoder_weight,
    decoder_bias,
):
    highest = lax.Precision.HIGHEST
    data_count = lax.axis_size("dp")
    row_count, step_count = char_ids.shape
    vocab_size, width_in = embedding.shape
    local_units = input_weight.shape[2]
    gate_cols = 4 * local_units
    tokens_here = row_count * step_count
    tokens_all = tokens_here * data_count
    gathered_rec, gathered_dec = (
        lax.all_gather(recurrent_weight, "dp", axis=0, tiled=True),
        lax.all_gather(decoder_weight, "dp", axis=1, tiled=True),
    )
    hidden_total = gathered_rec.shape[0]
    rec_matrix = gathered_rec.reshape(hidden_total, gate_cols)
    dec_matrix = gathered_dec.reshape(local_units, vocab_size)
    time_ids = char_ids.T
    keep_mask = (1 - resets.T).astype(f32)
    proj_table = jnp.dot(
        embedding, input_weight.reshape(width_in, gate_cols), preferred_element_type=f32
    )
    projected = jnp.take(proj_table, time_ids, axis=0) + gate_bias.reshape(gate_cols)

    def forward_step(state_pair, inputs):
        hidden_loc, cell_state = state_pair
        proj_now, keep_now = inputs
        hidden_full = lax.all_gather(hidden_loc, "mp", axis=1, tiled=True)
        previous = hidden_full * keep_now[:, None].astype(bf16)
        preact = proj_now + jnp.dot(previous, rec_matrix, preferred_element_type=f32)
        gate_vals = preact.reshape(row_count, 4, local_units)
        in_gate = jax.nn.sigmoid(gate_vals[:, 0])
        forget_gate = jax.nn.sigmoid(gate_vals[:, 1])
        cell_gate = jnp.tanh(gate_vals[:, 2])
        out_gate = jax.nn.sigmoid(gate_vals[:, 3])
        new_cell = forget_gate * cell_state * keep_now[:, None] + in_gate * cell_gate
        new_hidden = (out_gate * jnp.tanh(new_cell)).astype(bf16)
        return ((new_hidden, new_cell), (previous, preact, new_cell, new_hidden))

    first_state = (
        jnp.zeros((row_count, local_units), bf16),
        jnp.zeros((row_count, local_units), f32),
    )
    _, (prevs, preacts, cells, hiddens) = lax.scan(
        forward_step, first_state, (projected, keep_mask)
    )
    flat_hidden = hiddens.reshape(tokens_here, local_units)
    partial_value = jnp.dot(flat_hidden, dec_matrix, preferred_element_type=f32)
    flat_targets = next_chars.T.reshape(tokens_here)
    logit_rows = lax.psum(partial_value, "mp")
    shifted_in = logit_rows + decoder_bias
    row_max = jnp.max(shifted_in, axis=1)
    exp_total = jnp.sum(jnp.exp(shifted_in - row_max[:, None]), axis=1)
    log_total = row_max + jnp.log(exp_total)
    softmax_out = jnp.exp(shifted_in - log_total[:, None])
    onehot = (flat_targets[:, None] == jnp.arange(vocab_size, dtype=jnp.int32)[None, :]).astype(f32)
    picked = jnp.sum(shifted_in * onehot, axis=1)
    grad_rows = ((softmax_out - onehot) / tokens_all).astype(bf16)
    local_loss = jnp.sum(log_total - picked) / tokens_all
    loss_part = jnp.where(lax.axis_index("mp") == 0, local_loss, jnp.zeros((), f32))
    out_grads = jnp.dot(grad_rows, dec_matrix.T, preferred_element_type=f32).reshape(
        step_count, row_count, local_units
    )
    dec_bias_part = jnp.sum(grad_rows.astype(f32), axis=0)
    columns = flat_hidden
    dec_grad = lax.psum_scatter(
        lax.dot_general(columns, grad_rows, (((0,), (0,)), ((), ())), preferred_element_type=f32),
        "dp",
        scatter_dimension=0,
        tiled=True,
    ).reshape(decoder_weight.shape)
    prev_cells = (
        jnp.concatenate([jnp.zeros((1, row_count, local_units), f32), cells[:-1]], axis=0)
        * keep_mask[:, :, None]
    )

    def backward_step(state_pair, inputs):
        carry_hidden, carry_cell = state_pair
        preact, cell_state, prev_cell, hidden_out, keep_now = inputs
        gate_vals = preact.reshape(row_count, 4, local_units)
        in_gate = jax.nn.sigmoid(gate_vals[:, 0])
        forget_gate = jax.nn.sigmoid(gate_vals[:, 1])
        cell_gate = jnp.tanh(gate_vals[:, 2])
        out_gate = jax.nn.sigmoid(gate_vals[:, 3])
        hidden_grad = hidden_out + carry_hidden
        squash = jnp.tanh(cell_state)
        cell_grad = hidden_grad * out_gate * (1.0 - squash * squash) + carry_cell
        grad_in = cell_grad * cell_gate * in_gate * (1.0 - in_gate)
        grad_forget = cell_grad * prev_cell * forget_gate * (1.0 - forget_gate)
        grad_cand = cell_grad * in_gate * (1.0 - cell_gate * cell_gate)
        grad_out = hidden_grad * squash * out_gate * (1.0 - out_gate)
        preact_grad = (
            jnp.stack([grad_in, grad_forget, grad_cand, grad_out], axis=1)
            .reshape(row_count, gate_cols)
            .astype(bf16)
        )
        back_term = lax.dot_general(
            preact_grad, rec_matrix, (((1,), (1,)), ((), ())), preferred_element_type=f32
        )
        next_hidden = (
            lax.psum_scatter(back_term, "mp", scatter_dimension=1, tiled=True) * keep_now[:, None]
        )
        next_cell = cell_grad * forget_gate * keep_now[:, None]
        return ((next_hidden, next_cell), preact_grad)

    zero_rows = jnp.zeros((row_count, local_units), f32)
    _, preact_grads = lax.scan(
        backward_step,
        (zero_rows, zero_rows),
        (preacts, cells, prev_cells, out_grads, keep_mask),
        reverse=True,
    )
    flat_prev = prevs.reshape(tokens_here, hidden_total)
    flat_pgrad = preact_grads.reshape(tokens_here, gate_cols)
    columns = flat_prev
    rec_grad = lax.psum_scatter(
        lax.dot_general(columns, flat_pgrad, (((0,), (0,)), ((), ())), preferred_element_type=f32),
        "dp",
        scatter_dimension=0,
        tiled=True,
    ).reshape(recurrent_weight.shape)
    onehot_ids = (
        time_ids.reshape(tokens_here)[:, None] == jnp.arange(vocab_size, dtype=jnp.int32)[None, :]
    ).astype(bf16)
    table_part = lax.dot_general(
        onehot_ids, flat_pgrad, (((0,), (0,)), ((), ())), preferred_element_type=f32
    )
    table_sum, dec_bias_grad, loss_data = lax.psum((table_part, dec_bias_part, loss_part), "dp")
    in_grad = jnp.dot(embedding.astype(f32).T, table_sum, precision=highest).reshape(
        width_in, 4, local_units
    )
    bias_grad = jnp.sum(table_sum, axis=0).reshape(4, local_units)
    emb_part = lax.dot_general(
        table_sum,
        input_weight.reshape(width_in, gate_cols).astype(f32),
        (((1,), (1,)), ((), ())),
        precision=highest,
    )
    emb_grad, loss = lax.psum((emb_part, loss_data), "mp")
    return (loss, emb_grad, in_grad, rec_grad, bias_grad, dec_grad, dec_bias_grad)


def solution(mesh):
    in_specs = (
        P("dp", None),
        P("dp", None),
        P("dp", None),
        P(),
        P(None, None, "mp"),
        P("dp", None, "mp"),
        P(None, "mp"),
        P("mp", "dp", None, None),
        P(),
    )
    out_specs = (
        P(),
        P(),
        P(None, None, "mp"),
        P("dp", None, "mp"),
        P(None, "mp"),
        P("mp", "dp", None, None),
        P(),
    )
    fits = (mesh.shape["dp"], mesh.shape["mp"]) == (8, 4)
    return jax.shard_map(
        grouped if fits else on_device,
        mesh=mesh,
        in_specs=in_specs,
        out_specs=out_specs,
        check_vma=False,
    )
```
